512 devices in a mesh: dom: 512 (over x, y, z, core).
Axes of the slice: x: 4, y: 8, z: 8, core: 2. Of those that a mesh axis runs over, the one named last changes fastest.
Arguments:
- saved_states: float32 [4, 3, 28, 65536], P(None, None, None, 'dom'), may hold values from -3.375 to 3.75, as said below
- adjoint_final: float32 [3, 28, 65536], P(None, None, 'dom'), may hold values from -6 to 6
- bathymetry: float32 [28, 65536], P(None, 'dom'), may hold values from 0.7 to 3.9
- wind_speed: float32 [28, 65536], P(None, 'dom'), may hold values from 0.5 to 1.5
- wind_angle: float32 [28, 65536], P(None, 'dom'), may hold values from -3.140625 to 3.140625
- drag_rate: float32 [1], replicated, may hold values from 2 to 8
- metrics: float32 [4, 65536], P(None, 'dom'), may hold values from -0.42 to 1.82
- face_link: int32 [3, 65536], P(None, 'dom'), may hold values from 0 to 511, as said below
- face_tag: int32 [3, 65536], P(None, 'dom'), may hold values from 0 to 2, as said below
- send_faces: int32 [8, 8192], P(None, 'dom'), may hold values from -1 to 383, as said below
Outputs:
- initial_adjoint: float32 [3, 28, 65536], P(None, None, 'dom')
- depth_gradient: float32 [28, 65536], P(None, 'dom')
- speed_gradient: float32 [28, 65536], P(None, 'dom')
- angle_gradient: float32 [28, 65536], P(None, 'dom')
- drag_gradient: float32 [1], replicated
The draws below stay inside these ranges and needn't reach their ends.
Inputs may be any that keep to these rules, and one draw needn't show every extreme that they name: `send_faces`: row j lists the faces (local index f * 128 + e) that this device shares with the device at offset j + 1 (j < 4) or 4 - j - 1 (otherwise), in slots 0 to n - 1, and -1 in the other slots; that neighbor's row toward this device has the same n, and slot c of both names the two sides of one face. n is at most 16, equals 16 for some pair in every draw, and some device has n = 16 in all 8 rows. No face is listed twice and no row leads past the ends of the axis. `face_link`: A value below 384 names the partner face on the same device, which links back; 384 + j * 16 + c means the face stands in slot c of row j of send_faces; a face with face_tag 1 or 2 links to itself. `face_tag`: 0 for faces with a partner, 1 for walls, 2 for open boundaries. `saved_states`: heights (component 0) lie between 0.75 and 3.75.
All inputs are finite; a program needn't handle non-finite values.
Results may differ from the reference program's by a relative error of at most 0.0003.
Values sent between devices are 32-bit elements; how exact they have to be, the bound alone decides.
No kernel may reach another device: no remote copies, remote signals or barrier semaphores. Data moves between devices by JAX's collectives and lax.ppermute only.
A program may use at most 64 MiB of HBM per device.

```python
import math
import jax
import jax.numpy as jnp
import numpy as np
from jax import lax

NP = 28
EDEV = 128
NREACH = 4
NOFF = 8
CAP = 16
SECTIONS = 4
ELEMS = 65536


def mesh_links(key):
    devices = ELEMS // EDEV
    face_total = 3 * EDEV
    slot_total = NOFF * CAP
    key_count, key_coast, key_shuffle, key_bound, key_kind = jax.random.split(key, 5)
    coast_width = max(devices // 8, 2 * NREACH + 1)
    coast_start = jax.random.randint(key_coast, (), NREACH, devices - coast_width - NREACH + 1)
    device_ids = jnp.arange(devices, dtype=jnp.int32)
    coastal = (device_ids >= coast_start) & (device_ids < coast_start + coast_width)
    base_counts = jax.random.randint(key_count, (devices, NREACH), CAP // 6, CAP // 3 + 1)
    steps_ahead = jnp.arange(1, NREACH + 1, dtype=jnp.int32)[None, :]
    ahead_ids = device_ids[:, None] + steps_ahead
    upward = jnp.where(coastal[:, None], CAP, base_counts)
    upward = jnp.where(ahead_ids < devices, upward, 0)
    behind_ids = device_ids[:, None] - steps_ahead
    backward = upward[jnp.clip(behind_ids, 0, devices - 1), jnp.arange(NREACH)[None, :]]
    backward = jnp.where(behind_ids >= 0, backward, 0)
    counts = jnp.concatenate([upward, backward], axis=1)
    active = jnp.arange(CAP)[None, None, :] < counts[:, :, None]
    flat_active = active.reshape(devices, slot_total)
    shared_total = jnp.sum(flat_active.astype(jnp.int32), axis=1)
    rank_slot = jnp.cumsum(flat_active.astype(jnp.int32), axis=1) - 1
    shuffle = jax.vmap(lambda single: jax.random.permutation(single, face_total))(jax.random.split(key_shuffle, devices)).astype(jnp.int32)
    send_list = jnp.where(flat_active, jnp.take_along_axis(shuffle, jnp.clip(rank_slot, 0, face_total - 1), axis=1), -1)
    slot_ids = jnp.arange(slot_total, dtype=jnp.int32)[None, :]
    ranking = jnp.argsort(jnp.where(flat_active, slot_ids, slot_total + slot_ids), axis=1).astype(jnp.int32)
    position = jnp.arange(face_total, dtype=jnp.int32)[None, :]
    slot_at = jnp.take_along_axis(ranking, jnp.clip(position, 0, slot_total - 1), axis=1)
    remaining = face_total - shared_total
    bound_count = remaining % 2 + 2 * jax.random.randint(key_bound, (devices,), 0, remaining // 8 + 1)
    first_pair = (shared_total + bound_count)[:, None]
    partner_pos = jnp.clip(first_pair + jnp.bitwise_xor(position - first_pair, 1), 0, face_total - 1)
    partner_face = jnp.take_along_axis(shuffle, partner_pos, axis=1)
    is_shared = position < shared_total[:, None]
    is_bound = ~is_shared & (position < first_pair)
    link_pos = jnp.where(is_shared, face_total + slot_at, jnp.where(is_bound, shuffle, partner_face))
    kinds = jax.random.randint(key_kind, (devices, face_total), 1, 3)
    tag_pos = jnp.where(is_bound, kinds, 0)
    place_of = jnp.argsort(shuffle, axis=1)
    link_face = jnp.take_along_axis(link_pos, place_of, axis=1)
    tag_face = jnp.take_along_axis(tag_pos, place_of, axis=1)
    link_whole = jnp.transpose(link_face.reshape(devices, 3, EDEV), (1, 0, 2)).reshape(3, ELEMS)
    tag_whole = jnp.transpose(tag_face.reshape(devices, 3, EDEV), (1, 0, 2)).reshape(3, ELEMS)
    send_whole = jnp.transpose(send_list.reshape(devices, NOFF, CAP), (1, 0, 2)).reshape(NOFF, devices * CAP)
    return (link_whole.astype(jnp.int32), tag_whole.astype(jnp.int32), send_whole.astype(jnp.int32))


def draw_face_link(key, part):
    return mesh_links(key)[0]


def draw_face_tag(key, part):
    return mesh_links(key)[1]


def draw_send_faces(key, part):
    return mesh_links(key)[2]


def draw_bathymetry(key, part):
    key = jax.random.fold_in(key, 11)
    fraction = jnp.arange(ELEMS, dtype=jnp.float32) / (ELEMS - 1)
    profile = 3.0 - 2.0 * fraction
    rough = jax.random.uniform(key, (NP, ELEMS), jnp.float32, 0.8, 1.2)
    return profile[None, :] * rough


def draw_saved_states(key, part):
    key = jax.random.fold_in(key, 12)
    key_height, key_flow = jax.random.split(key)
    fraction = jnp.arange(ELEMS, dtype=jnp.float32) / (ELEMS - 1)
    profile = 3.0 - 2.0 * fraction
    height = profile * jax.random.uniform(key_height, (SECTIONS, 1, NP, ELEMS), jnp.float32, 0.75, 1.25)
    velocity = (1.0 + 2.0 * fraction) * 0.1 * jnp.clip(jax.random.normal(key_flow, (SECTIONS, 2, NP, ELEMS), jnp.float32), -3.0, 3.0)
    return jnp.concatenate([height, height * velocity], axis=1)


def draw_metrics(key, part):
    key = jax.random.fold_in(key, 13)
    key_size, key_shear = jax.random.split(key)
    scaling = jax.random.uniform(key_size, (1, ELEMS), jnp.float32, 0.7, 1.4)
    shear = jax.random.uniform(key_shear, (4, ELEMS), jnp.float32, -0.3, 0.3)
    identity_rows = jnp.array([1.0, 0.0, 0.0, 1.0], jnp.float32)[:, None]
    return scaling * (identity_rows + shear)


def block_levels(key, shape, cuts, least, high):
    factor_of, own = 1.0, jax.random.fold_in(key, 6)
    for dim, blocks in cuts:
        draws = jnp.exp(jax.random.uniform(jax.random.fold_in(own, dim), (blocks,), jnp.float32, least / len(cuts), high / len(cuts)))
        factor_of = factor_of * jnp.repeat(draws, shape[dim] // blocks).reshape([-1 if axis == dim else 1 for axis in range(len(shape))])
    return factor_of


def gaussian(stream_key, shape, scale, most, cuts=(), kind=jnp.bfloat16):
    values = scale * jax.random.normal(stream_key, shape, jnp.float32)
    if cuts:
        values = values * block_levels(stream_key, shape, cuts, -0.22, 0.18)
    return jnp.clip(values, -most, most).astype(kind)


def setup_inputs(seed: int = 0) -> dict:
    streams_of = jax.random.split(jax.random.key(seed), 11)
    return {
        "saved_states": draw_saved_states(jax.random.fold_in(streams_of[10], 71), 0),
        "adjoint_final": gaussian(streams_of[1], (3, NP, ELEMS), 1.0, 6.0, ((2, 512),), jnp.float32),
        "bathymetry": draw_bathymetry(jax.random.fold_in(streams_of[10], 71), 0),
        "wind_speed": jnp.clip(0.5 + 1.0 * jax.random.uniform(streams_of[3], (NP, ELEMS), jnp.float32) ** block_levels(streams_of[3], (NP, ELEMS), ((1, 512),), -0.2, 0.2), 0.5, 1.5),
        "wind_angle": jnp.clip(jax.random.uniform(streams_of[4], (NP, ELEMS), jnp.float32, -3.140625, 3.140625), -3.140625, 3.140625),
        "drag_rate": jnp.clip(jnp.exp(jax.random.uniform(streams_of[5], (1,), jnp.float32, math.log(2.0), math.log(8.0))), 2.0, 8.0),
        "metrics": draw_metrics(jax.random.fold_in(streams_of[10], 71), 0),
        "face_link": draw_face_link(jax.random.fold_in(streams_of[10], 71), 0),
        "face_tag": draw_face_tag(jax.random.fold_in(streams_of[10], 71), 0),
        "send_faces": draw_send_faces(jax.random.fold_in(streams_of[10], 71), 0),
    }


GRAVITY = 1.0
PENALTY = 3.0
WIND_COEF = 5.0
TIME_STEP = 0.01

def solve_dense(matrix, right):
    system = np.array(matrix) + 0.0
    result = np.array(right) + 0.0
    extent = system.shape[0]
    for column in range(extent):
        pivot_index = column + int(np.argmax(np.abs(system[column:, column])))
        system[[column, pivot_index]] = system[[pivot_index, column]]
        result[[column, pivot_index]] = result[[pivot_index, column]]
        for target in range(column + 1, extent):
            factor = system[target, column] / system[column, column]
            system[target] = system[target] - factor * system[column]
            result[target] = result[target] - factor * result[column]
    solution = np.zeros(result.shape)
    for column in range(extent - 1, -1, -1):
        solution[column] = (result[column] - system[column, column + 1:] @ solution[column + 1:]) / system[column, column]
    return solution

def element_tables():
    degree = 6
    nodes = [(column, row_index) for row_index in range(degree + 1) for column in range(degree + 1 - row_index)]
    node_total = len(nodes)
    coord_x = np.array([node[0] / degree for node in nodes])
    coord_y = np.array([node[1] / degree for node in nodes])
    vander = np.zeros((node_total, node_total))
    vander_r = np.zeros((node_total, node_total))
    vander_s = np.zeros((node_total, node_total))
    grams = np.zeros((node_total, node_total))
    for column_index, power in enumerate(nodes):
        first, second = power
        vander[:, column_index] = coord_x ** first * coord_y ** second
        if first > 0:
            vander_r[:, column_index] = 0.5 * first * coord_x ** (first - 1) * coord_y ** second
        if second > 0:
            vander_s[:, column_index] = 0.5 * second * coord_x ** first * coord_y ** (second - 1)
        for other_index, other_power in enumerate(nodes):
            sum_x = first + other_power[0]
            sum_y = second + other_power[1]
            grams[column_index, other_index] = 4.0 * math.factorial(sum_x) * math.factorial(sum_y) / math.factorial(sum_x + sum_y + 2)
    deriv_r = solve_dense(vander.T, vander_r.T).T
    deriv_s = solve_dense(vander.T, vander_s.T).T
    mass_inverse = vander @ solve_dense(grams, vander.T)
    points = np.arange(degree + 1) / degree
    line_vander = np.stack([points ** power for power in range(degree + 1)], axis=1)
    line_grams = np.array([[2.0 / (first + second + 1) for second in range(degree + 1)] for first in range(degree + 1)])
    line_inverse = solve_dense(line_vander, np.eye(degree + 1))
    line_mass = line_inverse.T @ line_grams @ line_inverse
    lookup = {node: number for number, node in enumerate(nodes)}
    face_nodes = [[lookup[step, 0] for step in range(degree + 1)], [lookup[degree - step, step] for step in range(degree + 1)], [lookup[0, degree - step] for step in range(degree + 1)]]
    embed = np.zeros((node_total, 3 * (degree + 1)))
    extract = np.zeros((3 * (degree + 1), node_total))
    for face_index in range(3):
        for step in range(degree + 1):
            extract[face_index * (degree + 1) + step, face_nodes[face_index][step]] = 1.0
            for other_step in range(degree + 1):
                embed[face_nodes[face_index][other_step], face_index * (degree + 1) + step] += line_mass[other_step, step]
    lifting = mass_inverse @ embed
    return (jnp.asarray(deriv_r, jnp.float32), jnp.asarray(deriv_s, jnp.float32), jnp.asarray(lifting, jnp.float32), jnp.asarray(extract, jnp.float32))

def face_fluxes(values):
    height = values[0]
    velocity_x = values[1] / height
    velocity_y = values[2] / height
    pressure = 0.5 * GRAVITY * height * height
    flux_x = jnp.stack([values[1], values[1] * velocity_x + pressure, values[2] * velocity_x])
    flux_y = jnp.stack([values[2], values[1] * velocity_y, values[2] * velocity_y + pressure])
    return (flux_x, flux_y)

def face_values(state_now, extract):
    elements = state_now.shape[-1]
    face_rows = jnp.einsum('ij,cjk->cik', extract, state_now, precision=lax.Precision.HIGHEST)
    return face_rows.reshape(3, 3, 7, elements).transpose(0, 2, 1, 3).reshape(3, 7, 3 * elements)

def node_values(faces_in, extract):
    elements = faces_in.shape[-1] // 3
    face_rows = faces_in.reshape(3, 7, 3, elements).transpose(0, 2, 1, 3).reshape(3, 21, elements)
    return jnp.einsum('ji,cjk->cik', extract, face_rows, precision=lax.Precision.HIGHEST)

def tendency(state_now, outer, depth_field, speed_field, angle_field, drag_rate, metrics, face_tag, tables):
    deriv_r, deriv_s, lifting, extract = tables
    highest = lax.Precision.HIGHEST
    elements = state_now.shape[-1]
    height = state_now[0]
    velocity_x = state_now[1] / height
    velocity_y = state_now[2] / height
    flux_x, flux_y = face_fluxes(state_now)
    fields = jnp.concatenate([flux_x, flux_y, depth_field[None]], axis=0)
    along_r = jnp.einsum('ij,cjk->cik', deriv_r, fields, precision=highest)
    along_s = jnp.einsum('ij,cjk->cik', deriv_s, fields, precision=highest)
    r_wrt_x, r_wrt_y, s_wrt_x, s_wrt_y = (metrics[0], metrics[1], metrics[2], metrics[3])
    gradient_x = r_wrt_x * along_r + s_wrt_x * along_s
    gradient_y = r_wrt_y * along_r + s_wrt_y * along_s
    divergence = gradient_x[0:3] + gradient_y[3:6]
    stress = WIND_COEF * speed_field * speed_field
    source_x = GRAVITY * height * gradient_x[6] + stress * jnp.cos(angle_field) - drag_rate[0] * velocity_x
    source_y = GRAVITY * height * gradient_y[6] + stress * jnp.sin(angle_field) - drag_rate[0] * velocity_y
    inner = jnp.einsum('ij,cjk->cik', extract, state_now, precision=highest).reshape(3, 3, 7, elements)
    depth_face = jnp.dot(extract, depth_field, precision=highest).reshape(3, 7, elements)
    given = jnp.flip(outer.reshape(3, 7, 3, elements), axis=1).transpose(0, 2, 1, 3)
    normal_x = jnp.stack([-s_wrt_x, r_wrt_x + s_wrt_x, -r_wrt_x])[:, None, :]
    normal_y = jnp.stack([-s_wrt_y, r_wrt_y + s_wrt_y, -r_wrt_y])[:, None, :]
    face_scale = jnp.sqrt(normal_x * normal_x + normal_y * normal_y)
    unit_x = normal_x / face_scale
    unit_y = normal_y / face_scale
    wall_mask = (face_tag == 1)[:, None, :]
    open_mask = (face_tag == 2)[:, None, :]
    normal_momentum = inner[1] * unit_x + inner[2] * unit_y
    outside_height = jnp.where(wall_mask, inner[0], jnp.where(open_mask, depth_face, given[0]))
    outside_first = jnp.where(wall_mask, inner[1] - 2.0 * normal_momentum * unit_x, jnp.where(open_mask, inner[1], given[1]))
    outside_second = jnp.where(wall_mask, inner[2] - 2.0 * normal_momentum * unit_y, jnp.where(open_mask, inner[2], given[2]))
    outside = jnp.stack([outside_height, outside_first, outside_second])
    inner_fx, inner_fy = face_fluxes(inner)
    outer_fx, outer_fy = face_fluxes(outside)
    flux_jump = 0.5 * (normal_x * (inner_fx - outer_fx) + normal_y * (inner_fy - outer_fy)) - 0.5 * PENALTY * face_scale * (inner - outside)
    lifted = jnp.einsum('ij,cjk->cik', lifting, flux_jump.reshape(3, 21, elements), precision=highest)
    sources = jnp.stack([jnp.zeros_like(height), source_x, source_y])
    return lifted - divergence + sources

def section_adjoint(state_now, outer, depth_field, speed_field, angle_field, drag_rate, metrics, face_tag, tables, weight):

    def local_map(state_in, outer_in, depth_in, speed_in, angle_in, drag_in):
        return tendency(state_in, outer_in, depth_in, speed_in, angle_in, drag_in, metrics, face_tag, tables)
    unused, pullback = jax.vjp(local_map, state_now, outer, depth_field, speed_field, angle_field, drag_rate)
    return pullback(weight)

def device_view(array):
    split = array.reshape(array.shape[:-1] + (ELEMS // EDEV, EDEV))
    return jnp.moveaxis(split, -2, 0)

def whole_view(array):
    moved = jnp.moveaxis(array, 0, -2)
    return moved.reshape(moved.shape[:-2] + (ELEMS,))

def reference(saved_states, adjoint_final, bathymetry, wind_speed, wind_angle, drag_rate, metrics, face_link, face_tag, send_faces):
    tables = element_tables()
    extract = tables[3]
    device_count = ELEMS // EDEV
    face_total = 3 * EDEV
    links = device_view(face_link).reshape(device_count, face_total)
    tag_dev = device_view(face_tag)
    interior = tag_dev.reshape(-1) == 0
    send_dev = jnp.transpose(send_faces.reshape(NOFF, device_count, CAP), (1, 0, 2))
    device_ids = jnp.arange(device_count, dtype=jnp.int32)[:, None]
    offsets = jnp.array([step + 1 for step in range(NREACH)] + [-(step + 1) for step in range(NREACH)], dtype=jnp.int32)
    shared = links >= face_total
    slot_index = jnp.clip(links - face_total, 0, NOFF * CAP - 1)
    direction = slot_index // CAP
    place = slot_index % CAP
    facing = (direction + NREACH) % NOFF
    neighbor = jnp.clip(device_ids + offsets[direction], 0, device_count - 1)
    far_face = send_dev[neighbor, facing, place]
    partner = jnp.where(shared, neighbor * face_total + far_face, device_ids * face_total + links).reshape(-1).astype(jnp.int32)
    depth_dev = device_view(bathymetry)
    speed_dev = device_view(wind_speed)
    angle_dev = device_view(wind_angle)
    metric_dev = device_view(metrics)

    def one_section(section_index, weight_dev):
        state_dev = device_view(saved_states[section_index])
        own = jax.vmap(lambda single: face_values(single, extract))(state_dev)
        trace_pool = jnp.moveaxis(own, 0, 2).reshape(3, 7, -1)
        outer = jnp.take(trace_pool, partner, axis=2)
        outer_dev = jnp.moveaxis(outer.reshape(3, 7, device_count, face_total), 2, 0)

        def per_block(block_items):
            state_now, outer_now, depth_now, speed_now, angle_now, metric_now, tag_now, weight_now = block_items
            return section_adjoint(state_now, outer_now, depth_now, speed_now, angle_now, drag_rate, metric_now, tag_now, tables, weight_now)
        terms = lax.map(per_block, (state_dev, outer_dev, depth_dev, speed_dev, angle_dev, metric_dev, tag_dev, weight_dev))
        back_pool = jnp.moveaxis(terms[1], 0, 2).reshape(3, 7, -1)
        gathered = jnp.where(interior, jnp.take(back_pool, partner, axis=2), 0.0)
        gathered_dev = jnp.moveaxis(gathered.reshape(3, 7, device_count, face_total), 2, 0)
        state_term = terms[0] + jax.vmap(lambda single: node_values(single, extract))(gathered_dev)
        return (state_term, terms[2], terms[3], terms[4], lax.optimization_barrier(jnp.sum(terms[5], axis=0)))
    half_step = 0.5 * TIME_STEP
    adjoint = device_view(adjoint_final)
    state_term, depth_sum, speed_sum, angle_sum, drag_sum = one_section(3, half_step * adjoint)
    adjoint = adjoint + state_term
    state_term, depth_term, speed_term, angle_term, drag_term = one_section(2, TIME_STEP / 6.0 * adjoint)
    kept = 2.0 / 3.0 * adjoint
    adjoint = adjoint / 3.0 + state_term
    depth_sum, speed_sum, angle_sum, drag_sum = (depth_sum + depth_term, speed_sum + speed_term, angle_sum + angle_term, drag_sum + drag_term)
    state_term, depth_term, speed_term, angle_term, drag_term = one_section(1, half_step * adjoint)
    adjoint = adjoint + state_term
    depth_sum, speed_sum, angle_sum, drag_sum = (depth_sum + depth_term, speed_sum + speed_term, angle_sum + angle_term, drag_sum + drag_term)
    state_term, depth_term, speed_term, angle_term, drag_term = one_section(0, half_step * adjoint)
    adjoint = kept + adjoint + state_term
    depth_sum, speed_sum, angle_sum, drag_sum = (depth_sum + depth_term, speed_sum + speed_term, angle_sum + angle_term, drag_sum + drag_term)
    return (whole_view(adjoint), whole_view(depth_sum), whole_view(speed_sum), whole_view(angle_sum), drag_sum)
```

```python
import math

import jax
import jax.numpy as jnp
import ml_dtypes
import numpy as np
from jax import lax
from jax.experimental import pallas as pl
from jax.experimental.pallas import tpu as pltpu
from jax.sharding import PartitionSpec as P

GRAVITY = 1.0
PENALTY = 3.0
WIND_COEF = 5.0
TIME_STEP = 0.01
HALF = 0.5 * TIME_STEP
SIXTH = TIME_STEP / 6.0

GROUP = 32
ROW = 16
REACH = 4
DIRS = 8
SLOTS = 16
E = 128
F32 = jnp.float32
BF16 = jnp.bfloat16


def solve_dense(matrix, right):
    system = np.array(matrix) + 0.0
    result = np.array(right) + 0.0
    extent = system.shape[0]
    for column in range(extent):
        pivot_index = column + int(np.argmax(np.abs(system[column:, column])))
        system[[column, pivot_index]] = system[[pivot_index, column]]
        result[[column, pivot_index]] = result[[pivot_index, column]]
        for target in range(column + 1, extent):
            factor = system[target, column] / system[column, column]
            system[target] = system[target] - factor * system[column]
            result[target] = result[target] - factor * result[column]
    solution = np.zeros(result.shape)
    for column in range(extent - 1, -1, -1):
        solution[column] = (
            result[column] - system[column, column + 1 :] @ solution[column + 1 :]
        ) / system[column, column]
    return solution


def element_tables():
    degree = 6
    nodes = [
        (column, row_index)
        for row_index in range(degree + 1)
        for column in range(degree + 1 - row_index)
    ]
    node_total = len(nodes)
    coord_x = np.array([node[0] / degree for node in nodes])
    coord_y = np.array([node[1] / degree for node in nodes])
    vander = np.zeros((node_total, node_total))
    vander_r = np.zeros((node_total, node_total))
    vander_s = np.zeros((node_total, node_total))
    grams = np.zeros((node_total, node_total))
    for column_index, power in enumerate(nodes):
        first, second = power
        vander[:, column_index] = coord_x**first * coord_y**second
        if first > 0:
            vander_r[:, column_index] = 0.5 * first * coord_x ** (first - 1) * coord_y**second
        if second > 0:
            vander_s[:, column_index] = 0.5 * second * coord_x**first * coord_y ** (second - 1)
        for other_index, other_power in enumerate(nodes):
            sum_x = first + other_power[0]
            sum_y = second + other_power[1]
            grams[column_index, other_index] = (
                4.0
                * math.factorial(sum_x)
                * math.factorial(sum_y)
                / math.factorial(sum_x + sum_y + 2)
            )
    deriv_r = solve_dense(vander.T, vander_r.T).T
    deriv_s = solve_dense(vander.T, vander_s.T).T
    mass_inverse = vander @ solve_dense(grams, vander.T)
    points = np.arange(degree + 1) / degree
    line_vander = np.stack([points**power for power in range(degree + 1)], axis=1)
    line_grams = np.array(
        [
            [2.0 / (first + second + 1) for second in range(degree + 1)]
            for first in range(degree + 1)
        ]
    )
    line_inverse = solve_dense(line_vander, np.eye(degree + 1))
    line_mass = line_inverse.T @ line_grams @ line_inverse
    lookup = {node: number for number, node in enumerate(nodes)}
    face_nodes = [
        [lookup[step, 0] for step in range(degree + 1)],
        [lookup[degree - step, step] for step in range(degree + 1)],
        [lookup[0, degree - step] for step in range(degree + 1)],
    ]
    embed = np.zeros((node_total, 3 * (degree + 1)))
    extract = np.zeros((3 * (degree + 1), node_total))
    for face_index in range(3):
        for step in range(degree + 1):
            extract[face_index * (degree + 1) + step, face_nodes[face_index][step]] = 1.0
            for other_step in range(degree + 1):
                embed[
                    face_nodes[face_index][other_step], face_index * (degree + 1) + step
                ] += line_mass[other_step, step]
    lifting = mass_inverse @ embed
    return deriv_r, deriv_s, lifting, extract


def offset_of(direction):
    return direction + 1 if direction < REACH else REACH - direction - 1


def direction_of(offset):
    if 1 <= offset <= REACH:
        return offset - 1
    if -REACH <= offset <= -1:
        return REACH - 1 - offset
    return None


def place_a(d):
    return ROW + d


def place_b(d):
    return d if d < ROW else d + ROW * 2


def holder(place):
    if place < ROW:
        return place, 1
    if place < ROW + GROUP:
        return place - ROW, 0
    return place - 2 * ROW, 1


def routes():
    table = np.zeros((GROUP, 128), np.int32)
    for d in range(GROUP):
        for which, place in ((0, place_a(d)), (1, place_b(d))):
            for e in range(GROUP):
                found = direction_of(place_a(e) - place)
                if found is None:
                    found = direction_of(place_b(e) - place)
                table[d, 32 * which + e] = DIRS if found is None else found
            for j in range(DIRS):
                source = place + offset_of(j)
                if 0 <= source < 4 * ROW:
                    e, kind = holder(source)
                else:
                    e, kind = 0, 2
                table[d, 64 + 16 * which + j] = e
                table[d, 72 + 16 * which + j] = kind
    return table


def parts3(matrix, width):
    padded = np.zeros((matrix.shape[0], width))
    padded[:, : matrix.shape[1]] = matrix
    hi = padded.astype(np.float32).astype(ml_dtypes.bfloat16)
    lo = (padded - hi.astype(np.float64)).astype(ml_dtypes.bfloat16)
    return np.concatenate([hi, lo, hi], axis=1)


def constants():
    deriv_r, deriv_s, lifting, extract = element_tables()

    def pad_rows(matrix):
        return np.concatenate([matrix, np.zeros((4, matrix.shape[1]))])

    lift = np.zeros((24, 28))
    flip = np.zeros((24, 28))
    take = np.zeros((24, 28))
    give = np.zeros((24, 28))
    for face in range(3):
        for k in range(7):
            lift[8 * face + k] = lifting[:, 7 * face + k]
            flip[8 * face + k] = lifting[:, 7 * face + 6 - k]
            take[8 * face + k] = extract[7 * face + k]
            give[8 * face + k] = extract[7 * face + k]
        take[8 * face + 7] = extract[7 * face + 6]
    back = np.concatenate([pad_rows(deriv_r.T), pad_rows(deriv_s.T), lift, flip])
    back3 = parts3(back, 32)
    flip3 = parts3(flip, 32)
    grad3 = parts3(np.concatenate([pad_rows(deriv_r), pad_rows(deriv_s)]), 32)
    take2 = np.zeros((24, 64))
    take2[:, 0:28] = take
    take2[:, 32:60] = take
    spread = np.concatenate([pad_rows(give.T), flip @ give.T])
    spread3 = parts3(spread, 24)
    spread3 = np.concatenate([spread3, np.zeros((56, 8), ml_dtypes.bfloat16)], axis=1)
    as_bf16 = lambda m: jnp.asarray(np.asarray(m).astype(ml_dtypes.bfloat16))
    return as_bf16(back3), as_bf16(flip3), as_bf16(grad3), as_bf16(take2), as_bf16(spread3)


def dot(a, b):
    return jnp.dot(a, b, preferred_element_type=F32)


def dot_nt(a, b):
    return lax.dot_general(a, b, (((1,), (1,)), ((), ())), preferred_element_type=F32)


def halves(x):
    hi = x.astype(BF16).astype(F32)
    return hi, x - hi


def times3(matrix3, x):
    hi = x.astype(BF16)
    lo = (x - hi.astype(F32)).astype(BF16)
    return dot(matrix3, jnp.concatenate([hi, hi, lo], axis=0))


def spread_faces(spread3, faces):
    hi, lo = halves(faces)
    stack = jnp.concatenate([hi, hi, lo, jnp.zeros((8, faces.shape[1]), F32)], axis=0)
    return dot(spread3, stack.astype(BF16))


def geometry(misc):
    rx, ry, sx, sy = misc[0:1], misc[1:2], misc[2:3], misc[3:4]
    normals = []
    for nx, ny in ((-sx, -sy), (rx + sx, ry + sy), (-rx, -ry)):
        normals.append((nx, ny, jnp.sqrt(nx * nx + ny * ny)))
    return (rx, ry, sx, sy), normals


def jump_back(n, t, u, v, gh):
    nx, ny, size = n
    un = nx * u + ny * v
    mixed = u * t[1] + v * t[2]
    pull = 0.5 * PENALTY * size
    return (
        0.5 * (gh * (nx * t[1] + ny * t[2]) - un * mixed) - pull * t[0],
        0.5 * (nx * (t[0] + mixed) + un * t[1]) - pull * t[1],
        0.5 * (ny * (t[0] + mixed) + un * t[2]) - pull * t[2],
    )


def traces(flipped, normals):
    last = lax.broadcasted_iota(jnp.int32, (8, E), 0) == 7
    rows = []
    for c in range(3):
        rows.append(
            jnp.concatenate(
                [jnp.where(last, normals[f][c], flipped[c][f]) for f in range(3)], axis=1
            )
        )
    return jnp.concatenate(rows, axis=0)


def far_index(link, block):
    v = link - 3 * E
    j = lax.shift_right_arithmetic(v, 4)
    c = jnp.bitwise_and(v, 15)
    row = lax.shift_right_arithmetic(c, 3) * 128 + j * 8 + jnp.bitwise_and(c, 7) + 64 * block
    return jnp.where(v >= 0, row, -1)


def send(x_ref, scratch, route, sends, trace_list):
    zero = lambda r, n: jnp.zeros((r, n), F32)
    for b in range(2):
        v = trace_list[b]
        n = 3 * E
        rows = []
        if b:
            rows.append(zero(64, 2 * n))
        rows += [
            jnp.concatenate([v, zero(24, n)], axis=1),
            zero(8, 2 * n),
            jnp.concatenate([zero(24, n), v], axis=1),
            zero(8 if b else 72, 2 * n),
        ]
        hi, lo = halves(jnp.concatenate(rows, axis=0))
        out = dot_nt(sends[b], hi.astype(BF16)) + dot_nt(sends[b], lo.astype(BF16))
        scratch[b, 0:64, :] = out
        scratch[b, 64:72, :] = zero(8, 128)
    for e in range(GROUP):
        first = pl.multiple_of(route[e] * 8, 8)
        second = pl.multiple_of(route[32 + e] * 8, 8)
        x_ref[8 * e : 8 * e + 8, :] = (
            scratch[0, pl.ds(first, 8), :] + scratch[1, pl.ds(second, 8), :]
        )


def send_matrix(misc):
    faces = misc[16:24]
    lane = lax.broadcasted_iota(jnp.int32, (8, 128), 1)
    low = jnp.where(lane < 8, faces, 0.0)
    high = jnp.where((lane >= 8) & (lane < 16), faces, 0.0)
    both = low + pltpu.roll(high, 56, 1)
    row = lax.broadcasted_iota(jnp.int32, (8, 128), 0)
    lined = jnp.zeros((8, 128), F32)
    for j in range(DIRS):
        moved = both if j == 0 else pltpu.roll(both, 8 * j, 1)
        lined = lined + jnp.where(row == j, moved, 0.0)
    line = jnp.sum(lined, axis=0, keepdims=True)
    column = jnp.transpose(jnp.broadcast_to(line, (128, 128)))
    face = lax.broadcasted_iota(jnp.int32, (64, 128), 1).astype(F32)
    pieces = []
    for half in range(2):
        part = column[64 * half : 64 * half + 64]
        for f in range(3):
            pieces.append(jnp.where(part == face + float(128 * f), 1.0, 0.0))
    return jnp.concatenate(pieces, axis=1).astype(BF16)


def pack_kernel(q_ref, lam_ref, depth_ref, metric_ref, tag_ref, link_ref, face_ref, out_ref):
    ones, zeros = jnp.ones((4, E), F32), jnp.zeros((4, E), F32)
    for s in range(3):
        for c in range(3):
            out_ref[3 * s + c, 0:28, :] = q_ref[s + 1, c]
            out_ref[3 * s + c, 28:32, :] = ones
    for c in range(3):
        out_ref[9 + c, 0:28, :] = lam_ref[c]
        out_ref[9 + c, 28:32, :] = zeros
    out_ref[12, 0:28, :] = depth_ref[...]
    out_ref[12, 28:32, :] = ones
    out_ref[13] = jnp.zeros((32, E), F32)
    out_ref[13, 0:4, :] = metric_ref[...]
    out_ref[13, 4:7, :] = tag_ref[...].astype(F32)
    out_ref[13, 8:11, :] = link_ref[...].astype(F32)
    out_ref[13, 16:24, 0:16] = face_ref[...].astype(F32)


def first_kernel(route, lam_a, lam_b, misc_a, misc_b, flip3, x_ref, sends_ref, scratch):
    weights = jnp.concatenate(
        [HALF * ref[c] for ref in (lam_a, lam_b) for c in range(3)], axis=1
    )
    flipped = times3(flip3[...], weights)
    trace_list, sends = [], []
    for b, misc_ref in enumerate((misc_a, misc_b)):
        misc = misc_ref[0]
        normals = geometry(misc)[1]
        pick = lambda c, f: flipped[8 * f : 8 * f + 8, 384 * b + 128 * c : 384 * b + 128 * c + 128]
        trace_list.append(traces([[pick(c, f) for f in range(3)] for c in range(3)], normals))
        sends.append(send_matrix(misc))
        sends_ref[b] = sends[b]
    send(x_ref, scratch, route, sends, trace_list)


def near_kernel(section, blocks, *refs):
    refs = list(refs)
    drag = refs.pop(0)
    back3, flip3, grad3, take2, spread3 = [refs.pop(0)[...] for _ in range(5)]
    lams = [refs.pop(0) for _ in range(blocks)]
    states = [refs.pop(0) for _ in range(blocks)]
    depths = [refs.pop(0) for _ in range(blocks)]
    miscs = [refs.pop(0) for _ in range(blocks)]
    old_ref = refs.pop(0) if section < 3 else None
    if section == 0:
        lam3_ref, speed_ref, angle_ref = refs.pop(0), refs.pop(0), refs.pop(0)
    base_ref = refs.pop(0)
    if section > 0:
        ahead_ref = refs.pop(0)
    motion_ref = refs.pop(0)
    if section > 0:
        sum_ref = refs.pop(0)
    else:
        depth_out, speed_out, angle_out = refs.pop(0), refs.pop(0), refs.pop(0)
    scale = SIXTH if section == 2 else HALF
    later = SIXTH if section == 3 else HALF
    drag_rate = drag[0]
    pad = jnp.ones((4, E), F32)

    lam = [[lams[b][c] for c in range(3)] for b in range(blocks)]
    w = [[scale * x for x in lam[b]] for b in range(blocks)]
    if section == 0:
        q = [[jnp.concatenate([states[0][0, c], pad], axis=0) for c in range(3)]]
    else:
        q = [[states[b][c] for c in range(3)] for b in range(blocks)]
    z = [depths[b][0] for b in range(blocks)]
    pulled = times3(back3, jnp.concatenate([x for b in range(blocks) for x in w[b]], axis=1))
    slopes = times3(grad3, jnp.concatenate(z, axis=1))
    fields = jnp.concatenate([x for b in range(blocks) for x in q[b] + [z[b]]], axis=1)
    hi, lo = halves(fields)
    at_faces = dot(take2, jnp.concatenate([hi, lo], axis=0).astype(BF16))

    face_sums, volumes, opens = [], [], []
    for b in range(blocks):
        misc = miscs[b][0]
        (rx, ry, sx, sy), normals = geometry(misc)
        part = lambda r0, r1, c: pulled[r0:r1, 384 * b + 128 * c : 384 * b + 128 * c + 128]
        h = q[b][0]
        inv = 1.0 / h
        u, v = q[b][1] * inv, q[b][2] * inv
        gh = GRAVITY * h
        along = [part(0, 32, c) for c in range(3)]
        across = [part(32, 64, c) for c in range(3)]
        fx = [-(rx * along[c] + sx * across[c]) for c in range(3)]
        fy = [-(ry * along[c] + sy * across[c]) for c in range(3)]
        cross = fx[2] + fy[1]
        slope_r = slopes[0:32, 128 * b : 128 * b + 128]
        slope_s = slopes[32:64, 128 * b : 128 * b + 128]
        slope_x = rx * slope_r + sx * slope_s
        slope_y = ry * slope_r + sy * slope_s
        flow = u * w[b][1] + v * w[b][2]
        drag_inv = drag_rate * inv
        volumes.append(
            (
                gh * (fx[1] + fy[2])
                - u * (u * fx[1] + v * cross)
                - v * v * fy[2]
                + GRAVITY * (slope_x * w[b][1] + slope_y * w[b][2])
                + drag_inv * flow,
                fx[0] + 2.0 * u * fx[1] + v * cross - drag_inv * w[b][1],
                fy[0] + u * cross + 2.0 * v * fy[2] - drag_inv * w[b][2],
            )
        )
        own = [[part(64 + 8 * f, 72 + 8 * f, c) for f in range(3)] for c in range(3)]
        flipped = [[part(88 + 8 * f, 96 + 8 * f, c) for f in range(3)] for c in range(3)]
        hi, lo = halves(traces(flipped, normals))
        pool = jnp.concatenate([hi, lo], axis=0).astype(BF16)
        links = misc[8:11].astype(jnp.int32)
        rows = lax.broadcasted_iota(jnp.int32, (3 * E, E), 0)
        opened = []
        sums = [[], [], []]
        for f in range(3):
            match = jnp.where(rows == links[f : f + 1], 1.0, 0.0).astype(BF16)
            got = dot(pool, match)
            got = got[0:24] + got[24:48]
            value = lambda i: at_faces[
                8 * f : 8 * f + 8, 512 * b + 128 * i : 512 * b + 128 * i + 128
            ]
            fh, fm, fn, fz = value(0), value(1), value(2), value(3)
            finv = 1.0 / fh
            fu, fv, fgh = fm * finv, fn * finv, GRAVITY * fh
            motion_ref[b, 0, 8 * f : 8 * f + 8, :] = fu
            motion_ref[b, 1, 8 * f : 8 * f + 8, :] = fv
            motion_ref[b, 2, 8 * f : 8 * f + 8, :] = fgh
            tag = misc[4 + f : 5 + f]
            linked, wall, free = tag == 0.0, tag == 1.0, tag == 2.0
            nx, ny, size = normals[f]
            t = [own[c][f] for c in range(3)]
            mine = jump_back(normals[f], t, fu, fv, fgh)
            inv_size = 1.0 / size
            ux, uy = nx * inv_size, ny * inv_size
            twice = 2.0 * (ux * t[1] + uy * t[2])
            mirrored = (t[0], t[1] - twice * ux, t[2] - twice * uy)
            near = (got[0:8], got[8:16], got[16:24])
            other_n = tuple(
                jnp.where(linked, near[c][7:8], jnp.where(wall, m, 0.0))
                for c, m in enumerate((-nx, -ny, size))
            )
            other_t = [
                jnp.where(linked, near[c], jnp.where(wall, mirrored[c], 0.0)) for c in range(3)
            ]
            theirs = jump_back(other_n, other_t, fu, fv, fgh)
            zinv = 1.0 / fz
            out = jump_back(normals[f], t, fm * zinv, fn * zinv, GRAVITY * fz)
            opened.append(jnp.where(free, -out[0], 0.0))
            sums[0].append(mine[0] - theirs[0])
            sums[1].append(mine[1] - theirs[1] - jnp.where(free, out[1], 0.0))
            sums[2].append(mine[2] - theirs[2] - jnp.where(free, out[2], 0.0))
        face_sums.append([jnp.concatenate(sums[c], axis=0) for c in range(3)])
        if b == 0:
            opens = jnp.concatenate(opened, axis=0)
            height, moved = h, flow
    to_nodes = [x for b in range(blocks) for x in face_sums[b]]
    if section == 0:
        old = [old_ref[i] for i in range(5)]
        opens = opens + old[4][0:24]
        to_nodes.append(opens)
    nodes = spread_faces(spread3, jnp.concatenate(to_nodes, axis=1))
    for b in range(blocks):
        bases = []
        for c in range(3):
            first = lam[b][c]
            if section == 2:
                first = first * (1.0 / 3.0)
            if section == 0:
                first = first + (2.0 / 3.0) * lam3_ref[c]
            where = 384 * b + 128 * c
            bases.append(first + volumes[b][c] + nodes[0:32, where : where + 128])
            base_ref[b, c] = bases[c]
        if section > 0:
            ahead = times3(flip3, later * jnp.concatenate(bases, axis=1))
            for c in range(3):
                ahead_ref[b, c] = ahead[:, 128 * c : 128 * c + 128]
    w1, w2 = w[0][1], w[0][2]
    g1, g2 = height * w1, height * w2
    if section == 3:
        fold = moved[0:8] + moved[8:16] + moved[16:24] + moved[24:32]
        news = [w1, w2, g1, g2]
    else:
        if section > 0:
            old = [old_ref[i] for i in range(5)]
            opens = opens + old[4][0:24]
            fold = old[4][24:32] + (moved[0:8] + moved[8:16] + moved[16:24] + moved[24:32])
        news = [x + y for x, y in zip(old[0:4], (w1, w2, g1, g2))]
    if section > 0:
        for i in range(4):
            sum_ref[i] = news[i]
        sum_ref[4, 0:24, :] = opens
        sum_ref[4, 24:32, :] = fold
    else:
        rx, ry, sx, sy = geometry(miscs[0][0])[0]
        w1, w2, g1, g2 = news
        pair = GRAVITY * jnp.concatenate([rx * g1 + ry * g2, sx * g1 + sy * g2], axis=1)
        pulled = times3(back3, pair)
        depth = pulled[0:32, 0:128] + pulled[32:64, 128:256] + nodes[0:32, 384:512]
        depth_out[...] = depth[0:28]
        speed, angle = speed_ref[...], angle_ref[...]
        cosine, sine = jnp.cos(angle), jnp.sin(angle)
        w1, w2 = w1[0:28], w2[0:28]
        speed_out[...] = (2.0 * WIND_COEF) * speed * (cosine * w1 + sine * w2)
        angle_out[...] = WIND_COEF * speed * speed * (cosine * w2 - sine * w1)


def far_kernel(section, blocks, *refs):
    refs = list(refs)
    route, y_ref, spread3_ref, base_ref, motion_ref = [refs.pop(0) for _ in range(5)]
    miscs = [refs.pop(0) for _ in range(blocks)]
    if section > 0:
        ahead_ref, sends_ref = refs.pop(0), refs.pop(0)
    if section == 1:
        q0_ref, sum_ref = refs.pop(0), refs.pop(0)
    lam_refs = [refs.pop(0) for _ in range(blocks)]
    if section > 0:
        x_ref, scratch = refs.pop(0), refs.pop(0)
    later = SIXTH if section == 3 else HALF

    boxes = []
    for b in range(2):
        for j in range(DIRS):
            if b < blocks:
                place = pl.multiple_of(route[64 + 16 * b + j] * 8, 8)
                kind = route[72 + 16 * b + j]
                box = y_ref[pl.ds(place, 8), :]
                box = jnp.where(kind == 1, pltpu.roll(box, 64, 1), box)
                boxes.append(jnp.where(kind == 2, 0.0, box))
            else:
                boxes.append(jnp.zeros((8, 128), F32))
    turned = jnp.transpose(jnp.concatenate(boxes, axis=0))
    hi, lo = halves(jnp.concatenate([turned[0:24], turned[32:56]], axis=1))
    pool = jnp.concatenate([hi, lo], axis=0).astype(BF16)
    rows = lax.broadcasted_iota(jnp.int32, (256, E), 0)
    face_sums = []
    for b in range(blocks):
        links = miscs[b][0][8:11].astype(jnp.int32)
        sums = [[], [], []]
        for f in range(3):
            match = jnp.where(rows == far_index(links[f : f + 1], b), 1.0, 0.0).astype(BF16)
            got = dot(pool, match)
            got = got[0:24] + got[24:48]
            far = (got[0:8], got[8:16], got[16:24])
            motion = [motion_ref[b, i, 8 * f : 8 * f + 8, :] for i in range(3)]
            theirs = jump_back(tuple(x[7:8] for x in far), far, *motion)
            for c in range(3):
                sums[c].append(-theirs[c])
        face_sums += [jnp.concatenate(sums[c], axis=0) for c in range(3)]
    spread = spread_faces(spread3_ref[...], jnp.concatenate(face_sums, axis=1))
    trace_list = []
    for b in range(blocks):
        lam = []
        for c in range(3):
            where = 384 * b + 128 * c
            lam.append(base_ref[b, c] + spread[0:32, where : where + 128])
        if section > 0:
            for c in range(3):
                lam_refs[b][c] = lam[c]
            flipped = [
                ahead_ref[b, c]
                + later * spread[32:56, 384 * b + 128 * c : 384 * b + 128 * c + 128]
                for c in range(3)
            ]
            split = [[flipped[c][8 * f : 8 * f + 8] for f in range(3)] for c in range(3)]
            trace_list.append(traces(split, geometry(miscs[b][0])[1]))
        else:
            for c in range(3):
                lam_refs[b][c] = lam[c][0:28]
        if section == 1 and b == 0:
            first = lam
    if section > 0:
        send(x_ref, scratch, route, [sends_ref[0], sends_ref[1]], trace_list)
    if section == 1:
        q0 = [q0_ref[0, c] for c in range(3)]
        flow = (q0[1] * first[1][0:28] + q0[2] * first[2][0:28]) * (HALF / q0[0])
        total = jnp.sum(sum_ref[4, 24:32, :]) + jnp.sum(flow)
        lane = lax.broadcasted_iota(jnp.int32, (8, 128), 1)
        for e in range(GROUP):
            part = x_ref[8 * e : 8 * e + 8, :]
            x_ref[8 * e : 8 * e + 8, :] = jnp.where(lane == 127, -total, part)


def whole(shape):
    return pl.BlockSpec(shape, lambda i: (0,) * len(shape))


def block(shape, first):
    return pl.BlockSpec(shape, lambda i: (first,) + (0,) * (len(shape) - 1))


SCALARS = pl.BlockSpec(memory_space=pltpu.SMEM)


def call(kernel, in_specs, outs, args, scratch=()):
    return pl.pallas_call(
        kernel,
        grid=(1,),
        in_specs=in_specs,
        out_specs=[whole(shape) for shape, _ in outs],
        out_shape=[jax.ShapeDtypeStruct(shape, dtype) for shape, dtype in outs],
        scratch_shapes=list(scratch),
        compiler_params=pltpu.CompilerParams(vmem_limit_bytes=32 * 1024 * 1024),
    )(*args)


def local(
    saved_states,
    adjoint_final,
    bathymetry,
    wind_speed,
    wind_angle,
    drag_rate,
    metrics,
    face_link,
    face_tag,
    send_faces,
):
    devices = lax.axis_size("dom")
    groups = [list(range(g, g + GROUP)) for g in range(0, devices, GROUP)]
    strides = [list(range(d, devices, GROUP)) for d in range(GROUP)]
    back3, flip3, grad3, take2, spread3 = constants()
    tables = [back3, flip3, grad3, take2, spread3]
    table_specs = [whole(t.shape) for t in tables]
    me = lax.rem(lax.axis_index("dom"), GROUP)
    route = lax.dynamic_slice(jnp.asarray(routes()), (me, 0), (1, 128)).reshape(128)

    nodes, mixed = (32, E), (3, 32, E)
    mine = call(
        pack_kernel,
        [whole(x.shape) for x in (saved_states, adjoint_final, bathymetry, metrics)]
        + [whole(x.shape) for x in (face_tag, face_link, send_faces)],
        [((14, 32, E), F32)],
        (saved_states, adjoint_final, bathymetry, metrics, face_tag, face_link, send_faces),
    )[0]
    pairs = [(i, i) for i in range(ROW)] + [(i, i) for i in range(devices - ROW, devices)]
    for row in range(1, devices // ROW - 1, 2):
        for i in range(row * ROW, row * ROW + ROW):
            pairs += [(i, i + ROW), (i + ROW, i)]
    halo = lax.ppermute(mine, "dom", pairs)
    both = (mine, halo)

    scratch = [pltpu.VMEM((2, 72, 128), F32)]
    x_out = ((GROUP * 8, 128), F32)
    x, sends = call(
        first_kernel,
        [SCALARS]
        + [block((3, 32, E), 3)] * 2
        + [block((1, 32, E), 13)] * 2
        + [whole(flip3.shape)],
        [x_out, ((2, 64, 768), BF16)],
        (route, mine, halo, mine, halo, flip3),
        scratch,
    )
    lams = both
    lam3 = sums = None
    for section in (3, 2, 1, 0):
        y = lax.all_to_all(x, "dom", 0, 0, tiled=True, axis_index_groups=groups)
        blocks = 2 if section > 0 else 1
        args = [drag_rate] + tables + list(lams[:blocks])
        specs = [SCALARS] + table_specs
        specs += [block(mixed, 3)] * blocks if section == 3 else [whole(mixed)] * blocks
        if section > 0:
            args += list(both)
            specs += [block(mixed, section - 1)] * blocks
        else:
            args += [saved_states]
            specs += [pl.BlockSpec((1, 3, 28, E), lambda i: (0, 0, 0, 0))]
        args += list(both[:blocks]) * 2
        specs += [block((1, 32, E), 12)] * blocks + [block((1, 32, E), 13)] * blocks
        if section < 3:
            args.append(sums)
            specs.append(whole((5, 32, E)))
        outs = [((blocks, 3, 32, E), F32)]
        if section > 0:
            outs.append(((blocks, 3, 24, E), F32))
        outs.append(((blocks, 3, 24, E), F32))
        if section > 0:
            outs.append(((5, 32, E), F32))
        else:
            args += [lam3, wind_speed, wind_angle]
            specs += [whole(mixed), whole((28, E)), whole((28, E))]
            outs += [((28, E), F32)] * 3
        got = call(
            lambda *refs, s=section, n=blocks: near_kernel(s, n, *refs), specs, outs, args
        )
        if section > 0:
            base, ahead, motion, sums = got
        else:
            base, motion, depth_gradient, speed_gradient, angle_gradient = got

        args = [route, y, spread3, base, motion] + list(both[:blocks])
        specs = [SCALARS] + [whole(v.shape) for v in (y, spread3, base, motion)]
        specs += [block((1, 32, E), 13)] * blocks
        if section > 0:
            args += [ahead, sends]
            specs += [whole(ahead.shape), whole(sends.shape)]
        if section == 1:
            args += [saved_states, sums]
            specs += [pl.BlockSpec((1, 3, 28, E), lambda i: (0, 0, 0, 0)), whole((5, 32, E))]
        if section > 0:
            outs = [(mixed, F32)] * 2 + [x_out]
        else:
            outs = [((3, 28, E), F32)]
        got = call(
            lambda *refs, s=section, n=blocks: far_kernel(s, n, *refs),
            specs,
            outs,
            args,
            scratch if section > 0 else (),
        )
        if section > 0:
            lams, x = got[0:2], got[2]
            if section == 3:
                lam3 = lams[0]
        else:
            initial = got[0]
    within = jnp.sum(y.reshape(GROUP, 8, 128)[:, 0, 127])
    spread = lax.all_to_all(
        jnp.broadcast_to(within, (devices // GROUP, 128)),
        "dom",
        0,
        0,
        tiled=True,
        axis_index_groups=strides,
    )
    drag_gradient = jnp.sum(spread[:, 0]).reshape(1)
    return (initial, depth_gradient, speed_gradient, angle_gradient, drag_gradient)


def solution(mesh):
    return jax.shard_map(
        local,
        mesh=mesh,
        in_specs=(
            P(None, None, None, "dom"),
            P(None, None, "dom"),
            P(None, "dom"),
            P(None, "dom"),
            P(None, "dom"),
            P(),
            P(None, "dom"),
            P(None, "dom"),
            P(None, "dom"),
            P(None, "dom"),
        ),
        out_specs=(P(None, None, "dom"), P(None, "dom"), P(None, "dom"), P(None, "dom"), P()),
        check_vma=False,
    )
```

```python
import math

import jax
import jax.numpy as jnp
import ml_dtypes
import numpy as np
from jax import lax
from jax.experimental import pallas as pl
from jax.experimental.pallas import tpu as pltpu
from jax.sharding import PartitionSpec as P

GRAVITY = 1.0
PENALTY = 3.0
WIND_COEF = 5.0
TIME_STEP = 0.01
HALF = 0.5 * TIME_STEP
SIXTH = TIME_STEP / 6.0

GROUP = 32
ROW = 16
REACH = 4
DIRS = 8
SLOTS = 16
E = 128
DEPTH, MISC = 12, 13
F32 = jnp.float32
BF16 = jnp.bfloat16


def solve_dense(matrix, right):
    system = np.array(matrix) + 0.0
    result = np.array(right) + 0.0
    extent = system.shape[0]
    for column in range(extent):
        pivot_index = column + int(np.argmax(np.abs(system[column:, column])))
        system[[column, pivot_index]] = system[[pivot_index, column]]
        result[[column, pivot_index]] = result[[pivot_index, column]]
        for target in range(column + 1, extent):
            factor = system[target, column] / system[column, column]
            system[target] = system[target] - factor * system[column]
            result[target] = result[target] - factor * result[column]
    solution = np.zeros(result.shape)
    for column in range(extent - 1, -1, -1):
        solution[column] = (
            result[column] - system[column, column + 1 :] @ solution[column + 1 :]
        ) / system[column, column]
    return solution


def element_tables():
    degree = 6
    nodes = [
        (column, row_index)
        for row_index in range(degree + 1)
        for column in range(degree + 1 - row_index)
    ]
    node_total = len(nodes)
    coord_x = np.array([node[0] / degree for node in nodes])
    coord_y = np.array([node[1] / degree for node in nodes])
    vander = np.zeros((node_total, node_total))
    vander_r = np.zeros((node_total, node_total))
    vander_s = np.zeros((node_total, node_total))
    grams = np.zeros((node_total, node_total))
    for column_index, power in enumerate(nodes):
        first, second = power
        vander[:, column_index] = coord_x**first * coord_y**second
        if first > 0:
            vander_r[:, column_index] = 0.5 * first * coord_x ** (first - 1) * coord_y**second
        if second > 0:
            vander_s[:, column_index] = 0.5 * second * coord_x**first * coord_y ** (second - 1)
        for other_index, other_power in enumerate(nodes):
            sum_x = first + other_power[0]
            sum_y = second + other_power[1]
            grams[column_index, other_index] = (
                4.0
                * math.factorial(sum_x)
                * math.factorial(sum_y)
                / math.factorial(sum_x + sum_y + 2)
            )
    deriv_r = solve_dense(vander.T, vander_r.T).T
    deriv_s = solve_dense(vander.T, vander_s.T).T
    mass_inverse = vander @ solve_dense(grams, vander.T)
    points = np.arange(degree + 1) / degree
    line_vander = np.stack([points**power for power in range(degree + 1)], axis=1)
    line_grams = np.array(
        [
            [2.0 / (first + second + 1) for second in range(degree + 1)]
            for first in range(degree + 1)
        ]
    )
    line_inverse = solve_dense(line_vander, np.eye(degree + 1))
    line_mass = line_inverse.T @ line_grams @ line_inverse
    lookup = {node: number for number, node in enumerate(nodes)}
    face_nodes = [
        [lookup[step, 0] for step in range(degree + 1)],
        [lookup[degree - step, step] for step in range(degree + 1)],
        [lookup[0, degree - step] for step in range(degree + 1)],
    ]
    embed = np.zeros((node_total, 3 * (degree + 1)))
    extract = np.zeros((3 * (degree + 1), node_total))
    for face_index in range(3):
        for step in range(degree + 1):
            extract[face_index * (degree + 1) + step, face_nodes[face_index][step]] = 1.0
            for other_step in range(degree + 1):
                embed[
                    face_nodes[face_index][other_step], face_index * (degree + 1) + step
                ] += line_mass[other_step, step]
    lifting = mass_inverse @ embed
    return deriv_r, deriv_s, lifting, extract


def offset_of(direction):
    return direction + 1 if direction < REACH else REACH - direction - 1


def neighbours():
    me = jnp.bitwise_and(lax.axis_index("dom"), GROUP - 1)
    found = []
    for own in (me + ROW, jnp.where(me < ROW, me, me + 2 * ROW)):
        for j in range(DIRS):
            place = own + offset_of(j)
            inner = (place >= ROW) & (place < ROW + GROUP)
            exists = (place >= 0) & (place < 4 * ROW)
            device = jnp.where(inner, place - ROW, jnp.where(place < ROW, place, place - 2 * ROW))
            found.append((jnp.where(exists, device, 0), jnp.where(inner, 0, 1), exists))
    return found


def parts3(matrix, width):
    padded = np.zeros((matrix.shape[0], width))
    padded[:, : matrix.shape[1]] = matrix
    hi = padded.astype(np.float32).astype(ml_dtypes.bfloat16)
    lo = (padded - hi.astype(np.float64)).astype(ml_dtypes.bfloat16)
    return np.concatenate([hi, lo, hi], axis=1)


def constants():
    deriv_r, deriv_s, lifting, extract = element_tables()

    def pad_rows(matrix):
        return np.concatenate([matrix, np.zeros((4, matrix.shape[1]))])

    lift = np.zeros((24, 28))
    flip = np.zeros((24, 28))
    take = np.zeros((24, 28))
    give = np.zeros((24, 28))
    for face in range(3):
        for k in range(7):
            lift[8 * face + k] = lifting[:, 7 * face + k]
            flip[8 * face + k] = lifting[:, 7 * face + 6 - k]
            take[8 * face + k] = extract[7 * face + k]
            give[8 * face + k] = extract[7 * face + k]
        take[8 * face + 7] = extract[7 * face + 6]
    back = np.concatenate([pad_rows(deriv_r.T), pad_rows(deriv_s.T), lift, flip])
    back3 = parts3(back, 32)
    flip3 = parts3(flip, 32)
    grad3 = parts3(np.concatenate([pad_rows(deriv_r), pad_rows(deriv_s)]), 32)
    take2 = np.zeros((24, 64))
    take2[:, 0:28] = take
    take2[:, 32:60] = take
    spread = np.concatenate([pad_rows(give.T), flip @ give.T])
    spread3 = parts3(spread, 24)
    spread3 = np.concatenate([spread3, np.zeros((56, 8), ml_dtypes.bfloat16)], axis=1)
    as_bf16 = lambda m: jnp.asarray(np.asarray(m).astype(ml_dtypes.bfloat16))
    return as_bf16(back3), as_bf16(flip3), as_bf16(grad3), as_bf16(take2), as_bf16(spread3)


def dot(a, b):
    return jnp.dot(a, b, preferred_element_type=F32)


def dot_nt(a, b):
    return lax.dot_general(a, b, (((1,), (1,)), ((), ())), preferred_element_type=F32)


def halves(x):
    hi = x.astype(BF16).astype(F32)
    return hi, x - hi


def times3(matrix3, x):
    hi = x.astype(BF16)
    lo = (x - hi.astype(F32)).astype(BF16)
    return dot(matrix3, jnp.concatenate([hi, hi, lo], axis=0))


def spread_faces(spread3, faces):
    hi, lo = halves(faces)
    stack = jnp.concatenate([hi, hi, lo, jnp.zeros((8, faces.shape[1]), F32)], axis=0)
    return dot(spread3, stack.astype(BF16))


def geometry(misc):
    rx, ry, sx, sy = misc[0:1], misc[1:2], misc[2:3], misc[3:4]
    normals = []
    for nx, ny in ((-sx, -sy), (rx + sx, ry + sy), (-rx, -ry)):
        normals.append((nx, ny, jnp.sqrt(nx * nx + ny * ny)))
    return (rx, ry, sx, sy), normals


def jump_back(n, t, u, v, gh):
    nx, ny, size = n
    un = nx * u + ny * v
    mixed = u * t[1] + v * t[2]
    pull = 0.5 * PENALTY * size
    return (
        0.5 * (gh * (nx * t[1] + ny * t[2]) - un * mixed) - pull * t[0],
        0.5 * (nx * (t[0] + mixed) + un * t[1]) - pull * t[1],
        0.5 * (ny * (t[0] + mixed) + un * t[2]) - pull * t[2],
    )


def traces(flipped, normals):
    last = lax.broadcasted_iota(jnp.int32, (8, E), 0) == 7
    rows = []
    for c in range(3):
        rows.append(
            jnp.concatenate(
                [jnp.where(last, normals[f][c], flipped[c][f]) for f in range(3)], axis=1
            )
        )
    return jnp.concatenate(rows, axis=0)


def far_index(link):
    v = link - 3 * E
    j = lax.shift_right_arithmetic(v, 4)
    c = jnp.bitwise_and(v, 15)
    row = lax.shift_right_arithmetic(c, 3) * 64 + j * 8 + jnp.bitwise_and(c, 7)
    return jnp.where(v >= 0, row, -1)


def slot_rows(sends, v, block):
    first = 64 * block
    n = v.shape[1]
    hi, lo = halves(v)
    rows = [jnp.zeros((first, n), F32)] if block else []
    rest = [jnp.zeros((32 - v.shape[0], n), F32)] if v.shape[0] < 32 else []
    rows += [hi] + rest + [lo] + rest + [jnp.zeros((64 - first, n), F32)] * (1 - block)
    out = dot_nt(sends, jnp.concatenate(rows, axis=0).astype(BF16))
    lane = lax.broadcasted_iota(jnp.int32, (128, 128), 1)
    out = jnp.where((lane >= first) & (lane < first + 32), out + pltpu.roll(out, 96, 1), 0.0)
    return out[0:64] + pltpu.roll(out[64:128], 32, 1)


def send(x_ref, near_by, boxes):
    x_ref[...] = jnp.zeros(x_ref.shape, F32)
    for b in range(2):
        for j in range(DIRS):
            device, _, exists = near_by[DIRS * b + j]
            rows = pl.ds(pl.multiple_of(device * 8, 8), 8)
            box = jnp.where(exists, boxes[b][8 * j : 8 * j + 8], 0.0)
            x_ref[rows, :] = x_ref[rows, :] + box


def send_matrix(misc):
    faces = misc[16:24]
    lane = lax.broadcasted_iota(jnp.int32, (8, 128), 1)
    low = jnp.where(lane < 8, faces, 0.0)
    high = jnp.where((lane >= 8) & (lane < 16), faces, 0.0)
    both = low + pltpu.roll(high, 56, 1)
    row = lax.broadcasted_iota(jnp.int32, (8, 128), 0)
    lined = jnp.zeros((8, 128), F32)
    for j in range(DIRS):
        moved = both if j == 0 else pltpu.roll(both, 8 * j, 1)
        lined = lined + jnp.where(row == j, moved, 0.0)
    line = jnp.sum(lined, axis=0, keepdims=True)
    column = jnp.transpose(jnp.broadcast_to(line, (128, 128)))
    face = lax.broadcasted_iota(jnp.int32, (128, 128), 1).astype(F32)
    pieces = [jnp.where(column == face + float(128 * f), 1.0, 0.0) for f in range(3)]
    return jnp.concatenate(pieces, axis=1).astype(BF16)


def pack_kernel(q_ref, lam_ref, depth_ref, metric_ref, tag_ref, link_ref, face_ref, out_ref):
    ones = jnp.ones((4, E), F32)
    for c in range(3):
        out_ref[c, 0:28, :] = lam_ref[c]
        out_ref[c, 28:32, :] = jnp.zeros((4, E), F32)
    for s in range(3):
        for c in range(3):
            out_ref[3 * (3 - s) + c, 0:28, :] = q_ref[s + 1, c]
            out_ref[3 * (3 - s) + c, 28:32, :] = ones
    out_ref[DEPTH, 0:28, :] = depth_ref[...]
    out_ref[DEPTH, 28:32, :] = ones
    out_ref[MISC] = jnp.zeros((32, E), F32)
    out_ref[MISC, 0:4, :] = metric_ref[...]
    out_ref[MISC, 4:7, :] = tag_ref[...].astype(F32)
    out_ref[MISC, 8:11, :] = link_ref[...].astype(F32)
    out_ref[MISC, 16:24, 0:16] = face_ref[...].astype(F32)


def first_boxes(part_ref, flip3, block):
    misc = part_ref[MISC]
    weights = jnp.concatenate([HALF * part_ref[c] for c in range(3)], axis=1)
    flipped = times3(flip3[...], weights)
    split = [
        [flipped[8 * f : 8 * f + 8, 128 * c : 128 * c + 128] for f in range(3)] for c in range(3)
    ]
    sends = send_matrix(misc)
    return sends, slot_rows(sends, traces(split, geometry(misc)[1]), block)


def own_first_kernel(part_ref, flip3, sends_ref, boxes_ref):
    sends_ref[...], boxes_ref[...] = first_boxes(part_ref, flip3, 0)


def halo_first_kernel(part_ref, flip3, boxes_ref, x_ref, sends_ref):
    sends_ref[...], boxes = first_boxes(part_ref, flip3, 1)
    send(x_ref, neighbours(), [boxes_ref[...], boxes])


def fold_kernel(y_ref, out_ref):
    total = y_ref[0:8, :]
    for e in range(1, GROUP):
        total = total + y_ref[8 * e : 8 * e + 8, :]
    out_ref[...] = jnp.broadcast_to(total[0:1, 127:128], out_ref.shape)


def near_kernel(section, blocks, *refs):
    refs = list(refs)
    drag = refs.pop(0)
    back3, flip3, grad3, take2, spread3 = [refs.pop(0)[...] for _ in range(5)]
    lams = [refs.pop(0) for _ in range(blocks)]
    parts = [refs.pop(0) for _ in range(blocks)]
    old_ref = refs.pop(0) if section < 3 else None
    if section == 0:
        state_ref, lam3_ref = refs.pop(0), refs.pop(0)
        speed_ref, angle_ref = refs.pop(0), refs.pop(0)
    base_ref = refs.pop(0)
    if section > 0:
        ahead_ref = refs.pop(0)
    motion_ref = refs.pop(0)
    if section > 0:
        sum_ref = refs.pop(0)
    else:
        depth_out, speed_out, angle_out = refs.pop(0), refs.pop(0), refs.pop(0)
    scale = SIXTH if section == 2 else HALF
    later = SIXTH if section == 3 else HALF
    drag_rate = drag[0]
    pad = jnp.ones((4, E), F32)

    lam = [[lams[b][c] for c in range(3)] for b in range(blocks)]
    w = [[scale * x for x in lam[b]] for b in range(blocks)]
    if section == 0:
        q = [[jnp.concatenate([state_ref[0, c], pad], axis=0) for c in range(3)]]
    else:
        q = [[parts[b][3 * (4 - section) + c] for c in range(3)] for b in range(blocks)]
    z = [parts[b][DEPTH] for b in range(blocks)]
    pulled = times3(back3, jnp.concatenate([x for b in range(blocks) for x in w[b]], axis=1))
    slopes = times3(grad3, jnp.concatenate(z, axis=1))
    fields = jnp.concatenate([x for b in range(blocks) for x in q[b] + [z[b]]], axis=1)
    hi, lo = halves(fields)
    at_faces = dot(take2, jnp.concatenate([hi, lo], axis=0).astype(BF16))

    face_sums, volumes, opens = [], [], []
    for b in range(blocks):
        misc = parts[b][MISC]
        (rx, ry, sx, sy), normals = geometry(misc)
        part = lambda r0, r1, c: pulled[r0:r1, 384 * b + 128 * c : 384 * b + 128 * c + 128]
        h = q[b][0]
        inv = 1.0 / h
        u, v = q[b][1] * inv, q[b][2] * inv
        gh = GRAVITY * h
        along = [part(0, 32, c) for c in range(3)]
        across = [part(32, 64, c) for c in range(3)]
        fx = [-(rx * along[c] + sx * across[c]) for c in range(3)]
        fy = [-(ry * along[c] + sy * across[c]) for c in range(3)]
        cross = fx[2] + fy[1]
        slope_r = slopes[0:32, 128 * b : 128 * b + 128]
        slope_s = slopes[32:64, 128 * b : 128 * b + 128]
        slope_x = rx * slope_r + sx * slope_s
        slope_y = ry * slope_r + sy * slope_s
        flow = u * w[b][1] + v * w[b][2]
        drag_inv = drag_rate * inv
        volumes.append(
            (
                gh * (fx[1] + fy[2])
                - u * (u * fx[1] + v * cross)
                - v * v * fy[2]
                + GRAVITY * (slope_x * w[b][1] + slope_y * w[b][2])
                + drag_inv * flow,
                fx[0] + 2.0 * u * fx[1] + v * cross - drag_inv * w[b][1],
                fy[0] + u * cross + 2.0 * v * fy[2] - drag_inv * w[b][2],
            )
        )
        own = [[part(64 + 8 * f, 72 + 8 * f, c) for f in range(3)] for c in range(3)]
        flipped = [[part(88 + 8 * f, 96 + 8 * f, c) for f in range(3)] for c in range(3)]
        hi, lo = halves(traces(flipped, normals))
        pool = jnp.concatenate([hi, lo], axis=0).astype(BF16)
        links = misc[8:11].astype(jnp.int32)
        rows = lax.broadcasted_iota(jnp.int32, (3 * E, E), 0)
        opened = []
        sums = [[], [], []]
        for f in range(3):
            match = jnp.where(rows == links[f : f + 1], 1.0, 0.0).astype(BF16)
            got = dot(pool, match)
            got = got[0:24] + got[24:48]
            value = lambda i: at_faces[
                8 * f : 8 * f + 8, 512 * b + 128 * i : 512 * b + 128 * i + 128
            ]
            fh, fm, fn, fz = value(0), value(1), value(2), value(3)
            finv = 1.0 / fh
            fu, fv, fgh = fm * finv, fn * finv, GRAVITY * fh
            motion_ref[b, 0, 8 * f : 8 * f + 8, :] = fu
            motion_ref[b, 1, 8 * f : 8 * f + 8, :] = fv
            motion_ref[b, 2, 8 * f : 8 * f + 8, :] = fgh
            tag = misc[4 + f : 5 + f]
            linked, wall, free = tag == 0.0, tag == 1.0, tag == 2.0
            nx, ny, size = normals[f]
            t = [own[c][f] for c in range(3)]
            mine = jump_back(normals[f], t, fu, fv, fgh)
            inv_size = 1.0 / size
            ux, uy = nx * inv_size, ny * inv_size
            twice = 2.0 * (ux * t[1] + uy * t[2])
            mirrored = (t[0], t[1] - twice * ux, t[2] - twice * uy)
            near = (got[0:8], got[8:16], got[16:24])
            other_n = tuple(
                jnp.where(linked, near[c][7:8], jnp.where(wall, m, 0.0))
                for c, m in enumerate((-nx, -ny, size))
            )
            other_t = [
                jnp.where(linked, near[c], jnp.where(wall, mirrored[c], 0.0)) for c in range(3)
            ]
            theirs = jump_back(other_n, other_t, fu, fv, fgh)
            zinv = 1.0 / fz
            out = jump_back(normals[f], t, fm * zinv, fn * zinv, GRAVITY * fz)
            opened.append(jnp.where(free, -out[0], 0.0))
            sums[0].append(mine[0] - theirs[0])
            sums[1].append(mine[1] - theirs[1] - jnp.where(free, out[1], 0.0))
            sums[2].append(mine[2] - theirs[2] - jnp.where(free, out[2], 0.0))
        face_sums.append([jnp.concatenate(sums[c], axis=0) for c in range(3)])
        if b == 0:
            opens = jnp.concatenate(opened, axis=0)
            height, moved = h, flow
    to_nodes = [x for b in range(blocks) for x in face_sums[b]]
    if section == 0:
        old = [old_ref[i] for i in range(5)]
        opens = opens + old[4][0:24]
        to_nodes.append(opens)
    nodes = spread_faces(spread3, jnp.concatenate(to_nodes, axis=1))
    for b in range(blocks):
        bases = []
        for c in range(3):
            first = lam[b][c]
            if section == 2:
                first = first * (1.0 / 3.0)
            if section == 0:
                first = first + (2.0 / 3.0) * lam3_ref[c]
            where = 384 * b + 128 * c
            bases.append(first + volumes[b][c] + nodes[0:32, where : where + 128])
            base_ref[b, c] = bases[c]
        if section > 0:
            ahead = times3(flip3, later * jnp.concatenate(bases, axis=1))
            for c in range(3):
                ahead_ref[b, c] = ahead[:, 128 * c : 128 * c + 128]
    w1, w2 = w[0][1], w[0][2]
    g1, g2 = height * w1, height * w2
    if section == 3:
        fold = moved[0:8] + moved[8:16] + moved[16:24] + moved[24:32]
        news = [w1, w2, g1, g2]
    else:
        if section > 0:
            old = [old_ref[i] for i in range(5)]
            opens = opens + old[4][0:24]
            fold = old[4][24:32] + (moved[0:8] + moved[8:16] + moved[16:24] + moved[24:32])
        news = [x + y for x, y in zip(old[0:4], (w1, w2, g1, g2))]
    if section > 0:
        for i in range(4):
            sum_ref[i] = news[i]
        sum_ref[4, 0:24, :] = opens
        sum_ref[4, 24:32, :] = fold
    else:
        rx, ry, sx, sy = geometry(parts[0][MISC])[0]
        w1, w2, g1, g2 = news
        pair = GRAVITY * jnp.concatenate([rx * g1 + ry * g2, sx * g1 + sy * g2], axis=1)
        pulled = times3(back3, pair)
        depth = pulled[0:32, 0:128] + pulled[32:64, 128:256] + nodes[0:32, 384:512]
        depth_out[...] = depth[0:28]
        speed, angle = speed_ref[...], angle_ref[...]
        cosine, sine = jnp.cos(angle), jnp.sin(angle)
        w1, w2 = w1[0:28], w2[0:28]
        speed_out[...] = (2.0 * WIND_COEF) * speed * (cosine * w1 + sine * w2)
        angle_out[...] = WIND_COEF * speed * speed * (cosine * w2 - sine * w1)


def far_kernel(section, blocks, *refs):
    refs = list(refs)
    y_ref, spread3_ref, base_ref, motion_ref = [refs.pop(0) for _ in range(4)]
    parts = [refs.pop(0) for _ in range(blocks)]
    if section > 0:
        ahead_ref = refs.pop(0)
        sends_refs = [refs.pop(0), refs.pop(0)]
    if section == 1:
        q0_ref, sum_ref = refs.pop(0), refs.pop(0)
    lam_refs = [refs.pop(0) for _ in range(blocks)]
    if section > 0:
        x_ref = refs.pop(0)
    later = SIXTH if section == 3 else HALF

    near_by = neighbours()
    boxes = []
    for b in range(2):
        for j in range(DIRS):
            if b < blocks:
                device, second, exists = near_by[DIRS * b + j]
                box = y_ref[pl.ds(pl.multiple_of(device * 8, 8), 8), :]
                box = jnp.where(second == 1, pltpu.roll(box, 64, 1), box)
                boxes.append(jnp.where(exists, box, 0.0))
            else:
                boxes.append(jnp.zeros((8, 128), F32))
    turned = jnp.transpose(jnp.concatenate(boxes, axis=0))
    low, high = turned[0:24], turned[32:56]
    left = lax.broadcasted_iota(jnp.int32, (24, 128), 1) < 64
    rows = lax.broadcasted_iota(jnp.int32, (128, E), 0)
    face_sums = []
    for b in range(blocks):
        if b == 0:
            pool = jnp.where(left, low, pltpu.roll(high, 64, 1))
        else:
            pool = jnp.where(left, pltpu.roll(low, 64, 1), high)
        pool = jnp.concatenate(halves(pool), axis=0).astype(BF16)
        links = parts[b][MISC, 8:11].astype(jnp.int32)
        match = [
            jnp.where(rows == far_index(links[f : f + 1]), 1.0, 0.0).astype(BF16) for f in range(3)
        ]
        got = dot(pool, jnp.concatenate(match, axis=1))
        got = got[0:24] + got[24:48]
        sums = [[], [], []]
        for f in range(3):
            far = [got[8 * c : 8 * c + 8, 128 * f : 128 * f + 128] for c in range(3)]
            motion = [motion_ref[b, i, 8 * f : 8 * f + 8, :] for i in range(3)]
            theirs = jump_back(tuple(x[7:8] for x in far), far, *motion)
            for c in range(3):
                sums[c].append(-theirs[c])
        face_sums += [jnp.concatenate(sums[c], axis=0) for c in range(3)]
    spread = spread_faces(spread3_ref[...], jnp.concatenate(face_sums, axis=1))
    trace_list = []
    for b in range(blocks):
        lam = []
        for c in range(3):
            where = 384 * b + 128 * c
            lam.append(base_ref[b, c] + spread[0:32, where : where + 128])
        if section > 0:
            for c in range(3):
                lam_refs[b][c] = lam[c]
            flipped = [
                ahead_ref[b, c]
                + later * spread[32:56, 384 * b + 128 * c : 384 * b + 128 * c + 128]
                for c in range(3)
            ]
            split = [[flipped[c][8 * f : 8 * f + 8] for f in range(3)] for c in range(3)]
            trace_list.append(traces(split, geometry(parts[b][MISC])[1]))
        else:
            for c in range(3):
                lam_refs[b][c] = lam[c][0:28]
        if section == 1 and b == 0:
            first = lam
    if section > 0:
        boxes = [slot_rows(sends_refs[b][...], trace_list[b], b) for b in range(2)]
        send(x_ref, near_by, boxes)
    if section == 1:
        q0 = [q0_ref[0, c] for c in range(3)]
        flow = (q0[1] * first[1][0:28] + q0[2] * first[2][0:28]) * (HALF / q0[0])
        total = jnp.sum(sum_ref[4, 24:32, :]) + jnp.sum(flow)
        lane = lax.broadcasted_iota(jnp.int32, (8, 128), 1)
        for e in range(GROUP):
            part = x_ref[8 * e : 8 * e + 8, :]
            x_ref[8 * e : 8 * e + 8, :] = jnp.where(lane == 127, -total, part)


def call(kernel, outs, args, scalars=0):
    vmem, smem = pl.BlockSpec(memory_space=pltpu.VMEM), pl.BlockSpec(memory_space=pltpu.SMEM)
    return pl.pallas_call(
        kernel,
        in_specs=[smem] * scalars + [vmem] * (len(args) - scalars),
        out_specs=[vmem] * len(outs),
        out_shape=[jax.ShapeDtypeStruct(shape, dtype) for shape, dtype in outs],
        compiler_params=pltpu.CompilerParams(vmem_limit_bytes=32 * 1024 * 1024),
    )(*args)


def local(
    saved_states,
    adjoint_final,
    bathymetry,
    wind_speed,
    wind_angle,
    drag_rate,
    metrics,
    face_link,
    face_tag,
    send_faces,
):
    devices = lax.axis_size("dom")
    groups = [list(range(g, g + GROUP)) for g in range(0, devices, GROUP)]
    strides = [list(range(d, devices, GROUP)) for d in range(GROUP)]
    back3, flip3, grad3, take2, spread3 = constants()
    tables = [back3, flip3, grad3, take2, spread3]

    mixed, x_out = ((3, 32, E), F32), ((GROUP * 8, 128), F32)
    sends_out, sums_out = ((128, 384), BF16), ((5, 32, E), F32)
    pairs = [(i, i) for i in range(ROW)] + [(i, i) for i in range(devices - ROW, devices)]
    for row in range(1, devices // ROW - 1, 2):
        for i in range(row * ROW, row * ROW + ROW):
            pairs += [(i, i + ROW), (i + ROW, i)]
    pack_args = (saved_states, adjoint_final, bathymetry)
    pack_args += (metrics, face_tag, face_link, send_faces)
    mine = call(pack_kernel, [((14, 32, E), F32)], pack_args)[0]
    halo = lax.ppermute(mine, "dom", pairs)
    both = [mine, halo]

    my_sends, boxes = call(own_first_kernel, [sends_out, ((64, 128), F32)], (mine, flip3))
    x, halo_sends = call(halo_first_kernel, [x_out, sends_out], (halo, flip3, boxes))
    lams = both
    sums = []
    for section in (3, 2, 1, 0):
        y = lax.all_to_all(x, "dom", 0, 0, tiled=True, axis_index_groups=groups)
        blocks = 2 if section > 0 else 1
        bases, faces = ((blocks, 3, 32, E), F32), ((blocks, 3, 24, E), F32)
        args = [drag_rate] + tables + list(lams[:blocks]) + both[:blocks] + sums
        if section > 0:
            outs = [bases, faces, faces, sums_out]
        else:
            args += [saved_states, lam3, wind_speed, wind_angle]
            outs = [bases, faces] + [((28, E), F32)] * 3
        got = call(lambda *refs, s=section, n=blocks: near_kernel(s, n, *refs), outs, args, 1)
        if section > 0:
            base, ahead, motion = got[:3]
            sums = list(got[3:])
        else:
            base, motion, depth_gradient, speed_gradient, angle_gradient = got

        args = [y, spread3, base, motion] + both[:blocks]
        if section > 0:
            args += [ahead, my_sends, halo_sends]
            outs = [mixed] * 2 + [x_out]
        else:
            outs = [((3, 28, E), F32)]
        if section == 1:
            args += [saved_states] + sums
        got = call(lambda *refs, s=section, n=blocks: far_kernel(s, n, *refs), outs, args)
        if section > 0:
            lams, x = got[0:2], got[2]
            if section == 3:
                lam3 = lams[0]
        else:
            initial = got[0]
    y, initial = lax.optimization_barrier((y, initial))
    within = call(fold_kernel, [((devices // GROUP, 128), F32)], (y,))[0]
    spread = lax.all_to_all(within, "dom", 0, 0, tiled=True, axis_index_groups=strides)
    drag_gradient = jnp.sum(spread[:, 0]).reshape(1)
    return (initial, depth_gradient, speed_gradient, angle_gradient, drag_gradient)


def solution(mesh):
    return jax.shard_map(
        local,
        mesh=mesh,
        in_specs=(
            P(None, None, None, "dom"),
            P(None, None, "dom"),
            P(None, "dom"),
            P(None, "dom"),
            P(None, "dom"),
            P(),
            P(None, "dom"),
            P(None, "dom"),
            P(None, "dom"),
            P(None, "dom"),
        ),
        out_specs=(P(None, None, "dom"), P(None, "dom"), P(None, "dom"), P(None, "dom"), P()),
        check_vma=False,
    )
```

```python
import math

import jax
import jax.numpy as jnp
import ml_dtypes
import numpy as np
from jax import lax
from jax.experimental import pallas as pl
from jax.experimental.pallas import tpu as pltpu
from jax.sharding import PartitionSpec as P

GRAVITY = 1.0
PENALTY = 3.0
WIND_COEF = 5.0
TIME_STEP = 0.01
HALF = 0.5 * TIME_STEP
SIXTH = TIME_STEP / 6.0

GROUP = 32
STRIDE = 16
ROW = 16
REACH = 4
DIRS = 8
SLOTS = 16
E = 128
DEPTH, MISC = 12, 13
F32 = jnp.float32
BF16 = jnp.bfloat16


def solve_dense(matrix, right):
    system = np.array(matrix) + 0.0
    result = np.array(right) + 0.0
    extent = system.shape[0]
    for column in range(extent):
        pivot_index = column + int(np.argmax(np.abs(system[column:, column])))
        system[[column, pivot_index]] = system[[pivot_index, column]]
        result[[column, pivot_index]] = result[[pivot_index, column]]
        for target in range(column + 1, extent):
            factor = system[target, column] / system[column, column]
            system[target] = system[target] - factor * system[column]
            result[target] = result[target] - factor * result[column]
    solution = np.zeros(result.shape)
    for column in range(extent - 1, -1, -1):
        solution[column] = (
            result[column] - system[column, column + 1 :] @ solution[column + 1 :]
        ) / system[column, column]
    return solution


def element_tables():
    degree = 6
    nodes = [
        (column, row_index)
        for row_index in range(degree + 1)
        for column in range(degree + 1 - row_index)
    ]
    node_total = len(nodes)
    coord_x = np.array([node[0] / degree for node in nodes])
    coord_y = np.array([node[1] / degree for node in nodes])
    vander = np.zeros((node_total, node_total))
    vander_r = np.zeros((node_total, node_total))
    vander_s = np.zeros((node_total, node_total))
    grams = np.zeros((node_total, node_total))
    for column_index, power in enumerate(nodes):
        first, second = power
        vander[:, column_index] = coord_x**first * coord_y**second
        if first > 0:
            vander_r[:, column_index] = 0.5 * first * coord_x ** (first - 1) * coord_y**second
        if second > 0:
            vander_s[:, column_index] = 0.5 * second * coord_x**first * coord_y ** (second - 1)
        for other_index, other_power in enumerate(nodes):
            sum_x = first + other_power[0]
            sum_y = second + other_power[1]
            grams[column_index, other_index] = (
                4.0
                * math.factorial(sum_x)
                * math.factorial(sum_y)
                / math.factorial(sum_x + sum_y + 2)
            )
    deriv_r = solve_dense(vander.T, vander_r.T).T
    deriv_s = solve_dense(vander.T, vander_s.T).T
    mass_inverse = vander @ solve_dense(grams, vander.T)
    points = np.arange(degree + 1) / degree
    line_vander = np.stack([points**power for power in range(degree + 1)], axis=1)
    line_grams = np.array(
        [
            [2.0 / (first + second + 1) for second in range(degree + 1)]
            for first in range(degree + 1)
        ]
    )
    line_inverse = solve_dense(line_vander, np.eye(degree + 1))
    line_mass = line_inverse.T @ line_grams @ line_inverse
    lookup = {node: number for number, node in enumerate(nodes)}
    face_nodes = [
        [lookup[step, 0] for step in range(degree + 1)],
        [lookup[degree - step, step] for step in range(degree + 1)],
        [lookup[0, degree - step] for step in range(degree + 1)],
    ]
    embed = np.zeros((node_total, 3 * (degree + 1)))
    extract = np.zeros((3 * (degree + 1), node_total))
    for face_index in range(3):
        for step in range(degree + 1):
            extract[face_index * (degree + 1) + step, face_nodes[face_index][step]] = 1.0
            for other_step in range(degree + 1):
                embed[
                    face_nodes[face_index][other_step], face_index * (degree + 1) + step
                ] += line_mass[other_step, step]
    lifting = mass_inverse @ embed
    return deriv_r, deriv_s, lifting, extract


def offset_of(direction):
    return direction + 1 if direction < REACH else REACH - direction - 1


def neighbours():
    me = jnp.bitwise_and(lax.axis_index("dom"), GROUP - 1)
    found = []
    for own in (me + ROW, jnp.where(me < ROW, me, me + 2 * ROW)):
        for j in range(DIRS):
            place = own + offset_of(j)
            inner = (place >= ROW) & (place < ROW + GROUP)
            exists = (place >= 0) & (place < 4 * ROW)
            device = jnp.where(inner, place - ROW, jnp.where(place < ROW, place, place - 2 * ROW))
            found.append((jnp.where(exists, device, 0), jnp.where(inner, 0, 1), exists))
    return found


def spread_steps():
    return [(q // 4, q % 4, 1 if q % 4 in (1, 2) else 0) for q in range(STRIDE)]


def spread_pairs(devices):
    pairs = []
    for group in range(devices // GROUP):
        for q, (dx, dy, row) in enumerate(spread_steps()):
            other = (group // 4 + dx) % 4 * 4 + (group % 4 + dy) % 4
            other_row = 0 if dy == 0 else 1 - row
            pairs.append((other * GROUP + other_row * ROW + q, group * GROUP + row * ROW + q))
    return pairs


def parts3(matrix, width):
    padded = np.zeros((matrix.shape[0], width))
    padded[:, : matrix.shape[1]] = matrix
    hi = padded.astype(np.float32).astype(ml_dtypes.bfloat16)
    lo = (padded - hi.astype(np.float64)).astype(ml_dtypes.bfloat16)
    return np.concatenate([hi, lo, hi], axis=1)


def constants():
    deriv_r, deriv_s, lifting, extract = element_tables()

    def pad_rows(matrix):
        return np.concatenate([matrix, np.zeros((4, matrix.shape[1]))])

    lift = np.zeros((24, 28))
    flip = np.zeros((24, 28))
    take = np.zeros((24, 28))
    give = np.zeros((24, 28))
    for face in range(3):
        for k in range(7):
            lift[8 * face + k] = lifting[:, 7 * face + k]
            flip[8 * face + k] = lifting[:, 7 * face + 6 - k]
            take[8 * face + k] = extract[7 * face + k]
            give[8 * face + k] = extract[7 * face + k]
        take[8 * face + 7] = extract[7 * face + 6]
    back = np.concatenate([pad_rows(deriv_r.T), pad_rows(deriv_s.T), lift, flip])
    back3 = parts3(back, 32)
    flip3 = parts3(flip, 32)
    grad3 = parts3(np.concatenate([pad_rows(deriv_r), pad_rows(deriv_s)]), 32)
    take2 = np.zeros((24, 64))
    take2[:, 0:28] = take
    take2[:, 32:60] = take
    spread = np.concatenate([pad_rows(give.T), flip @ give.T])
    spread3 = parts3(spread, 24)
    spread3 = np.concatenate([spread3, np.zeros((56, 8), ml_dtypes.bfloat16)], axis=1)
    as_bf16 = lambda m: jnp.asarray(np.asarray(m).astype(ml_dtypes.bfloat16))
    return as_bf16(back3), as_bf16(flip3), as_bf16(grad3), as_bf16(take2), as_bf16(spread3)


def dot(a, b):
    return jnp.dot(a, b, preferred_element_type=F32)


def dot_nt(a, b):
    return lax.dot_general(a, b, (((1,), (1,)), ((), ())), preferred_element_type=F32)


def halves(x):
    hi = x.astype(BF16).astype(F32)
    return hi, x - hi


def times3(matrix3, x):
    hi = x.astype(BF16)
    lo = (x - hi.astype(F32)).astype(BF16)
    return dot(matrix3, jnp.concatenate([hi, hi, lo], axis=0))


def spread_faces(spread3, faces):
    hi, lo = halves(faces)
    stack = jnp.concatenate([hi, hi, lo, jnp.zeros((8, faces.shape[1]), F32)], axis=0)
    return dot(spread3, stack.astype(BF16))


def geometry(misc):
    rx, ry, sx, sy = misc[0:1], misc[1:2], misc[2:3], misc[3:4]
    normals = []
    for nx, ny in ((-sx, -sy), (rx + sx, ry + sy), (-rx, -ry)):
        normals.append((nx, ny, jnp.sqrt(nx * nx + ny * ny)))
    return (rx, ry, sx, sy), normals


def jump_back(n, t, u, v, gh):
    nx, ny, size = n
    un = nx * u + ny * v
    mixed = u * t[1] + v * t[2]
    pull = 0.5 * PENALTY * size
    return (
        0.5 * (gh * (nx * t[1] + ny * t[2]) - un * mixed) - pull * t[0],
        0.5 * (nx * (t[0] + mixed) + un * t[1]) - pull * t[1],
        0.5 * (ny * (t[0] + mixed) + un * t[2]) - pull * t[2],
    )


def traces(flipped, normals):
    last = lax.broadcasted_iota(jnp.int32, (8, E), 0) == 7
    rows = []
    for c in range(3):
        rows.append(
            jnp.concatenate(
                [jnp.where(last, normals[f][c], flipped[c][f]) for f in range(3)], axis=1
            )
        )
    return jnp.concatenate(rows, axis=0)


def far_index(link):
    v = link - 3 * E
    j = lax.shift_right_arithmetic(v, 4)
    c = jnp.bitwise_and(v, 15)
    row = lax.shift_right_arithmetic(c, 3) * 64 + j * 8 + jnp.bitwise_and(c, 7)
    return jnp.where(v >= 0, row, -1)


def slot_rows(sends, v, block):
    first = 64 * block
    n = v.shape[1]
    hi, lo = halves(v)
    rows = [jnp.zeros((first, n), F32)] if block else []
    rest = [jnp.zeros((32 - v.shape[0], n), F32)] if v.shape[0] < 32 else []
    rows += [hi] + rest + [lo] + rest + [jnp.zeros((64 - first, n), F32)] * (1 - block)
    out = dot_nt(sends, jnp.concatenate(rows, axis=0).astype(BF16))
    lane = lax.broadcasted_iota(jnp.int32, (128, 128), 1)
    out = jnp.where((lane >= first) & (lane < first + 32), out + pltpu.roll(out, 96, 1), 0.0)
    return out[0:64] + pltpu.roll(out[64:128], 32, 1)


def send(x_ref, near_by, boxes):
    x_ref[...] = jnp.zeros(x_ref.shape, F32)
    for b in range(2):
        for j in range(DIRS):
            device, _, exists = near_by[DIRS * b + j]
            rows = pl.ds(pl.multiple_of(device * 8, 8), 8)
            box = jnp.where(exists, boxes[b][8 * j : 8 * j + 8], 0.0)
            x_ref[rows, :] = x_ref[rows, :] + box


def send_matrix(misc):
    faces = misc[16:24]
    lane = lax.broadcasted_iota(jnp.int32, (8, 128), 1)
    low = jnp.where(lane < 8, faces, 0.0)
    high = jnp.where((lane >= 8) & (lane < 16), faces, 0.0)
    both = low + pltpu.roll(high, 56, 1)
    row = lax.broadcasted_iota(jnp.int32, (8, 128), 0)
    lined = jnp.zeros((8, 128), F32)
    for j in range(DIRS):
        moved = both if j == 0 else pltpu.roll(both, 8 * j, 1)
        lined = lined + jnp.where(row == j, moved, 0.0)
    line = jnp.sum(lined, axis=0, keepdims=True)
    column = jnp.transpose(jnp.broadcast_to(line, (128, 128)))
    face = lax.broadcasted_iota(jnp.int32, (128, 128), 1).astype(F32)
    pieces = [jnp.where(column == face + float(128 * f), 1.0, 0.0) for f in range(3)]
    return jnp.concatenate(pieces, axis=1).astype(BF16)


def pack_kernel(q_ref, lam_ref, depth_ref, metric_ref, tag_ref, link_ref, face_ref, out_ref):
    ones = jnp.ones((4, E), F32)
    for c in range(3):
        out_ref[c, 0:28, :] = lam_ref[c]
        out_ref[c, 28:32, :] = jnp.zeros((4, E), F32)
    for s in range(3):
        for c in range(3):
            out_ref[3 * (3 - s) + c, 0:28, :] = q_ref[s + 1, c]
            out_ref[3 * (3 - s) + c, 28:32, :] = ones
    out_ref[DEPTH, 0:28, :] = depth_ref[...]
    out_ref[DEPTH, 28:32, :] = ones
    out_ref[MISC] = jnp.zeros((32, E), F32)
    out_ref[MISC, 0:4, :] = metric_ref[...]
    out_ref[MISC, 4:7, :] = tag_ref[...].astype(F32)
    out_ref[MISC, 8:11, :] = link_ref[...].astype(F32)
    out_ref[MISC, 16:24, 0:16] = face_ref[...].astype(F32)


def first_boxes(part_ref, flip3, block):
    misc = part_ref[MISC]
    weights = jnp.concatenate([HALF * part_ref[c] for c in range(3)], axis=1)
    flipped = times3(flip3[...], weights)
    split = [
        [flipped[8 * f : 8 * f + 8, 128 * c : 128 * c + 128] for f in range(3)] for c in range(3)
    ]
    sends = send_matrix(misc)
    return sends, slot_rows(sends, traces(split, geometry(misc)[1]), block)


def own_first_kernel(part_ref, flip3, drag_ref, *refs):
    sends_ref, boxes_ref, rate_ref = refs[-3:]
    rate_ref[...] = jnp.full((8, E), drag_ref[0], F32)
    sends_ref[...], boxes_ref[...] = first_boxes(part_ref, flip3, 0)


def halo_first_kernel(part_ref, flip3, boxes_ref, x_ref, sends_ref):
    sends_ref[...], boxes = first_boxes(part_ref, flip3, 1)
    send(x_ref, neighbours(), [boxes_ref[...], boxes])


def near_kernel(section, blocks, *refs):
    refs = list(refs)
    back3, flip3, grad3, take2, spread3 = [refs.pop(0)[...] for _ in range(5)]
    rate_ref = refs.pop(0)
    lams = [refs.pop(0) for _ in range(blocks)]
    parts = [refs.pop(0) for _ in range(blocks)]
    old_ref = refs.pop(0) if section < 3 else None
    if section == 3:
        state_ref = refs.pop(0)
    if section == 0:
        state_ref, lam3_ref = refs.pop(0), refs.pop(0)
        speed_ref, angle_ref = refs.pop(0), refs.pop(0)
    base_ref = refs.pop(0)
    if section > 0:
        ahead_ref = refs.pop(0)
    motion_ref = refs.pop(0)
    if section == 3:
        past_ref = refs.pop(0)
    if section > 0:
        sum_ref = refs.pop(0)
    else:
        depth_out, speed_out, angle_out = refs.pop(0), refs.pop(0), refs.pop(0)
    scale = SIXTH if section == 2 else HALF
    later = SIXTH if section == 3 else HALF
    drag_rate = rate_ref[...][0:1]
    pad = jnp.ones((4, E), F32)

    lam = [[lams[b][c] for c in range(3)] for b in range(blocks)]
    w = [[scale * x for x in lam[b]] for b in range(blocks)]
    if section == 0:
        q = [[jnp.concatenate([state_ref[0, c], pad], axis=0) for c in range(3)]]
    else:
        q = [[parts[b][3 * (4 - section) + c] for c in range(3)] for b in range(blocks)]
    z = [parts[b][DEPTH] for b in range(blocks)]
    pulled = times3(back3, jnp.concatenate([x for b in range(blocks) for x in w[b]], axis=1))
    slopes = times3(grad3, jnp.concatenate(z, axis=1))
    fields = jnp.concatenate([x for b in range(blocks) for x in q[b] + [z[b]]], axis=1)
    hi, lo = halves(fields)
    at_faces = dot(take2, jnp.concatenate([hi, lo], axis=0).astype(BF16))

    if section == 3:
        fields = [jnp.concatenate([state_ref[0, c], pad], axis=0) for c in range(3)]
        fields += [parts[0][9 + c] for c in range(3)]
        hi, lo = halves(jnp.concatenate(fields, axis=1))
        past = dot(take2, jnp.concatenate([hi, lo], axis=0).astype(BF16))
        for i in range(2):
            finv = 1.0 / past[:, 384 * i : 384 * i + 128]
            past_ref[2 * i] = past[:, 384 * i + 128 : 384 * i + 256] * finv
            past_ref[2 * i + 1] = past[:, 384 * i + 256 : 384 * i + 384] * finv

    face_sums, volumes, opens = [], [], []
    for b in range(blocks):
        misc = parts[b][MISC]
        (rx, ry, sx, sy), normals = geometry(misc)
        part = lambda r0, r1, c: pulled[r0:r1, 384 * b + 128 * c : 384 * b + 128 * c + 128]
        h = q[b][0]
        inv = 1.0 / h
        u, v = q[b][1] * inv, q[b][2] * inv
        gh = GRAVITY * h
        along = [part(0, 32, c) for c in range(3)]
        across = [part(32, 64, c) for c in range(3)]
        fx = [-(rx * along[c] + sx * across[c]) for c in range(3)]
        fy = [-(ry * along[c] + sy * across[c]) for c in range(3)]
        cross = fx[2] + fy[1]
        slope_r = slopes[0:32, 128 * b : 128 * b + 128]
        slope_s = slopes[32:64, 128 * b : 128 * b + 128]
        slope_x = rx * slope_r + sx * slope_s
        slope_y = ry * slope_r + sy * slope_s
        flow = u * w[b][1] + v * w[b][2]
        drag_inv = drag_rate * inv
        volumes.append(
            (
                gh * (fx[1] + fy[2])
                - u * (u * fx[1] + v * cross)
                - v * v * fy[2]
                + GRAVITY * (slope_x * w[b][1] + slope_y * w[b][2])
                + drag_inv * flow,
                fx[0] + 2.0 * u * fx[1] + v * cross - drag_inv * w[b][1],
                fy[0] + u * cross + 2.0 * v * fy[2] - drag_inv * w[b][2],
            )
        )
        own = [[part(64 + 8 * f, 72 + 8 * f, c) for f in range(3)] for c in range(3)]
        flipped = [[part(88 + 8 * f, 96 + 8 * f, c) for f in range(3)] for c in range(3)]
        hi, lo = halves(traces(flipped, normals))
        pool = jnp.concatenate([hi, lo], axis=0).astype(BF16)
        links = misc[8:11].astype(jnp.int32)
        rows = lax.broadcasted_iota(jnp.int32, (3 * E, E), 0)
        opened = []
        sums = [[], [], []]
        for f in range(3):
            match = jnp.where(rows == links[f : f + 1], 1.0, 0.0).astype(BF16)
            got = dot(pool, match)
            got = got[0:24] + got[24:48]
            value = lambda i: at_faces[
                8 * f : 8 * f + 8, 512 * b + 128 * i : 512 * b + 128 * i + 128
            ]
            fh, fm, fn, fz = value(0), value(1), value(2), value(3)
            finv = 1.0 / fh
            fu, fv, fgh = fm * finv, fn * finv, GRAVITY * fh
            motion_ref[b, 0, 8 * f : 8 * f + 8, :] = fu
            motion_ref[b, 1, 8 * f : 8 * f + 8, :] = fv
            motion_ref[b, 2, 8 * f : 8 * f + 8, :] = fgh
            tag = misc[4 + f : 5 + f]
            linked, wall, free = tag == 0.0, tag == 1.0, tag == 2.0
            nx, ny, size = normals[f]
            t = [own[c][f] for c in range(3)]
            mine = jump_back(normals[f], t, fu, fv, fgh)
            inv_size = 1.0 / size
            ux, uy = nx * inv_size, ny * inv_size
            twice = 2.0 * (ux * t[1] + uy * t[2])
            mirrored = (t[0], t[1] - twice * ux, t[2] - twice * uy)
            near = (got[0:8], got[8:16], got[16:24])
            other_n = tuple(
                jnp.where(linked, near[c][7:8], jnp.where(wall, m, 0.0))
                for c, m in enumerate((-nx, -ny, size))
            )
            other_t = [
                jnp.where(linked, near[c], jnp.where(wall, mirrored[c], 0.0)) for c in range(3)
            ]
            theirs = jump_back(other_n, other_t, fu, fv, fgh)
            zinv = 1.0 / fz
            out = jump_back(normals[f], t, fm * zinv, fn * zinv, GRAVITY * fz)
            opened.append(jnp.where(free, -out[0], 0.0))
            sums[0].append(mine[0] - theirs[0])
            sums[1].append(mine[1] - theirs[1] - jnp.where(free, out[1], 0.0))
            sums[2].append(mine[2] - theirs[2] - jnp.where(free, out[2], 0.0))
        face_sums.append([jnp.concatenate(sums[c], axis=0) for c in range(3)])
        if b == 0:
            opens = jnp.concatenate(opened, axis=0)
            height, moved = h, flow
    to_nodes = [x for b in range(blocks) for x in face_sums[b]]
    if section == 0:
        old = [old_ref[i] for i in range(5)]
        opens = opens + old[4][0:24]
        to_nodes.append(opens)
    nodes = spread_faces(spread3, jnp.concatenate(to_nodes, axis=1))
    for b in range(blocks):
        bases = []
        for c in range(3):
            first = lam[b][c]
            if section == 2:
                first = first * (1.0 / 3.0)
            if section == 0:
                first = first + (2.0 / 3.0) * lam3_ref[c]
            where = 384 * b + 128 * c
            bases.append(first + volumes[b][c] + nodes[0:32, where : where + 128])
            base_ref[b, c] = bases[c]
        if section > 0:
            ahead = times3(flip3, later * jnp.concatenate(bases, axis=1))
            for c in range(3):
                ahead_ref[b, c] = ahead[:, 128 * c : 128 * c + 128]
    w1, w2 = w[0][1], w[0][2]
    g1, g2 = height * w1, height * w2
    if section == 3:
        fold = moved[0:8] + moved[8:16] + moved[16:24] + moved[24:32]
        news = [w1, w2, g1, g2]
    else:
        if section > 0:
            old = [old_ref[i] for i in range(5)]
            opens = opens + old[4][0:24]
            fold = old[4][24:32] + (moved[0:8] + moved[8:16] + moved[16:24] + moved[24:32])
        news = [x + y for x, y in zip(old[0:4], (w1, w2, g1, g2))]
    if section > 0:
        for i in range(4):
            sum_ref[i] = news[i]
        sum_ref[4, 0:24, :] = opens
        sum_ref[4, 24:32, :] = fold
    else:
        rx, ry, sx, sy = geometry(parts[0][MISC])[0]
        w1, w2, g1, g2 = news
        pair = GRAVITY * jnp.concatenate([rx * g1 + ry * g2, sx * g1 + sy * g2], axis=1)
        pulled = times3(back3, pair)
        depth = pulled[0:32, 0:128] + pulled[32:64, 128:256] + nodes[0:32, 384:512]
        depth_out[...] = depth[0:28]
        speed, angle = speed_ref[...], angle_ref[...]
        cosine, sine = jnp.cos(angle), jnp.sin(angle)
        w1, w2 = w1[0:28], w2[0:28]
        speed_out[...] = (2.0 * WIND_COEF) * speed * (cosine * w1 + sine * w2)
        angle_out[...] = WIND_COEF * speed * speed * (cosine * w2 - sine * w1)


def far_kernel(section, blocks, *refs):
    refs = list(refs)
    y_ref, spread3_ref, base_ref, motion_ref = [refs.pop(0) for _ in range(4)]
    parts = [refs.pop(0) for _ in range(blocks)]
    if section < 3:
        normal_ref = refs.pop(0)
    if section > 0:
        ahead_ref = refs.pop(0)
        sends_refs = [refs.pop(0), refs.pop(0)]
    if section == 3:
        past_ref = refs.pop(0)
    lam_refs = [refs.pop(0) for _ in range(blocks)]
    if section > 0:
        x_ref = refs.pop(0)
    if section == 3:
        normal_ref = refs.pop(0)
    if section == 0:
        drag_ref = refs.pop(0)
    later = SIXTH if section == 3 else HALF

    lane = lax.broadcasted_iota(jnp.int32, (8, 128), 1)
    place_in = jnp.bitwise_and(lane, 31)
    spare = (place_in >= 24) | (place_in == 7) | (place_in == 15) | (place_in == 23)
    near_by = neighbours()
    boxes, extras = [], []
    for b in range(2):
        for j in range(DIRS):
            if b < blocks:
                device, second, exists = near_by[DIRS * b + j]
                raw = y_ref[pl.ds(pl.multiple_of(device * 8, 8), 8), :]
                turned = pltpu.roll(raw, 64, 1)
                if section == 2:
                    box = jnp.where(second == 1, jnp.where(spare, 0.0, turned), raw)
                    extras.append(jnp.where(exists & (second == 0), turned, 0.0))
                else:
                    box = jnp.where(second == 1, turned, raw)
                boxes.append(jnp.where(exists, box, 0.0))
            else:
                boxes.append(jnp.zeros((8, 128), F32))
    stacks = [jnp.transpose(jnp.concatenate(boxes, axis=0))]
    if section == 2:
        stacks.append(jnp.transpose(jnp.concatenate(extras, axis=0)))
    left = lax.broadcasted_iota(jnp.int32, (32, 128), 1) < 64
    rows = lax.broadcasted_iota(jnp.int32, (128, E), 0)
    row = lax.broadcasted_iota(jnp.int32, (8, E), 0)
    face_sums, factors = [], []
    for b in range(blocks):
        pools = []
        for turned in stacks:
            low, high = turned[0:32], turned[32:64]
            if b == 0:
                pools.append(jnp.where(left, low, pltpu.roll(high, 64, 1)))
            else:
                pools.append(jnp.where(left, pltpu.roll(low, 64, 1), high))
        pool = jnp.concatenate(pools, axis=0)
        tall = pool.shape[0]
        pool = jnp.concatenate(halves(pool), axis=0).astype(BF16)
        links = parts[b][MISC, 8:11].astype(jnp.int32)
        match = [
            jnp.where(rows == far_index(links[f : f + 1]), 1.0, 0.0).astype(BF16) for f in range(3)
        ]
        got = dot(pool, jnp.concatenate(match, axis=1))
        got = got[0:tall] + got[tall:]
        sums, scales = [[], [], []], [[], [], []]
        for f in range(3):
            piece = lambda r: got[r : r + 8, 128 * f : 128 * f + 128]
            far = [piece(8 * c) for c in range(3)]
            if section == 3:
                normal = tuple(x[7:8] for x in far)
                for i in range(3):
                    normal_ref[b, f, i : i + 1, :] = normal[i]
            else:
                normal = tuple(normal_ref[b, f, i : i + 1, :] for i in range(3))
            motion = [motion_ref[b, i, 8 * f : 8 * f + 8, :] for i in range(3)]
            theirs = jump_back(normal, far, *motion)
            for c in range(3):
                sums[c].append(-theirs[c])
            if section == 3 and b == 0:
                u0, v0, u1, v1 = [past_ref[i, 8 * f : 8 * f + 8, :] for i in range(4)]
                nx, ny, size = normal
                mean = 0.5 * (nx * u0 + ny * v0)
                rate = 0.5 * (nx * u1 + ny * v1) - 0.5 * PENALTY * size
                factors.append((mean, mean * u1 + u0 * rate, mean * v1 + v0 * rate))
            if section == 2:
                singles = (piece(24)[7:8], piece(56)[7:8], far[0][7:8], far[1][7:8], far[2][7:8])
                singles += (piece(32)[7:8], piece(40)[7:8])
                third = jnp.zeros((8, E), F32)
                for k in range(7):
                    third = jnp.where(row == k, singles[k], third)
                factors.append((piece(24), piece(56), third))
        face_sums += [jnp.concatenate(sums[c], axis=0) for c in range(3)]
    spread = spread_faces(spread3_ref[...], jnp.concatenate(face_sums, axis=1))
    slots = []
    partial = jnp.zeros((8, E), F32)
    for b in range(blocks):
        lam = []
        for c in range(3):
            where = 384 * b + 128 * c
            lam.append(base_ref[b, c] + spread[0:32, where : where + 128])
        if section > 0:
            for c in range(3):
                lam_refs[b][c] = lam[c]
            flipped = [
                ahead_ref[b, c]
                + later * spread[32:56, 384 * b + 128 * c : 384 * b + 128 * c + 128]
                for c in range(3)
            ]
            split = [[flipped[c][8 * f : 8 * f + 8] for f in range(3)] for c in range(3)]
            none = jnp.zeros((1, E), F32)
            lasts = [(none,) * 3] * 3
            if section == 3 and b == 0:
                lasts = [tuple(factors[f][2][k : k + 1] for k in (2, 3, 4)) for f in range(3)]
            trace = traces(split, lasts)
            if section == 3 and b == 0:
                last = row == 7
                third = lambda f, k: factors[f][2][k : k + 1]
                one = [jnp.where(last, third(f, 0), factors[f][0]) for f in range(3)]
                two = [jnp.where(last, third(f, 1), factors[f][1]) for f in range(3)]
                five = [jnp.where(last, third(f, 5), 0.0) for f in range(3)]
                six = [jnp.where(last, third(f, 6), 0.0) for f in range(3)]
                line = lambda parts: jnp.concatenate(parts, axis=1)
                trace = jnp.concatenate([trace, line(one)], axis=0)
                extra = [line(five), line(six), jnp.zeros((8, 3 * E), F32), line(two)]
                slots.append(
                    slot_rows(sends_refs[0][...], trace, 0)
                    + slot_rows(sends_refs[0][...], jnp.concatenate(extra, axis=0), 1)
                )
            else:
                slots.append(slot_rows(sends_refs[b][...], trace, b))
            if section == 2:
                for f in range(3):
                    for c in range(3):
                        partial = partial + split[c][f] * factors[3 * b + f][c]
        else:
            for c in range(3):
                lam_refs[b][c] = lam[c][0:28]
    if section > 0:
        send(x_ref, near_by, slots)
    else:
        group = lax.shift_right_logical(lax.axis_index("dom"), 5)
        total = jnp.zeros((8, 128), F32)
        for g in range(STRIDE):
            dx = jnp.bitwise_and(g // 4 - lax.shift_right_logical(group, 2), 3)
            dy = jnp.bitwise_and(g % 4 - jnp.bitwise_and(group, 3), 3)
            device = 4 * dx + dy + jnp.where((dy == 1) | (dy == 2), ROW, 0)
            total = total + y_ref[pl.ds(pl.multiple_of(device * 8, 8), 8), :]
        first = (lax.broadcasted_iota(jnp.int32, (8, 128), 0) == 0) & (lane == 127)
        drag_ref[0] = jnp.sum(jnp.where(first, total, 0.0))
    return partial


def round3_kernel(*refs):
    tables, parts, (state_ref, y_ref) = refs[0:6], refs[6:8], refs[8:10]
    sends, (lam, halo_lam, x_ref, normal_ref, sum_ref) = refs[10:12], refs[12:17]
    base, ahead, motion, past = refs[17:]
    near_kernel(
        3, 2, *tables, *parts, *parts, state_ref, base, ahead, motion, past, sum_ref
    )
    far_kernel(
        3, 2, y_ref, tables[4], base, motion, *parts, ahead, *sends, past,
        lam, halo_lam, x_ref, normal_ref,
    )


def round2_kernel(*refs):
    tables, lams, parts, (old_ref, state_ref, y_ref) = refs[0:6], refs[6:8], refs[8:10], refs[10:13]
    normal_ref, sends, (x_ref, base_ref, ahead_ref, motion_ref, sum_ref) = (
        refs[13], refs[14:16], refs[16:21],
    )
    base, ahead, motion, lam, halo_lam, sums = refs[21:]
    near_kernel(2, 2, *tables, *lams, *parts, old_ref, base, ahead, motion, sums)
    partial = far_kernel(
        2, 2, y_ref, tables[4], base, motion, *parts, normal_ref, ahead, *sends,
        lam, halo_lam, x_ref,
    )
    near_kernel(
        1, 2, *tables, lam, halo_lam, *parts, sums, base_ref, ahead_ref, motion_ref, sum_ref
    )
    flow = state_ref[0, 1] * base_ref[0, 1, 0:28, :] + state_ref[0, 2] * base_ref[0, 2, 0:28, :]
    total = jnp.sum(sum_ref[4, 24:32, :] - HALF * partial)
    total = total + jnp.sum(flow * (HALF / state_ref[0, 0]))
    put_value(x_ref, -total)


def put_value(x_ref, value):
    lane = lax.broadcasted_iota(jnp.int32, (8, 128), 1)
    for e in range(GROUP):
        part = x_ref[8 * e : 8 * e + 8, :]
        x_ref[8 * e : 8 * e + 8, :] = jnp.where(lane == 127, value, part)


def fold_kernel(y_ref, out_ref):
    total = y_ref[0:8, :]
    for e in range(1, GROUP):
        total = total + y_ref[8 * e : 8 * e + 8, :]
    out_ref[...] = jnp.broadcast_to(total[:, 127:128], (8, 128))


def insert_kernel(x_ref, value_ref, out_ref):
    lane = lax.broadcasted_iota(jnp.int32, (8, 128), 1)
    for e in range(GROUP):
        part = x_ref[8 * e : 8 * e + 8, :]
        out_ref[8 * e : 8 * e + 8, :] = jnp.where(lane == 127, value_ref[...], part)


def call(kernel, outs, args, values=0, scratch=(), smem=()):
    vmem, scalar = pl.BlockSpec(memory_space=pltpu.VMEM), pl.BlockSpec(memory_space=pltpu.SMEM)
    return pl.pallas_call(
        kernel,
        in_specs=[scalar if i in smem else vmem for i in range(len(args))],
        out_specs=[vmem] * (len(outs) - values) + [scalar] * values,
        out_shape=[jax.ShapeDtypeStruct(shape, dtype) for shape, dtype in outs],
        scratch_shapes=[pltpu.VMEM(shape, dtype) for shape, dtype in scratch],
        compiler_params=pltpu.CompilerParams(vmem_limit_bytes=32 * 1024 * 1024),
    )(*args)


def local(
    saved_states,
    adjoint_final,
    bathymetry,
    wind_speed,
    wind_angle,
    drag_rate,
    metrics,
    face_link,
    face_tag,
    send_faces,
):
    devices = lax.axis_size("dom")
    groups = [list(range(g, g + GROUP)) for g in range(0, devices, GROUP)]
    back3, flip3, grad3, take2, spread3 = constants()
    tables = [back3, flip3, grad3, take2, spread3]

    mixed, x_out = ((3, 32, E), F32), ((GROUP * 8, 128), F32)
    sends_out, sums_out = ((128, 384), BF16), ((5, 32, E), F32)
    pairs = [(i, i) for i in range(ROW)] + [(i, i) for i in range(devices - ROW, devices)]
    for row in range(1, devices // ROW - 1, 2):
        for i in range(row * ROW, row * ROW + ROW):
            pairs += [(i, i + ROW), (i + ROW, i)]
    pack_args = (saved_states, adjoint_final, bathymetry)
    pack_args += (metrics, face_tag, face_link, send_faces)
    mine = call(pack_kernel, [((14, 32, E), F32)], pack_args)[0]
    halo = lax.ppermute(mine, "dom", pairs)
    both = [mine, halo]

    my_sends, boxes, rate = call(
        own_first_kernel,
        [sends_out, ((64, 128), F32), ((8, E), F32)],
        [mine, flip3, drag_rate] + tables,
        smem=(2,),
    )
    tables.append(rate)
    x, halo_sends = call(halo_first_kernel, [x_out, sends_out], (halo, flip3, boxes))
    def exchange(x):
        return lax.all_to_all(x, "dom", 0, 0, tiled=True, axis_index_groups=groups)

    bases, faces = ((2, 3, 32, E), F32), ((2, 3, 24, E), F32)
    far_outs, near_outs = [mixed, mixed, x_out], [bases, faces, faces, sums_out]
    sends = [my_sends, halo_sends]

    y = exchange(x)
    lam3, _, x, normals, sums = got = call(
        round3_kernel,
        far_outs + [((2, 3, 8, E), F32), sums_out],
        tables + both + [saved_states, y] + sends,
        scratch=[bases, faces, faces, ((4, 24, E), F32)],
    )
    y = exchange(x)
    x, base, ahead, motion, sums = call(
        round2_kernel,
        [x_out] + near_outs,
        tables + list(got[0:2]) + both + [sums, saved_states, y, normals] + sends,
        scratch=[bases, faces, faces, mixed, mixed, sums_out],
    )
    y = exchange(x)
    within = call(fold_kernel, [((8, 128), F32)], (y,))[0]
    within = lax.ppermute(within, "dom", spread_pairs(devices))
    lam1, _, x = call(
        lambda *refs: (far_kernel(1, 2, *refs), None)[1],
        far_outs,
        [y, spread3, base, motion] + both + [normals, ahead] + sends,
    )
    args = tables + [lam1, mine, sums, saved_states, lam3, wind_speed, wind_angle]
    base, motion, depth_gradient, speed_gradient, angle_gradient = call(
        lambda *refs: near_kernel(0, 1, *refs),
        [((1, 3, 32, E), F32), ((1, 3, 24, E), F32)] + [((28, E), F32)] * 3,
        args,
    )
    x, base = lax.optimization_barrier((x, base))
    y = exchange(call(insert_kernel, [x_out], (x, within))[0])
    initial, drag_gradient = call(
        lambda *refs: (far_kernel(0, 1, *refs), None)[1],
        [((3, 28, E), F32), ((1,), F32)],
        [y, spread3, base, motion, mine, normals],
        values=1,
    )
    return (initial, depth_gradient, speed_gradient, angle_gradient, drag_gradient)


def solution(mesh):
    return jax.shard_map(
        local,
        mesh=mesh,
        in_specs=(
            P(None, None, None, "dom"),
            P(None, None, "dom"),
            P(None, "dom"),
            P(None, "dom"),
            P(None, "dom"),
            P(),
            P(None, "dom"),
            P(None, "dom"),
            P(None, "dom"),
            P(None, "dom"),
        ),
        out_specs=(P(None, None, "dom"), P(None, "dom"), P(None, "dom"), P(None, "dom"), P()),
        check_vma=False,
    )
```

```python
import math

import jax
import jax.numpy as jnp
import ml_dtypes
import numpy as np
from jax import lax
from jax.experimental import pallas as pl
from jax.experimental.pallas import tpu as pltpu
from jax.sharding import PartitionSpec as P

GRAVITY = 1.0
PENALTY = 3.0
WIND_COEF = 5.0
TIME_STEP = 0.01
HALF = 0.5 * TIME_STEP
SIXTH = TIME_STEP / 6.0

GROUP = 32
STRIDE = 16
ROW = 16
REACH = 4
DIRS = 8
SLOTS = 16
E = 128
DEPTH, MISC = 12, 24
PACKED = MISC + 28 * 13 + 4
F32 = jnp.float32
BF16 = jnp.bfloat16


def solve_dense(matrix, right):
    system = np.array(matrix) + 0.0
    result = np.array(right) + 0.0
    extent = system.shape[0]
    for column in range(extent):
        pivot_index = column + int(np.argmax(np.abs(system[column:, column])))
        system[[column, pivot_index]] = system[[pivot_index, column]]
        result[[column, pivot_index]] = result[[pivot_index, column]]
        for target in range(column + 1, extent):
            factor = system[target, column] / system[column, column]
            system[target] = system[target] - factor * system[column]
            result[target] = result[target] - factor * result[column]
    solution = np.zeros(result.shape)
    for column in range(extent - 1, -1, -1):
        solution[column] = (
            result[column] - system[column, column + 1 :] @ solution[column + 1 :]
        ) / system[column, column]
    return solution


def element_tables():
    degree = 6
    nodes = [
        (column, row_index)
        for row_index in range(degree + 1)
        for column in range(degree + 1 - row_index)
    ]
    node_total = len(nodes)
    coord_x = np.array([node[0] / degree for node in nodes])
    coord_y = np.array([node[1] / degree for node in nodes])
    vander = np.zeros((node_total, node_total))
    vander_r = np.zeros((node_total, node_total))
    vander_s = np.zeros((node_total, node_total))
    grams = np.zeros((node_total, node_total))
    for column_index, power in enumerate(nodes):
        first, second = power
        vander[:, column_index] = coord_x**first * coord_y**second
        if first > 0:
            vander_r[:, column_index] = 0.5 * first * coord_x ** (first - 1) * coord_y**second
        if second > 0:
            vander_s[:, column_index] = 0.5 * second * coord_x**first * coord_y ** (second - 1)
        for other_index, other_power in enumerate(nodes):
            sum_x = first + other_power[0]
            sum_y = second + other_power[1]
            grams[column_index, other_index] = (
                4.0
                * math.factorial(sum_x)
                * math.factorial(sum_y)
                / math.factorial(sum_x + sum_y + 2)
            )
    deriv_r = solve_dense(vander.T, vander_r.T).T
    deriv_s = solve_dense(vander.T, vander_s.T).T
    mass_inverse = vander @ solve_dense(grams, vander.T)
    points = np.arange(degree + 1) / degree
    line_vander = np.stack([points**power for power in range(degree + 1)], axis=1)
    line_grams = np.array(
        [
            [2.0 / (first + second + 1) for second in range(degree + 1)]
            for first in range(degree + 1)
        ]
    )
    line_inverse = solve_dense(line_vander, np.eye(degree + 1))
    line_mass = line_inverse.T @ line_grams @ line_inverse
    lookup = {node: number for number, node in enumerate(nodes)}
    face_nodes = [
        [lookup[step, 0] for step in range(degree + 1)],
        [lookup[degree - step, step] for step in range(degree + 1)],
        [lookup[0, degree - step] for step in range(degree + 1)],
    ]
    embed = np.zeros((node_total, 3 * (degree + 1)))
    extract = np.zeros((3 * (degree + 1), node_total))
    for face_index in range(3):
        for step in range(degree + 1):
            extract[face_index * (degree + 1) + step, face_nodes[face_index][step]] = 1.0
            for other_step in range(degree + 1):
                embed[
                    face_nodes[face_index][other_step], face_index * (degree + 1) + step
                ] += line_mass[other_step, step]
    lifting = mass_inverse @ embed
    return deriv_r, deriv_s, lifting, extract


def offset_of(direction):
    return direction + 1 if direction < REACH else REACH - direction - 1


def neighbours():
    me = jnp.bitwise_and(lax.axis_index("dom"), GROUP - 1)
    found = []
    for own in (me + ROW, jnp.where(me < ROW, me, me + 2 * ROW)):
        for j in range(DIRS):
            place = own + offset_of(j)
            inner = (place >= ROW) & (place < ROW + GROUP)
            exists = (place >= 0) & (place < 4 * ROW)
            device = jnp.where(inner, place - ROW, jnp.where(place < ROW, place, place - 2 * ROW))
            found.append((jnp.where(exists, device, 0), jnp.where(inner, 0, 1), exists))
    return found


def spread_place(dx, dy):
    half, odd = dx // 2, dx % 2
    if dy == 0:
        return 6 + half + ROW * odd
    if dy == 2:
        return 4 + half + ROW * (1 - odd)
    return dx + (ROW if dy == 1 else 0)


def spread_pairs(devices):
    pairs = []
    for group in range(devices // GROUP):
        for dx in range(4):
            for dy in range(4):
                other = (group // 4 + dx) % 4 * 4 + (group % 4 + dy) % 4
                place = spread_place(dx, dy)
                source = place if dy == 0 else (place + ROW) % GROUP
                pairs.append((other * GROUP + source, group * GROUP + place))
    return pairs


def parts3(matrix, width):
    padded = np.zeros((matrix.shape[0], width))
    padded[:, : matrix.shape[1]] = matrix
    hi = padded.astype(np.float32).astype(ml_dtypes.bfloat16)
    lo = (padded - hi.astype(np.float64)).astype(ml_dtypes.bfloat16)
    return np.concatenate([hi, lo, hi], axis=1)


def constants():
    deriv_r, deriv_s, lifting, extract = element_tables()

    def pad_rows(matrix):
        return np.concatenate([matrix, np.zeros((4, matrix.shape[1]))])

    lift = np.zeros((24, 28))
    flip = np.zeros((24, 28))
    take = np.zeros((24, 28))
    give = np.zeros((24, 28))
    for face in range(3):
        for k in range(7):
            lift[8 * face + k] = lifting[:, 7 * face + k]
            flip[8 * face + k] = lifting[:, 7 * face + 6 - k]
            take[8 * face + k] = extract[7 * face + k]
            give[8 * face + k] = extract[7 * face + k]
        take[8 * face + 7] = extract[7 * face + 6]
    back = np.concatenate([pad_rows(deriv_r.T), pad_rows(deriv_s.T), lift, flip])
    back3 = parts3(back, 32)
    flip3 = parts3(flip, 32)
    grad3 = parts3(np.concatenate([pad_rows(deriv_r), pad_rows(deriv_s)]), 32)
    take2 = np.zeros((24, 64))
    take2[:, 0:28] = take
    take2[:, 32:60] = take
    spread = np.concatenate([pad_rows(give.T), flip @ give.T])
    spread3 = parts3(spread, 24)
    spread3 = np.concatenate([spread3, np.zeros((56, 8), ml_dtypes.bfloat16)], axis=1)
    as_bf16 = lambda m: jnp.asarray(np.asarray(m).astype(ml_dtypes.bfloat16))
    return as_bf16(back3), as_bf16(flip3), as_bf16(grad3), as_bf16(take2), as_bf16(spread3)


def dot(a, b):
    return jnp.dot(a, b, preferred_element_type=F32)


def dot_nt(a, b):
    return lax.dot_general(a, b, (((1,), (1,)), ((), ())), preferred_element_type=F32)


def halves(x):
    hi = x.astype(BF16).astype(F32)
    return hi, x - hi


def times3(matrix3, x):
    hi = x.astype(BF16)
    lo = (x - hi.astype(F32)).astype(BF16)
    return dot(matrix3, jnp.concatenate([hi, hi, lo], axis=0))


def spread_faces(spread3, faces):
    hi, lo = halves(faces)
    stack = jnp.concatenate([hi, hi, lo, jnp.zeros((8, faces.shape[1]), F32)], axis=0)
    return dot(spread3, stack.astype(BF16))


def geometry(misc):
    rx, ry, sx, sy = misc[0:1], misc[1:2], misc[2:3], misc[3:4]
    normals = []
    for nx, ny in ((-sx, -sy), (rx + sx, ry + sy), (-rx, -ry)):
        normals.append((nx, ny, jnp.sqrt(nx * nx + ny * ny)))
    return (rx, ry, sx, sy), normals


def jump_back(n, t, u, v, gh):
    nx, ny, size = n
    un = nx * u + ny * v
    mixed = u * t[1] + v * t[2]
    pull = 0.5 * PENALTY * size
    return (
        0.5 * (gh * (nx * t[1] + ny * t[2]) - un * mixed) - pull * t[0],
        0.5 * (nx * (t[0] + mixed) + un * t[1]) - pull * t[1],
        0.5 * (ny * (t[0] + mixed) + un * t[2]) - pull * t[2],
    )


def traces(flipped, normals):
    last = lax.broadcasted_iota(jnp.int32, (8, E), 0) == 7
    rows = []
    for c in range(3):
        rows.append(
            jnp.concatenate(
                [jnp.where(last, normals[f][c], flipped[c][f]) for f in range(3)], axis=1
            )
        )
    return jnp.concatenate(rows, axis=0)


def far_index(link):
    v = link - 3 * E
    j = lax.shift_right_arithmetic(v, 4)
    c = jnp.bitwise_and(v, 15)
    row = lax.shift_right_arithmetic(c, 3) * 64 + j * 8 + jnp.bitwise_and(c, 7)
    return jnp.where(v >= 0, row, -1)


def slot_rows(sends, v, block):
    first = 64 * block
    n = v.shape[1]
    hi, lo = halves(v)
    rows = [jnp.zeros((first, n), F32)] if block else []
    rest = [jnp.zeros((32 - v.shape[0], n), F32)] if v.shape[0] < 32 else []
    rows += [hi] + rest + [lo] + rest + [jnp.zeros((64 - first, n), F32)] * (1 - block)
    out = dot_nt(sends, jnp.concatenate(rows, axis=0).astype(BF16))
    lane = lax.broadcasted_iota(jnp.int32, (128, 128), 1)
    out = jnp.where((lane >= first) & (lane < first + 32), out + pltpu.roll(out, 96, 1), 0.0)
    return out[0:64] + pltpu.roll(out[64:128], 32, 1)


def send(x_ref, near_by, boxes):
    x_ref[...] = jnp.zeros(x_ref.shape, F32)
    for b in range(2):
        for j in range(DIRS):
            device, _, exists = near_by[DIRS * b + j]
            rows = pl.ds(pl.multiple_of(device * 8, 8), 8)
            box = jnp.where(exists, boxes[b][8 * j : 8 * j + 8], 0.0)
            x_ref[rows, :] = x_ref[rows, :] + box


def send_matrix(misc):
    faces = misc[16:24]
    lane = lax.broadcasted_iota(jnp.int32, (8, 128), 1)
    low = jnp.where(lane < 8, faces, 0.0)
    high = jnp.where((lane >= 8) & (lane < 16), faces, 0.0)
    both = low + pltpu.roll(high, 56, 1)
    row = lax.broadcasted_iota(jnp.int32, (8, 128), 0)
    lined = jnp.zeros((8, 128), F32)
    for j in range(DIRS):
        moved = both if j == 0 else pltpu.roll(both, 8 * j, 1)
        lined = lined + jnp.where(row == j, moved, 0.0)
    line = jnp.sum(lined, axis=0, keepdims=True)
    column = jnp.transpose(jnp.broadcast_to(line, (128, 128)))
    face = lax.broadcasted_iota(jnp.int32, (128, 128), 1).astype(F32)
    pieces = [jnp.where(column == face + float(128 * f), 1.0, 0.0) for f in range(3)]
    return jnp.concatenate(pieces, axis=1).astype(BF16)


def pack_kernel(q_ref, lam_ref, depth_ref, metric_ref, tag_ref, link_ref, face_ref, out_ref):
    out_ref[0:MISC, :] = jnp.zeros((MISC, E), F32)
    out_ref[0:4, :] = metric_ref[...]
    out_ref[4:7, :] = tag_ref[...].astype(F32)
    out_ref[8:11, :] = link_ref[...].astype(F32)
    out_ref[16:24, 0:16] = face_ref[...].astype(F32)
    for c in range(3):
        out_ref[MISC + 28 * c : MISC + 28 * c + 28, :] = lam_ref[c]
    for s in range(3):
        for c in range(3):
            first = MISC + 28 * (3 * (3 - s) + c)
            out_ref[first : first + 28, :] = q_ref[s + 1, c]
    out_ref[MISC + 28 * DEPTH : MISC + 28 * DEPTH + 28, :] = depth_ref[...]
    out_ref[PACKED - 4 : PACKED, :] = jnp.zeros((4, E), F32)


def field(part_ref, i, fill):
    first = MISC + 28 * i
    row = lax.broadcasted_iota(jnp.int32, (32, E), 0)
    return jnp.where(row < 28, part_ref[first : first + 32, :], fill)


def first_boxes(part_ref, flip3, block):
    misc = part_ref[0:MISC, :]
    weights = jnp.concatenate([HALF * field(part_ref, c, 0.0) for c in range(3)], axis=1)
    flipped = times3(flip3[...], weights)
    split = [
        [flipped[8 * f : 8 * f + 8, 128 * c : 128 * c + 128] for f in range(3)] for c in range(3)
    ]
    sends = send_matrix(misc)
    return sends, slot_rows(sends, traces(split, geometry(misc)[1]), block)


def own_first_kernel(part_ref, flip3, drag_ref, *refs):
    sends_ref, boxes_ref, rate_ref = refs[-3:]
    rate_ref[...] = jnp.full((8, E), drag_ref[0], F32)
    sends_ref[...], boxes_ref[...] = first_boxes(part_ref, flip3, 0)


def halo_first_kernel(part_ref, flip3, boxes_ref, x_ref, sends_ref):
    sends_ref[...], boxes = first_boxes(part_ref, flip3, 1)
    send(x_ref, neighbours(), [boxes_ref[...], boxes])


def near_kernel(section, blocks, *refs):
    refs = list(refs)
    back3, flip3, grad3, take2, spread3 = [refs.pop(0)[...] for _ in range(5)]
    rate_ref = refs.pop(0)
    lams = [refs.pop(0) for _ in range(blocks)]
    parts = [refs.pop(0) for _ in range(blocks)]
    old_ref = refs.pop(0) if section < 3 else None
    if section == 3:
        state_ref = refs.pop(0)
    if section == 0:
        state_ref, lam3_ref = refs.pop(0), refs.pop(0)
        speed_ref, angle_ref = refs.pop(0), refs.pop(0)
    base_ref = refs.pop(0)
    if section > 0:
        ahead_ref = refs.pop(0)
    motion_ref = refs.pop(0)
    if section == 3:
        past_ref = refs.pop(0)
    if section > 0:
        sum_ref = refs.pop(0)
    else:
        depth_out, speed_out, angle_out = refs.pop(0), refs.pop(0), refs.pop(0)
    scale = SIXTH if section == 2 else HALF
    later = SIXTH if section == 3 else HALF
    drag_rate = rate_ref[...][0:1]
    pad = jnp.ones((4, E), F32)

    if section == 3:
        lam = [[field(lams[b], c, 0.0) for c in range(3)] for b in range(blocks)]
    else:
        lam = [[lams[b][c] for c in range(3)] for b in range(blocks)]
    w = [[scale * x for x in lam[b]] for b in range(blocks)]
    if section == 0:
        q = [[jnp.concatenate([state_ref[0, c], pad], axis=0) for c in range(3)]]
    else:
        q = [[field(parts[b], 3 * (4 - section) + c, 1.0) for c in range(3)] for b in range(blocks)]
    z = [field(parts[b], DEPTH, 1.0) for b in range(blocks)]
    pulled = times3(back3, jnp.concatenate([x for b in range(blocks) for x in w[b]], axis=1))
    slopes = times3(grad3, jnp.concatenate(z, axis=1))
    fields = jnp.concatenate([x for b in range(blocks) for x in q[b] + [z[b]]], axis=1)
    hi, lo = halves(fields)
    at_faces = dot(take2, jnp.concatenate([hi, lo], axis=0).astype(BF16))

    if section == 3:
        fields = [jnp.concatenate([state_ref[0, c], pad], axis=0) for c in range(3)]
        fields += [field(parts[0], 9 + c, 1.0) for c in range(3)]
        hi, lo = halves(jnp.concatenate(fields, axis=1))
        past = dot(take2, jnp.concatenate([hi, lo], axis=0).astype(BF16))
        for i in range(2):
            finv = 1.0 / past[:, 384 * i : 384 * i + 128]
            past_ref[2 * i] = past[:, 384 * i + 128 : 384 * i + 256] * finv
            past_ref[2 * i + 1] = past[:, 384 * i + 256 : 384 * i + 384] * finv

    face_sums, volumes, opens = [], [], []
    for b in range(blocks):
        misc = parts[b][0:MISC, :]
        (rx, ry, sx, sy), normals = geometry(misc)
        part = lambda r0, r1, c: pulled[r0:r1, 384 * b + 128 * c : 384 * b + 128 * c + 128]
        h = q[b][0]
        inv = 1.0 / h
        u, v = q[b][1] * inv, q[b][2] * inv
        gh = GRAVITY * h
        along = [part(0, 32, c) for c in range(3)]
        across = [part(32, 64, c) for c in range(3)]
        fx = [-(rx * along[c] + sx * across[c]) for c in range(3)]
        fy = [-(ry * along[c] + sy * across[c]) for c in range(3)]
        cross = fx[2] + fy[1]
        slope_r = slopes[0:32, 128 * b : 128 * b + 128]
        slope_s = slopes[32:64, 128 * b : 128 * b + 128]
        slope_x = rx * slope_r + sx * slope_s
        slope_y = ry * slope_r + sy * slope_s
        flow = u * w[b][1] + v * w[b][2]
        drag_inv = drag_rate * inv
        volumes.append(
            (
                gh * (fx[1] + fy[2])
                - u * (u * fx[1] + v * cross)
                - v * v * fy[2]
                + GRAVITY * (slope_x * w[b][1] + slope_y * w[b][2])
                + drag_inv * flow,
                fx[0] + 2.0 * u * fx[1] + v * cross - drag_inv * w[b][1],
                fy[0] + u * cross + 2.0 * v * fy[2] - drag_inv * w[b][2],
            )
        )
        own = [[part(64 + 8 * f, 72 + 8 * f, c) for f in range(3)] for c in range(3)]
        flipped = [[part(88 + 8 * f, 96 + 8 * f, c) for f in range(3)] for c in range(3)]
        hi, lo = halves(traces(flipped, normals))
        pool = jnp.concatenate([hi, lo], axis=0).astype(BF16)
        links = misc[8:11].astype(jnp.int32)
        rows = lax.broadcasted_iota(jnp.int32, (3 * E, E), 0)
        opened = []
        sums = [[], [], []]
        for f in range(3):
            match = jnp.where(rows == links[f : f + 1], 1.0, 0.0).astype(BF16)
            got = dot(pool, match)
            got = got[0:24] + got[24:48]
            value = lambda i: at_faces[
                8 * f : 8 * f + 8, 512 * b + 128 * i : 512 * b + 128 * i + 128
            ]
            fh, fm, fn, fz = value(0), value(1), value(2), value(3)
            finv = 1.0 / fh
            fu, fv, fgh = fm * finv, fn * finv, GRAVITY * fh
            motion_ref[b, 0, 8 * f : 8 * f + 8, :] = fu
            motion_ref[b, 1, 8 * f : 8 * f + 8, :] = fv
            motion_ref[b, 2, 8 * f : 8 * f + 8, :] = fgh
            tag = misc[4 + f : 5 + f]
            linked, wall, free = tag == 0.0, tag == 1.0, tag == 2.0
            nx, ny, size = normals[f]
            t = [own[c][f] for c in range(3)]
            mine = jump_back(normals[f], t, fu, fv, fgh)
            inv_size = 1.0 / size
            ux, uy = nx * inv_size, ny * inv_size
            twice = 2.0 * (ux * t[1] + uy * t[2])
            mirrored = (t[0], t[1] - twice * ux, t[2] - twice * uy)
            near = (got[0:8], got[8:16], got[16:24])
            other_n = tuple(
                jnp.where(linked, near[c][7:8], jnp.where(wall, m, 0.0))
                for c, m in enumerate((-nx, -ny, size))
            )
            other_t = [
                jnp.where(linked, near[c], jnp.where(wall, mirrored[c], 0.0)) for c in range(3)
            ]
            theirs = jump_back(other_n, other_t, fu, fv, fgh)
            zinv = 1.0 / fz
            out = jump_back(normals[f], t, fm * zinv, fn * zinv, GRAVITY * fz)
            opened.append(jnp.where(free, -out[0], 0.0))
            sums[0].append(mine[0] - theirs[0])
            sums[1].append(mine[1] - theirs[1] - jnp.where(free, out[1], 0.0))
            sums[2].append(mine[2] - theirs[2] - jnp.where(free, out[2], 0.0))
        face_sums.append([jnp.concatenate(sums[c], axis=0) for c in range(3)])
        if b == 0:
            opens = jnp.concatenate(opened, axis=0)
            height, moved = h, flow
    to_nodes = [x for b in range(blocks) for x in face_sums[b]]
    if section == 0:
        old = [old_ref[i] for i in range(5)]
        opens = opens + old[4][0:24]
        to_nodes.append(opens)
    nodes = spread_faces(spread3, jnp.concatenate(to_nodes, axis=1))
    for b in range(blocks):
        bases = []
        for c in range(3):
            first = lam[b][c]
            if section == 2:
                first = first * (1.0 / 3.0)
            if section == 0:
                first = first + (2.0 / 3.0) * lam3_ref[c]
            where = 384 * b + 128 * c
            bases.append(first + volumes[b][c] + nodes[0:32, where : where + 128])
            base_ref[b, c] = bases[c]
        if section > 0:
            ahead = times3(flip3, later * jnp.concatenate(bases, axis=1))
            for c in range(3):
                ahead_ref[b, c] = ahead[:, 128 * c : 128 * c + 128]
    w1, w2 = w[0][1], w[0][2]
    g1, g2 = height * w1, height * w2
    if section == 3:
        fold = moved[0:8] + moved[8:16] + moved[16:24] + moved[24:32]
        news = [w1, w2, g1, g2]
    else:
        if section > 0:
            old = [old_ref[i] for i in range(5)]
            opens = opens + old[4][0:24]
            fold = old[4][24:32] + (moved[0:8] + moved[8:16] + moved[16:24] + moved[24:32])
        news = [x + y for x, y in zip(old[0:4], (w1, w2, g1, g2))]
    if section > 0:
        for i in range(4):
            sum_ref[i] = news[i]
        sum_ref[4, 0:24, :] = opens
        sum_ref[4, 24:32, :] = fold
    else:
        rx, ry, sx, sy = geometry(parts[0][0:4, :])[0]
        w1, w2, g1, g2 = news
        pair = GRAVITY * jnp.concatenate([rx * g1 + ry * g2, sx * g1 + sy * g2], axis=1)
        pulled = times3(back3, pair)
        depth = pulled[0:32, 0:128] + pulled[32:64, 128:256] + nodes[0:32, 384:512]
        depth_out[...] = depth[0:28]
        speed, angle = speed_ref[...], angle_ref[...]
        cosine, sine = jnp.cos(angle), jnp.sin(angle)
        w1, w2 = w1[0:28], w2[0:28]
        speed_out[...] = (2.0 * WIND_COEF) * speed * (cosine * w1 + sine * w2)
        angle_out[...] = WIND_COEF * speed * speed * (cosine * w2 - sine * w1)


def far_kernel(section, blocks, *refs):
    refs = list(refs)
    y_ref, spread3_ref, base_ref, motion_ref = [refs.pop(0) for _ in range(4)]
    parts = [refs.pop(0) for _ in range(blocks)]
    if section < 3:
        normal_ref = refs.pop(0)
    if section > 0:
        ahead_ref = refs.pop(0)
        sends_refs = [refs.pop(0), refs.pop(0)]
    if section == 3:
        past_ref = refs.pop(0)
    lam_refs = [refs.pop(0) for _ in range(blocks)]
    if section > 0:
        x_ref = refs.pop(0)
    if section == 3:
        normal_ref = refs.pop(0)
    if section == 0:
        drag_ref = refs.pop(0)
    later = SIXTH if section == 3 else HALF

    lane = lax.broadcasted_iota(jnp.int32, (8, 128), 1)
    place_in = jnp.bitwise_and(lane, 31)
    spare = (place_in >= 24) | (place_in == 7) | (place_in == 15) | (place_in == 23)
    near_by = neighbours()
    boxes, extras = [], []
    for b in range(2):
        for j in range(DIRS):
            if b < blocks:
                device, second, exists = near_by[DIRS * b + j]
                raw = y_ref[pl.ds(pl.multiple_of(device * 8, 8), 8), :]
                turned = pltpu.roll(raw, 64, 1)
                if section == 2:
                    box = jnp.where(second == 1, jnp.where(spare, 0.0, turned), raw)
                    extras.append(jnp.where(exists & (second == 0), turned, 0.0))
                else:
                    box = jnp.where(second == 1, turned, raw)
                boxes.append(jnp.where(exists, box, 0.0))
            else:
                boxes.append(jnp.zeros((8, 128), F32))
    stacks = [jnp.transpose(jnp.concatenate(boxes, axis=0))]
    if section == 2:
        stacks.append(jnp.transpose(jnp.concatenate(extras, axis=0)))
    left = lax.broadcasted_iota(jnp.int32, (32, 128), 1) < 64
    rows = lax.broadcasted_iota(jnp.int32, (128, E), 0)
    row = lax.broadcasted_iota(jnp.int32, (8, E), 0)
    face_sums, factors = [], []
    for b in range(blocks):
        pools = []
        for turned in stacks:
            low, high = turned[0:32], turned[32:64]
            if b == 0:
                pools.append(jnp.where(left, low, pltpu.roll(high, 64, 1)))
            else:
                pools.append(jnp.where(left, pltpu.roll(low, 64, 1), high))
        pool = jnp.concatenate(pools, axis=0)
        tall = pool.shape[0]
        pool = jnp.concatenate(halves(pool), axis=0).astype(BF16)
        links = parts[b][8:11, :].astype(jnp.int32)
        match = [
            jnp.where(rows == far_index(links[f : f + 1]), 1.0, 0.0).astype(BF16) for f in range(3)
        ]
        got = dot(pool, jnp.concatenate(match, axis=1))
        got = got[0:tall] + got[tall:]
        sums, scales = [[], [], []], [[], [], []]
        for f in range(3):
            piece = lambda r: got[r : r + 8, 128 * f : 128 * f + 128]
            far = [piece(8 * c) for c in range(3)]
            if section == 3:
                normal = tuple(x[7:8] for x in far)
                for i in range(3):
                    normal_ref[b, f, i : i + 1, :] = normal[i]
            else:
                normal = tuple(normal_ref[b, f, i : i + 1, :] for i in range(3))
            motion = [motion_ref[b, i, 8 * f : 8 * f + 8, :] for i in range(3)]
            theirs = jump_back(normal, far, *motion)
            for c in range(3):
                sums[c].append(-theirs[c])
            if section == 3 and b == 0:
                u0, v0, u1, v1 = [past_ref[i, 8 * f : 8 * f + 8, :] for i in range(4)]
                nx, ny, size = normal
                mean = 0.5 * (nx * u0 + ny * v0)
                rate = 0.5 * (nx * u1 + ny * v1) - 0.5 * PENALTY * size
                factors.append((mean, mean * u1 + u0 * rate, mean * v1 + v0 * rate))
            if section == 2:
                singles = (piece(24)[7:8], piece(56)[7:8], far[0][7:8], far[1][7:8], far[2][7:8])
                singles += (piece(32)[7:8], piece(40)[7:8])
                third = jnp.zeros((8, E), F32)
                for k in range(7):
                    third = jnp.where(row == k, singles[k], third)
                factors.append((piece(24), piece(56), third))
        face_sums += [jnp.concatenate(sums[c], axis=0) for c in range(3)]
    spread = spread_faces(spread3_ref[...], jnp.concatenate(face_sums, axis=1))
    slots = []
    partial = jnp.zeros((8, E), F32)
    for b in range(blocks):
        lam = []
        for c in range(3):
            where = 384 * b + 128 * c
            lam.append(base_ref[b, c] + spread[0:32, where : where + 128])
        if section > 0:
            for c in range(3):
                lam_refs[b][c] = lam[c]
            flipped = [
                ahead_ref[b, c]
                + later * spread[32:56, 384 * b + 128 * c : 384 * b + 128 * c + 128]
                for c in range(3)
            ]
            split = [[flipped[c][8 * f : 8 * f + 8] for f in range(3)] for c in range(3)]
            none = jnp.zeros((1, E), F32)
            lasts = [(none,) * 3] * 3
            if section == 3 and b == 0:
                lasts = [tuple(factors[f][2][k : k + 1] for k in (2, 3, 4)) for f in range(3)]
            trace = traces(split, lasts)
            if section == 3 and b == 0:
                last = row == 7
                third = lambda f, k: factors[f][2][k : k + 1]
                one = [jnp.where(last, third(f, 0), factors[f][0]) for f in range(3)]
                two = [jnp.where(last, third(f, 1), factors[f][1]) for f in range(3)]
                five = [jnp.where(last, third(f, 5), 0.0) for f in range(3)]
                six = [jnp.where(last, third(f, 6), 0.0) for f in range(3)]
                line = lambda parts: jnp.concatenate(parts, axis=1)
                trace = jnp.concatenate([trace, line(one)], axis=0)
                extra = [line(five), line(six), jnp.zeros((8, 3 * E), F32), line(two)]
                slots.append(
                    slot_rows(sends_refs[0][...], trace, 0)
                    + slot_rows(sends_refs[0][...], jnp.concatenate(extra, axis=0), 1)
                )
            else:
                slots.append(slot_rows(sends_refs[b][...], trace, b))
            if section == 2:
                for f in range(3):
                    for c in range(3):
                        partial = partial + split[c][f] * factors[3 * b + f][c]
        else:
            for c in range(3):
                lam_refs[b][c] = lam[c][0:28]
    if section > 0:
        send(x_ref, near_by, slots)
    else:
        group = lax.shift_right_logical(lax.axis_index("dom"), 5)
        total = jnp.zeros((8, 128), F32)
        for g in range(STRIDE):
            dx = jnp.bitwise_and(g // 4 - lax.shift_right_logical(group, 2), 3)
            dy = jnp.bitwise_and(g % 4 - jnp.bitwise_and(group, 3), 3)
            device = jnp.int32(0)
            for x in range(4):
                for y in range(4):
                    device = jnp.where((dx == x) & (dy == y), spread_place(x, y), device)
            total = total + y_ref[pl.ds(pl.multiple_of(device * 8, 8), 8), :]
        drag_ref[0] = jnp.sum(jnp.where(lane == 127, total, 0.0))
    return partial


def round3_kernel(*refs):
    tables, parts, (state_ref, y_ref) = refs[0:6], refs[6:8], refs[8:10]
    sends, (lam, halo_lam, x_ref, normal_ref, sum_ref) = refs[10:12], refs[12:17]
    base, ahead, motion, past = refs[17:]
    near_kernel(
        3, 2, *tables, *parts, *parts, state_ref, base, ahead, motion, past, sum_ref
    )
    far_kernel(
        3, 2, y_ref, tables[4], base, motion, *parts, ahead, *sends, past,
        lam, halo_lam, x_ref, normal_ref,
    )


def round2_kernel(*refs):
    tables, lams, parts, (old_ref, state_ref, y_ref) = refs[0:6], refs[6:8], refs[8:10], refs[10:13]
    normal_ref, sends, (x_ref, base_ref, ahead_ref, motion_ref, sum_ref) = (
        refs[13], refs[14:16], refs[16:21],
    )
    base, ahead, motion, lam, halo_lam, sums = refs[21:]
    near_kernel(2, 2, *tables, *lams, *parts, old_ref, base, ahead, motion, sums)
    partial = far_kernel(
        2, 2, y_ref, tables[4], base, motion, *parts, normal_ref, ahead, *sends,
        lam, halo_lam, x_ref,
    )
    near_kernel(
        1, 2, *tables, lam, halo_lam, *parts, sums, base_ref, ahead_ref, motion_ref, sum_ref
    )
    flow = state_ref[0, 1] * base_ref[0, 1, 0:28, :] + state_ref[0, 2] * base_ref[0, 2, 0:28, :]
    flow = jnp.concatenate([flow * (HALF / state_ref[0, 0]), jnp.zeros((4, E), F32)], axis=0)
    flow = flow[0:8] + flow[8:16] + flow[16:24] + flow[24:32]
    total = sum_ref[4, 24:32, :] - HALF * partial + flow
    put_value(x_ref, -jnp.sum(total, axis=1, keepdims=True))


def put_value(x_ref, value):
    lane = lax.broadcasted_iota(jnp.int32, (8, 128), 1)
    for e in range(GROUP):
        part = x_ref[8 * e : 8 * e + 8, :]
        x_ref[8 * e : 8 * e + 8, :] = jnp.where(lane == 127, value, part)


def fold_kernel(y_ref, out_ref):
    total = y_ref[0:8, :]
    for e in range(1, GROUP):
        total = total + y_ref[8 * e : 8 * e + 8, :]
    out_ref[...] = jnp.broadcast_to(total[:, 127:128], (8, 128))


def insert_kernel(x_ref, value_ref, out_ref):
    lane = lax.broadcasted_iota(jnp.int32, (8, 128), 1)
    for e in range(GROUP):
        part = x_ref[8 * e : 8 * e + 8, :]
        out_ref[8 * e : 8 * e + 8, :] = jnp.where(lane == 127, value_ref[...], part)


def call(kernel, outs, args, values=0, scratch=(), smem=()):
    vmem, scalar = pl.BlockSpec(memory_space=pltpu.VMEM), pl.BlockSpec(memory_space=pltpu.SMEM)
    return pl.pallas_call(
        kernel,
        in_specs=[scalar if i in smem else vmem for i in range(len(args))],
        out_specs=[vmem] * (len(outs) - values) + [scalar] * values,
        out_shape=[jax.ShapeDtypeStruct(shape, dtype) for shape, dtype in outs],
        scratch_shapes=[pltpu.VMEM(shape, dtype) for shape, dtype in scratch],
        compiler_params=pltpu.CompilerParams(vmem_limit_bytes=32 * 1024 * 1024),
    )(*args)


def local(
    saved_states,
    adjoint_final,
    bathymetry,
    wind_speed,
    wind_angle,
    drag_rate,
    metrics,
    face_link,
    face_tag,
    send_faces,
):
    devices = lax.axis_size("dom")
    groups = [list(range(g, g + GROUP)) for g in range(0, devices, GROUP)]
    back3, flip3, grad3, take2, spread3 = constants()
    tables = [back3, flip3, grad3, take2, spread3]

    mixed, x_out = ((3, 32, E), F32), ((GROUP * 8, 128), F32)
    sends_out, sums_out = ((128, 384), BF16), ((5, 32, E), F32)
    pairs = [(i, i) for i in range(ROW)] + [(i, i) for i in range(devices - ROW, devices)]
    for row in range(1, devices // ROW - 1, 2):
        for i in range(row * ROW, row * ROW + ROW):
            pairs += [(i, i + ROW), (i + ROW, i)]
    pack_args = (saved_states, adjoint_final, bathymetry)
    pack_args += (metrics, face_tag, face_link, send_faces)
    mine = call(pack_kernel, [((PACKED, E), F32)], pack_args)[0]
    halo = lax.ppermute(mine, "dom", pairs)
    both = [mine, halo]

    my_sends, boxes, rate = call(
        own_first_kernel,
        [sends_out, ((64, 128), F32), ((8, E), F32)],
        [mine, flip3, drag_rate] + tables,
        smem=(2,),
    )
    tables.append(rate)
    x, halo_sends = call(halo_first_kernel, [x_out, sends_out], (halo, flip3, boxes))
    def exchange(x):
        return lax.all_to_all(x, "dom", 0, 0, tiled=True, axis_index_groups=groups)

    bases, faces = ((2, 3, 32, E), F32), ((2, 3, 24, E), F32)
    far_outs, near_outs = [mixed, mixed, x_out], [bases, faces, faces, sums_out]
    sends = [my_sends, halo_sends]

    y = exchange(x)
    lam3, _, x, normals, sums = got = call(
        round3_kernel,
        far_outs + [((2, 3, 8, E), F32), sums_out],
        tables + both + [saved_states, y] + sends,
        scratch=[bases, faces, faces, ((4, 24, E), F32)],
    )
    y = exchange(x)
    x, base, ahead, motion, sums = call(
        round2_kernel,
        [x_out] + near_outs,
        tables + list(got[0:2]) + both + [sums, saved_states, y, normals] + sends,
        scratch=[bases, faces, faces, mixed, mixed, sums_out],
    )
    y = exchange(x)
    within = call(fold_kernel, [((8, 128), F32)], (y,))[0]
    within = lax.ppermute(within, "dom", spread_pairs(devices))
    lam1, _, x = call(
        lambda *refs: (far_kernel(1, 2, *refs), None)[1],
        far_outs,
        [y, spread3, base, motion] + both + [normals, ahead] + sends,
    )
    args = tables + [lam1, mine, sums, saved_states, lam3, wind_speed, wind_angle]
    base, motion, depth_gradient, speed_gradient, angle_gradient = call(
        lambda *refs: near_kernel(0, 1, *refs),
        [((1, 3, 32, E), F32), ((1, 3, 24, E), F32)] + [((28, E), F32)] * 3,
        args,
    )
    x, base = lax.optimization_barrier((x, base))
    y = exchange(call(insert_kernel, [x_out], (x, within))[0])
    initial, drag_gradient = call(
        lambda *refs: (far_kernel(0, 1, *refs), None)[1],
        [((3, 28, E), F32), ((1,), F32)],
        [y, spread3, base, motion, mine, normals],
        values=1,
    )
    return (initial, depth_gradient, speed_gradient, angle_gradient, drag_gradient)


def solution(mesh):
    return jax.shard_map(
        local,
        mesh=mesh,
        in_specs=(
            P(None, None, None, "dom"),
            P(None, None, "dom"),
            P(None, "dom"),
            P(None, "dom"),
            P(None, "dom"),
            P(),
            P(None, "dom"),
            P(None, "dom"),
            P(None, "dom"),
            P(None, "dom"),
        ),
        out_specs=(P(None, None, "dom"), P(None, "dom"), P(None, "dom"), P(None, "dom"), P()),
        check_vma=False,
    )
```

```python
import math

import jax
import jax.numpy as jnp
import ml_dtypes
import numpy as np
from jax import lax
from jax.experimental import pallas as pl
from jax.experimental.pallas import tpu as pltpu
from jax.sharding import PartitionSpec as P

GRAVITY = 1.0
PENALTY = 3.0
WIND_COEF = 5.0
TIME_STEP = 0.01
HALF = 0.5 * TIME_STEP
SIXTH = TIME_STEP / 6.0

GROUP = 32
STRIDE = 16
ROW = 16
REACH = 4
DIRS = 8
SLOTS = 16
E = 128
DEPTH, MISC = 12, 24
PACKED = MISC + 28 * 13 + 4
F32 = jnp.float32
BF16 = jnp.bfloat16


def solve_dense(matrix, right):
    system = np.array(matrix) + 0.0
    result = np.array(right) + 0.0
    extent = system.shape[0]
    for column in range(extent):
        pivot_index = column + int(np.argmax(np.abs(system[column:, column])))
        system[[column, pivot_index]] = system[[pivot_index, column]]
        result[[column, pivot_index]] = result[[pivot_index, column]]
        for target in range(column + 1, extent):
            factor = system[target, column] / system[column, column]
            system[target] = system[target] - factor * system[column]
            result[target] = result[target] - factor * result[column]
    solution = np.zeros(result.shape)
    for column in range(extent - 1, -1, -1):
        solution[column] = (
            result[column] - system[column, column + 1 :] @ solution[column + 1 :]
        ) / system[column, column]
    return solution


def element_tables():
    degree = 6
    nodes = [
        (column, row_index)
        for row_index in range(degree + 1)
        for column in range(degree + 1 - row_index)
    ]
    node_total = len(nodes)
    coord_x = np.array([node[0] / degree for node in nodes])
    coord_y = np.array([node[1] / degree for node in nodes])
    vander = np.zeros((node_total, node_total))
    vander_r = np.zeros((node_total, node_total))
    vander_s = np.zeros((node_total, node_total))
    grams = np.zeros((node_total, node_total))
    for column_index, power in enumerate(nodes):
        first, second = power
        vander[:, column_index] = coord_x**first * coord_y**second
        if first > 0:
            vander_r[:, column_index] = 0.5 * first * coord_x ** (first - 1) * coord_y**second
        if second > 0:
            vander_s[:, column_index] = 0.5 * second * coord_x**first * coord_y ** (second - 1)
        for other_index, other_power in enumerate(nodes):
            sum_x = first + other_power[0]
            sum_y = second + other_power[1]
            grams[column_index, other_index] = (
                4.0
                * math.factorial(sum_x)
                * math.factorial(sum_y)
                / math.factorial(sum_x + sum_y + 2)
            )
    deriv_r = solve_dense(vander.T, vander_r.T).T
    deriv_s = solve_dense(vander.T, vander_s.T).T
    mass_inverse = vander @ solve_dense(grams, vander.T)
    points = np.arange(degree + 1) / degree
    line_vander = np.stack([points**power for power in range(degree + 1)], axis=1)
    line_grams = np.array(
        [
            [2.0 / (first + second + 1) for second in range(degree + 1)]
            for first in range(degree + 1)
        ]
    )
    line_inverse = solve_dense(line_vander, np.eye(degree + 1))
    line_mass = line_inverse.T @ line_grams @ line_inverse
    lookup = {node: number for number, node in enumerate(nodes)}
    face_nodes = [
        [lookup[step, 0] for step in range(degree + 1)],
        [lookup[degree - step, step] for step in range(degree + 1)],
        [lookup[0, degree - step] for step in range(degree + 1)],
    ]
    embed = np.zeros((node_total, 3 * (degree + 1)))
    extract = np.zeros((3 * (degree + 1), node_total))
    for face_index in range(3):
        for step in range(degree + 1):
            extract[face_index * (degree + 1) + step, face_nodes[face_index][step]] = 1.0
            for other_step in range(degree + 1):
                embed[
                    face_nodes[face_index][other_step], face_index * (degree + 1) + step
                ] += line_mass[other_step, step]
    lifting = mass_inverse @ embed
    return deriv_r, deriv_s, lifting, extract


def offset_of(direction):
    return direction + 1 if direction < REACH else REACH - direction - 1


def neighbours():
    me = jnp.bitwise_and(lax.axis_index("dom"), GROUP - 1)
    found = []
    for own in (me + ROW, jnp.where(me < ROW, me, me + 2 * ROW)):
        for j in range(DIRS):
            place = own + offset_of(j)
            inner = (place >= ROW) & (place < ROW + GROUP)
            exists = (place >= 0) & (place < 4 * ROW)
            device = jnp.where(inner, place - ROW, jnp.where(place < ROW, place, place - 2 * ROW))
            found.append((jnp.where(exists, device, 0), jnp.where(inner, 0, 1), exists))
    return found


def spread_place(dx, dy):
    half, odd = dx // 2, dx % 2
    if dy == 0:
        return 6 + half + ROW * odd
    if dy == 2:
        return 4 + half + ROW * (1 - odd)
    return dx + (ROW if dy == 1 else 0)


def spread_pairs(devices):
    pairs = []
    for group in range(devices // GROUP):
        for dx in range(4):
            for dy in range(4):
                other = (group // 4 + dx) % 4 * 4 + (group % 4 + dy) % 4
                place = spread_place(dx, dy)
                source = place if dy == 0 else (place + ROW) % GROUP
                pairs.append((other * GROUP + source, group * GROUP + place))
    return pairs


def parts3(matrix, width):
    padded = np.zeros((matrix.shape[0], width))
    padded[:, : matrix.shape[1]] = matrix
    hi = padded.astype(np.float32).astype(ml_dtypes.bfloat16)
    lo = (padded - hi.astype(np.float64)).astype(ml_dtypes.bfloat16)
    return np.concatenate([hi, lo, hi], axis=1)


def constants():
    deriv_r, deriv_s, lifting, extract = element_tables()

    def pad_rows(matrix):
        return np.concatenate([matrix, np.zeros((4, matrix.shape[1]))])

    lift = np.zeros((24, 28))
    flip = np.zeros((24, 28))
    take = np.zeros((24, 28))
    give = np.zeros((24, 28))
    for face in range(3):
        for k in range(7):
            lift[8 * face + k] = lifting[:, 7 * face + k]
            flip[8 * face + k] = lifting[:, 7 * face + 6 - k]
            take[8 * face + k] = extract[7 * face + k]
            give[8 * face + k] = extract[7 * face + k]
        take[8 * face + 7] = extract[7 * face + 6]
    back = np.concatenate([pad_rows(deriv_r.T), pad_rows(deriv_s.T), lift, flip])
    back3 = parts3(back, 32)
    flip3 = parts3(flip, 32)
    grad3 = parts3(np.concatenate([pad_rows(deriv_r), pad_rows(deriv_s)]), 32)
    take2 = np.zeros((24, 64))
    take2[:, 0:28] = take
    take2[:, 32:60] = take
    spread = np.concatenate([pad_rows(give.T), flip @ give.T])
    spread3 = parts3(spread, 24)
    spread3 = np.concatenate([spread3, np.zeros((56, 8), ml_dtypes.bfloat16)], axis=1)
    as_bf16 = lambda m: jnp.asarray(np.asarray(m).astype(ml_dtypes.bfloat16))
    return as_bf16(back3), as_bf16(flip3), as_bf16(grad3), as_bf16(take2), as_bf16(spread3)


def dot(a, b):
    return jnp.dot(a, b, preferred_element_type=F32)


def dot_nt(a, b):
    return lax.dot_general(a, b, (((1,), (1,)), ((), ())), preferred_element_type=F32)


def halves(x):
    hi = x.astype(BF16).astype(F32)
    return hi, x - hi


def times3(matrix3, x):
    hi = x.astype(BF16)
    lo = (x - hi.astype(F32)).astype(BF16)
    return dot(matrix3, jnp.concatenate([hi, hi, lo], axis=0))


def spread_faces(spread3, faces):
    hi, lo = halves(faces)
    stack = jnp.concatenate([hi, hi, lo, jnp.zeros((8, faces.shape[1]), F32)], axis=0)
    return dot(spread3, stack.astype(BF16))


def geometry(misc):
    rx, ry, sx, sy = misc[0:1], misc[1:2], misc[2:3], misc[3:4]
    normals = []
    for nx, ny in ((-sx, -sy), (rx + sx, ry + sy), (-rx, -ry)):
        normals.append((nx, ny, jnp.sqrt(nx * nx + ny * ny)))
    return (rx, ry, sx, sy), normals


def jump_back(n, t, u, v, gh):
    nx, ny, size = n
    un = nx * u + ny * v
    mixed = u * t[1] + v * t[2]
    pull = 0.5 * PENALTY * size
    return (
        0.5 * (gh * (nx * t[1] + ny * t[2]) - un * mixed) - pull * t[0],
        0.5 * (nx * (t[0] + mixed) + un * t[1]) - pull * t[1],
        0.5 * (ny * (t[0] + mixed) + un * t[2]) - pull * t[2],
    )


def traces(flipped, normals):
    last = lax.broadcasted_iota(jnp.int32, (8, E), 0) == 7
    rows = []
    for c in range(3):
        rows.append(
            jnp.concatenate(
                [jnp.where(last, normals[f][c], flipped[c][f]) for f in range(3)], axis=1
            )
        )
    return jnp.concatenate(rows, axis=0)


def far_index(link):
    v = link - 3 * E
    j = lax.shift_right_arithmetic(v, 4)
    c = jnp.bitwise_and(v, 15)
    row = lax.shift_right_arithmetic(c, 3) * 64 + j * 8 + jnp.bitwise_and(c, 7)
    return jnp.where(v >= 0, row, -1)


def slot_rows(sends, v, block):
    first = 64 * block
    n = v.shape[1]
    hi, lo = halves(v)
    rows = [jnp.zeros((first, n), F32)] if block else []
    rest = [jnp.zeros((32 - v.shape[0], n), F32)] if v.shape[0] < 32 else []
    rows += [hi] + rest + [lo] + rest + [jnp.zeros((64 - first, n), F32)] * (1 - block)
    out = dot_nt(sends, jnp.concatenate(rows, axis=0).astype(BF16))
    lane = lax.broadcasted_iota(jnp.int32, (128, 128), 1)
    out = jnp.where((lane >= first) & (lane < first + 32), out + pltpu.roll(out, 96, 1), 0.0)
    return out[0:64] + pltpu.roll(out[64:128], 32, 1)


def send(x_ref, near_by, boxes):
    x_ref[...] = jnp.zeros(x_ref.shape, F32)
    for b in range(2):
        for j in range(DIRS):
            device, _, exists = near_by[DIRS * b + j]
            rows = pl.ds(pl.multiple_of(device * 8, 8), 8)
            box = jnp.where(exists, boxes[b][8 * j : 8 * j + 8], 0.0)
            x_ref[rows, :] = x_ref[rows, :] + box


def send_matrix(misc):
    faces = misc[16:24]
    lane = lax.broadcasted_iota(jnp.int32, (8, 128), 1)
    low = jnp.where(lane < 8, faces, 0.0)
    high = jnp.where((lane >= 8) & (lane < 16), faces, 0.0)
    both = low + pltpu.roll(high, 56, 1)
    row = lax.broadcasted_iota(jnp.int32, (8, 128), 0)
    lined = jnp.zeros((8, 128), F32)
    for j in range(DIRS):
        moved = both if j == 0 else pltpu.roll(both, 8 * j, 1)
        lined = lined + jnp.where(row == j, moved, 0.0)
    line = jnp.sum(lined, axis=0, keepdims=True)
    column = jnp.transpose(jnp.broadcast_to(line, (128, 128)))
    face = lax.broadcasted_iota(jnp.int32, (128, 128), 1).astype(F32)
    pieces = [jnp.where(column == face + float(128 * f), 1.0, 0.0) for f in range(3)]
    return jnp.concatenate(pieces, axis=1).astype(BF16)


def pack_kernel(q_ref, lam_ref, depth_ref, metric_ref, tag_ref, link_ref, face_ref, out_ref):
    out_ref[0:MISC, :] = jnp.zeros((MISC, E), F32)
    out_ref[0:4, :] = metric_ref[...]
    out_ref[4:7, :] = tag_ref[...].astype(F32)
    out_ref[8:11, :] = link_ref[...].astype(F32)
    out_ref[16:24, 0:16] = face_ref[...].astype(F32)
    for c in range(3):
        out_ref[MISC + 28 * c : MISC + 28 * c + 28, :] = lam_ref[c]
    for s in range(3):
        for c in range(3):
            first = MISC + 28 * (3 * (3 - s) + c)
            out_ref[first : first + 28, :] = q_ref[s + 1, c]
    out_ref[MISC + 28 * DEPTH : MISC + 28 * DEPTH + 28, :] = depth_ref[...]
    out_ref[PACKED - 4 : PACKED, :] = jnp.zeros((4, E), F32)


def field(part_ref, i, fill):
    first = MISC + 28 * i
    row = lax.broadcasted_iota(jnp.int32, (32, E), 0)
    return jnp.where(row < 28, part_ref[first : first + 32, :], fill)


def first_boxes(part_ref, flip3, block):
    misc = part_ref[0:MISC, :]
    weights = jnp.concatenate([HALF * field(part_ref, c, 0.0) for c in range(3)], axis=1)
    flipped = times3(flip3[...], weights)
    split = [
        [flipped[8 * f : 8 * f + 8, 128 * c : 128 * c + 128] for f in range(3)] for c in range(3)
    ]
    sends = send_matrix(misc)
    return sends, slot_rows(sends, traces(split, geometry(misc)[1]), block)


def own_first_kernel(part_ref, flip3, drag_ref, *refs):
    sends_ref, boxes_ref, rate_ref, near_ref, far_ref = refs[-5:]
    links = part_ref[8:11, :].astype(jnp.int32)
    near_ref[...], far_ref[...] = near_match(links), far_match(links)
    rate_ref[...] = jnp.full((8, E), drag_ref[0], F32)
    sends_ref[...], boxes_ref[...] = first_boxes(part_ref, flip3, 0)


def halo_first_kernel(part_ref, flip3, boxes_ref, x_ref, sends_ref):
    sends_ref[...], boxes = first_boxes(part_ref, flip3, 1)
    send(x_ref, neighbours(), [boxes_ref[...], boxes])


def near_match(links):
    rows = lax.broadcasted_iota(jnp.int32, (3 * E, E), 0)
    return jnp.concatenate(
        [jnp.where(rows == links[f : f + 1], 1.0, 0.0).astype(BF16) for f in range(3)], axis=1
    )


def far_match(links):
    rows = lax.broadcasted_iota(jnp.int32, (128, E), 0)
    found = [rows == far_index(links[f : f + 1]) for f in range(3)]
    return jnp.concatenate([jnp.where(x, 1.0, 0.0).astype(BF16) for x in found], axis=1)


def near_kernel(section, blocks, *refs):
    refs = list(refs)
    back3, flip3, grad3, take2, spread3 = [refs.pop(0)[...] for _ in range(5)]
    rate_ref = refs.pop(0)
    lams = [refs.pop(0) for _ in range(blocks)]
    parts = [refs.pop(0) for _ in range(blocks)]
    matches = [refs.pop(0) for _ in range(blocks)]
    old_ref = refs.pop(0) if section < 3 else None
    if section == 3:
        state_ref = refs.pop(0)
    if section == 0:
        state_ref, lam3_ref = refs.pop(0), refs.pop(0)
        speed_ref, angle_ref = refs.pop(0), refs.pop(0)
    base_ref = refs.pop(0)
    if section > 0:
        ahead_ref = refs.pop(0)
    motion_ref = refs.pop(0)
    if section == 3:
        past_ref = refs.pop(0)
    if section > 0:
        sum_ref = refs.pop(0)
    else:
        depth_out, speed_out, angle_out = refs.pop(0), refs.pop(0), refs.pop(0)
    scale = SIXTH if section == 2 else HALF
    later = SIXTH if section == 3 else HALF
    drag_rate = rate_ref[...][0:1]
    pad = jnp.ones((4, E), F32)

    if section == 3:
        lam = [[field(lams[b], c, 0.0) for c in range(3)] for b in range(blocks)]
    else:
        lam = [[lams[b][c] for c in range(3)] for b in range(blocks)]
    w = [[scale * x for x in lam[b]] for b in range(blocks)]
    if section == 0:
        q = [[jnp.concatenate([state_ref[0, c], pad], axis=0) for c in range(3)]]
    else:
        q = [[field(parts[b], 3 * (4 - section) + c, 1.0) for c in range(3)] for b in range(blocks)]
    z = [field(parts[b], DEPTH, 1.0) for b in range(blocks)]
    pulled = times3(back3, jnp.concatenate([x for b in range(blocks) for x in w[b]], axis=1))
    slopes = times3(grad3, jnp.concatenate(z, axis=1))
    fields = jnp.concatenate([x for b in range(blocks) for x in q[b] + [z[b]]], axis=1)
    hi, lo = halves(fields)
    at_faces = dot(take2, jnp.concatenate([hi, lo], axis=0).astype(BF16))

    if section == 3:
        fields = [jnp.concatenate([state_ref[0, c], pad], axis=0) for c in range(3)]
        fields += [field(parts[0], 9 + c, 1.0) for c in range(3)]
        hi, lo = halves(jnp.concatenate(fields, axis=1))
        past = dot(take2, jnp.concatenate([hi, lo], axis=0).astype(BF16))
        for i in range(2):
            finv = 1.0 / past[:, 384 * i : 384 * i + 128]
            past_ref[2 * i] = past[:, 384 * i + 128 : 384 * i + 256] * finv
            past_ref[2 * i + 1] = past[:, 384 * i + 256 : 384 * i + 384] * finv

    face_sums, volumes, opens = [], [], []
    for b in range(blocks):
        misc = parts[b][0:MISC, :]
        (rx, ry, sx, sy), normals = geometry(misc)
        part = lambda r0, r1, c: pulled[r0:r1, 384 * b + 128 * c : 384 * b + 128 * c + 128]
        h = q[b][0]
        inv = 1.0 / h
        u, v = q[b][1] * inv, q[b][2] * inv
        gh = GRAVITY * h
        along = [part(0, 32, c) for c in range(3)]
        across = [part(32, 64, c) for c in range(3)]
        fx = [-(rx * along[c] + sx * across[c]) for c in range(3)]
        fy = [-(ry * along[c] + sy * across[c]) for c in range(3)]
        cross = fx[2] + fy[1]
        slope_r = slopes[0:32, 128 * b : 128 * b + 128]
        slope_s = slopes[32:64, 128 * b : 128 * b + 128]
        slope_x = rx * slope_r + sx * slope_s
        slope_y = ry * slope_r + sy * slope_s
        flow = u * w[b][1] + v * w[b][2]
        drag_inv = drag_rate * inv
        volumes.append(
            (
                gh * (fx[1] + fy[2])
                - u * (u * fx[1] + v * cross)
                - v * v * fy[2]
                + GRAVITY * (slope_x * w[b][1] + slope_y * w[b][2])
                + drag_inv * flow,
                fx[0] + 2.0 * u * fx[1] + v * cross - drag_inv * w[b][1],
                fy[0] + u * cross + 2.0 * v * fy[2] - drag_inv * w[b][2],
            )
        )
        own = [[part(64 + 8 * f, 72 + 8 * f, c) for f in range(3)] for c in range(3)]
        flipped = [[part(88 + 8 * f, 96 + 8 * f, c) for f in range(3)] for c in range(3)]
        hi, lo = halves(traces(flipped, normals))
        pool = jnp.concatenate([hi, lo], axis=0).astype(BF16)
        found = dot(pool, matches[b][...])
        found = found[0:24] + found[24:48]
        opened = []
        sums = [[], [], []]
        for f in range(3):
            got = found[:, 128 * f : 128 * f + 128]
            value = lambda i: at_faces[
                8 * f : 8 * f + 8, 512 * b + 128 * i : 512 * b + 128 * i + 128
            ]
            fh, fm, fn, fz = value(0), value(1), value(2), value(3)
            finv = 1.0 / fh
            fu, fv, fgh = fm * finv, fn * finv, GRAVITY * fh
            motion_ref[b, 0, 8 * f : 8 * f + 8, :] = fu
            motion_ref[b, 1, 8 * f : 8 * f + 8, :] = fv
            motion_ref[b, 2, 8 * f : 8 * f + 8, :] = fgh
            tag = misc[4 + f : 5 + f]
            linked, wall, free = tag == 0.0, tag == 1.0, tag == 2.0
            nx, ny, size = normals[f]
            t = [own[c][f] for c in range(3)]
            mine = jump_back(normals[f], t, fu, fv, fgh)
            inv_size = 1.0 / size
            ux, uy = nx * inv_size, ny * inv_size
            twice = 2.0 * (ux * t[1] + uy * t[2])
            mirrored = (t[0], t[1] - twice * ux, t[2] - twice * uy)
            near = (got[0:8], got[8:16], got[16:24])
            other_n = tuple(
                jnp.where(linked, near[c][7:8], jnp.where(wall, m, 0.0))
                for c, m in enumerate((-nx, -ny, size))
            )
            other_t = [
                jnp.where(linked, near[c], jnp.where(wall, mirrored[c], 0.0)) for c in range(3)
            ]
            theirs = jump_back(other_n, other_t, fu, fv, fgh)
            zinv = 1.0 / fz
            out = jump_back(normals[f], t, fm * zinv, fn * zinv, GRAVITY * fz)
            opened.append(jnp.where(free, -out[0], 0.0))
            sums[0].append(mine[0] - theirs[0])
            sums[1].append(mine[1] - theirs[1] - jnp.where(free, out[1], 0.0))
            sums[2].append(mine[2] - theirs[2] - jnp.where(free, out[2], 0.0))
        face_sums.append([jnp.concatenate(sums[c], axis=0) for c in range(3)])
        if b == 0:
            opens = jnp.concatenate(opened, axis=0)
            height, moved = h, flow
    to_nodes = [x for b in range(blocks) for x in face_sums[b]]
    if section == 0:
        old = [old_ref[i] for i in range(5)]
        opens = opens + old[4][0:24]
        to_nodes.append(opens)
    nodes = spread_faces(spread3, jnp.concatenate(to_nodes, axis=1))
    for b in range(blocks):
        bases = []
        for c in range(3):
            first = lam[b][c]
            if section == 2:
                first = first * (1.0 / 3.0)
            if section == 0:
                first = first + (2.0 / 3.0) * lam3_ref[c]
            where = 384 * b + 128 * c
            bases.append(first + volumes[b][c] + nodes[0:32, where : where + 128])
            base_ref[b, c] = bases[c]
        if section > 0:
            ahead = times3(flip3, later * jnp.concatenate(bases, axis=1))
            for c in range(3):
                ahead_ref[b, c] = ahead[:, 128 * c : 128 * c + 128]
    w1, w2 = w[0][1], w[0][2]
    g1, g2 = height * w1, height * w2
    if section == 3:
        fold = moved[0:8] + moved[8:16] + moved[16:24] + moved[24:32]
        news = [w1, w2, g1, g2]
    else:
        if section > 0:
            old = [old_ref[i] for i in range(5)]
            opens = opens + old[4][0:24]
            fold = old[4][24:32] + (moved[0:8] + moved[8:16] + moved[16:24] + moved[24:32])
        news = [x + y for x, y in zip(old[0:4], (w1, w2, g1, g2))]
    if section > 0:
        for i in range(4):
            sum_ref[i] = news[i]
        sum_ref[4, 0:24, :] = opens
        sum_ref[4, 24:32, :] = fold
    else:
        rx, ry, sx, sy = geometry(parts[0][0:4, :])[0]
        w1, w2, g1, g2 = news
        pair = GRAVITY * jnp.concatenate([rx * g1 + ry * g2, sx * g1 + sy * g2], axis=1)
        pulled = times3(back3, pair)
        depth = pulled[0:32, 0:128] + pulled[32:64, 128:256] + nodes[0:32, 384:512]
        depth_out[...] = depth[0:28]
        speed, angle = speed_ref[...], angle_ref[...]
        cosine, sine = jnp.cos(angle), jnp.sin(angle)
        w1, w2 = w1[0:28], w2[0:28]
        speed_out[...] = (2.0 * WIND_COEF) * speed * (cosine * w1 + sine * w2)
        angle_out[...] = WIND_COEF * speed * speed * (cosine * w2 - sine * w1)


def far_kernel(section, blocks, *refs):
    refs = list(refs)
    y_ref, spread3_ref, base_ref, motion_ref = [refs.pop(0) for _ in range(4)]
    parts = [refs.pop(0) for _ in range(blocks)]
    matches = [refs.pop(0) for _ in range(blocks)]
    if section < 3:
        normal_ref = refs.pop(0)
    if section > 0:
        ahead_ref = refs.pop(0)
        sends_refs = [refs.pop(0), refs.pop(0)]
    if section == 3:
        past_ref = refs.pop(0)
    lam_refs = [refs.pop(0) for _ in range(blocks)]
    if section > 0:
        x_ref = refs.pop(0)
    if section == 3:
        normal_ref = refs.pop(0)
    if section == 0:
        drag_ref = refs.pop(0)
    later = SIXTH if section == 3 else HALF

    lane = lax.broadcasted_iota(jnp.int32, (8, 128), 1)
    place_in = jnp.bitwise_and(lane, 31)
    spare = (place_in >= 24) | (place_in == 7) | (place_in == 15) | (place_in == 23)
    near_by = neighbours()
    boxes, extras = [], []
    for b in range(2):
        for j in range(DIRS):
            if b < blocks:
                device, second, exists = near_by[DIRS * b + j]
                raw = y_ref[pl.ds(pl.multiple_of(device * 8, 8), 8), :]
                turned = pltpu.roll(raw, 64, 1)
                if section == 2:
                    box = jnp.where(second == 1, jnp.where(spare, 0.0, turned), raw)
                    extras.append(jnp.where(exists & (second == 0), turned, 0.0))
                else:
                    box = jnp.where(second == 1, turned, raw)
                boxes.append(jnp.where(exists, box, 0.0))
            else:
                boxes.append(jnp.zeros((8, 128), F32))
    stacks = [jnp.transpose(jnp.concatenate(boxes, axis=0))]
    if section == 2:
        stacks.append(jnp.transpose(jnp.concatenate(extras, axis=0)))
    left = lax.broadcasted_iota(jnp.int32, (32, 128), 1) < 64
    row = lax.broadcasted_iota(jnp.int32, (8, E), 0)
    face_sums, factors = [], []
    for b in range(blocks):
        pools = []
        for turned in stacks:
            low, high = turned[0:32], turned[32:64]
            if b == 0:
                pools.append(jnp.where(left, low, pltpu.roll(high, 64, 1)))
            else:
                pools.append(jnp.where(left, pltpu.roll(low, 64, 1), high))
        pool = jnp.concatenate(pools, axis=0)
        tall = pool.shape[0]
        pool = jnp.concatenate(halves(pool), axis=0).astype(BF16)
        got = dot(pool, matches[b][...])
        got = got[0:tall] + got[tall:]
        sums, scales = [[], [], []], [[], [], []]
        for f in range(3):
            piece = lambda r: got[r : r + 8, 128 * f : 128 * f + 128]
            far = [piece(8 * c) for c in range(3)]
            if section == 3:
                normal = tuple(x[7:8] for x in far)
                for i in range(3):
                    normal_ref[b, f, i : i + 1, :] = normal[i]
            else:
                normal = tuple(normal_ref[b, f, i : i + 1, :] for i in range(3))
            motion = [motion_ref[b, i, 8 * f : 8 * f + 8, :] for i in range(3)]
            theirs = jump_back(normal, far, *motion)
            for c in range(3):
                sums[c].append(-theirs[c])
            if section == 3 and b == 0:
                u0, v0, u1, v1 = [past_ref[i, 8 * f : 8 * f + 8, :] for i in range(4)]
                nx, ny, size = normal
                mean = 0.5 * (nx * u0 + ny * v0)
                rate = 0.5 * (nx * u1 + ny * v1) - 0.5 * PENALTY * size
                factors.append((mean, mean * u1 + u0 * rate, mean * v1 + v0 * rate))
            if section == 2:
                singles = (piece(24)[7:8], piece(56)[7:8], far[0][7:8], far[1][7:8], far[2][7:8])
                singles += (piece(32)[7:8], piece(40)[7:8])
                third = jnp.zeros((8, E), F32)
                for k in range(7):
                    third = jnp.where(row == k, singles[k], third)
                factors.append((piece(24), piece(56), third))
        face_sums += [jnp.concatenate(sums[c], axis=0) for c in range(3)]
    spread = spread_faces(spread3_ref[...], jnp.concatenate(face_sums, axis=1))
    slots = []
    partial = jnp.zeros((8, E), F32)
    for b in range(blocks):
        lam = []
        for c in range(3):
            where = 384 * b + 128 * c
            lam.append(base_ref[b, c] + spread[0:32, where : where + 128])
        if section > 0:
            for c in range(3):
                lam_refs[b][c] = lam[c]
            flipped = [
                ahead_ref[b, c]
                + later * spread[32:56, 384 * b + 128 * c : 384 * b + 128 * c + 128]
                for c in range(3)
            ]
            split = [[flipped[c][8 * f : 8 * f + 8] for f in range(3)] for c in range(3)]
            none = jnp.zeros((1, E), F32)
            lasts = [(none,) * 3] * 3
            if section == 3 and b == 0:
                lasts = [tuple(factors[f][2][k : k + 1] for k in (2, 3, 4)) for f in range(3)]
            trace = traces(split, lasts)
            if section == 3 and b == 0:
                last = row == 7
                third = lambda f, k: factors[f][2][k : k + 1]
                one = [jnp.where(last, third(f, 0), factors[f][0]) for f in range(3)]
                two = [jnp.where(last, third(f, 1), factors[f][1]) for f in range(3)]
                five = [jnp.where(last, third(f, 5), 0.0) for f in range(3)]
                six = [jnp.where(last, third(f, 6), 0.0) for f in range(3)]
                line = lambda parts: jnp.concatenate(parts, axis=1)
                trace = jnp.concatenate([trace, line(one)], axis=0)
                extra = [line(five), line(six), jnp.zeros((8, 3 * E), F32), line(two)]
                slots.append(
                    slot_rows(sends_refs[0][...], trace, 0)
                    + slot_rows(sends_refs[0][...], jnp.concatenate(extra, axis=0), 1)
                )
            else:
                slots.append(slot_rows(sends_refs[b][...], trace, b))
            if section == 2:
                for f in range(3):
                    for c in range(3):
                        partial = partial + split[c][f] * factors[3 * b + f][c]
        else:
            for c in range(3):
                lam_refs[b][c] = lam[c][0:28]
    if section > 0:
        send(x_ref, near_by, slots)
    else:
        group = lax.shift_right_logical(lax.axis_index("dom"), 5)
        total = jnp.zeros((8, 128), F32)
        for g in range(STRIDE):
            dx = jnp.bitwise_and(g // 4 - lax.shift_right_logical(group, 2), 3)
            dy = jnp.bitwise_and(g % 4 - jnp.bitwise_and(group, 3), 3)
            device = jnp.int32(0)
            for x in range(4):
                for y in range(4):
                    device = jnp.where((dx == x) & (dy == y), spread_place(x, y), device)
            total = total + y_ref[pl.ds(pl.multiple_of(device * 8, 8), 8), :]
        drag_ref[0] = jnp.sum(jnp.where(lane == 127, total, 0.0))
    return partial


def round3_kernel(*refs):
    refs = list(refs)
    take = lambda n: [refs.pop(0) for _ in range(n)]
    tables, parts, (state_ref, y_ref), sends = take(6), take(2), take(2), take(2)
    my_near, my_far = take(2)
    lams, (x_ref, normal_ref, sum_ref, halo_near, halo_far) = take(2), take(5)
    base, ahead, motion, past = refs
    links = parts[1][8:11, :].astype(jnp.int32)
    halo_near[...], halo_far[...] = near_match(links), far_match(links)
    near_kernel(
        3, 2, *tables, *parts, *parts, my_near, halo_near, state_ref,
        base, ahead, motion, past, sum_ref,
    )
    far_kernel(
        3, 2, y_ref, tables[4], base, motion, *parts, my_far, halo_far, ahead, *sends, past,
        *lams, x_ref, normal_ref,
    )


def round2_kernel(*refs):
    refs = list(refs)
    take = lambda n: [refs.pop(0) for _ in range(n)]
    tables, lams, parts, (old_ref, state_ref, y_ref) = take(6), take(2), take(2), take(3)
    (normal_ref,), sends, near_matches, far_matches = take(1), take(2), take(2), take(2)
    x_ref, base_ref, ahead_ref, motion_ref, sum_ref = take(5)
    base, ahead, motion, lam, halo_lam, sums = refs
    near_kernel(
        2, 2, *tables, *lams, *parts, *near_matches, old_ref, base, ahead, motion, sums
    )
    partial = far_kernel(
        2, 2, y_ref, tables[4], base, motion, *parts, *far_matches, normal_ref, ahead, *sends,
        lam, halo_lam, x_ref,
    )
    near_kernel(
        1, 2, *tables, lam, halo_lam, *parts, *near_matches, sums,
        base_ref, ahead_ref, motion_ref, sum_ref,
    )
    flow = state_ref[0, 1] * base_ref[0, 1, 0:28, :] + state_ref[0, 2] * base_ref[0, 2, 0:28, :]
    flow = jnp.concatenate([flow * (HALF / state_ref[0, 0]), jnp.zeros((4, E), F32)], axis=0)
    flow = flow[0:8] + flow[8:16] + flow[16:24] + flow[24:32]
    total = sum_ref[4, 24:32, :] - HALF * partial + flow
    put_value(x_ref, -jnp.sum(total, axis=1, keepdims=True))


def put_value(x_ref, value):
    lane = lax.broadcasted_iota(jnp.int32, (8, 128), 1)
    for e in range(GROUP):
        part = x_ref[8 * e : 8 * e + 8, :]
        x_ref[8 * e : 8 * e + 8, :] = jnp.where(lane == 127, value, part)


def fold_kernel(y_ref, out_ref):
    total = y_ref[0:8, :]
    for e in range(1, GROUP):
        total = total + y_ref[8 * e : 8 * e + 8, :]
    out_ref[...] = jnp.broadcast_to(total[:, 127:128], (8, 128))


def insert_kernel(x_ref, value_ref, out_ref):
    lane = lax.broadcasted_iota(jnp.int32, (8, 128), 1)
    for e in range(GROUP):
        part = x_ref[8 * e : 8 * e + 8, :]
        out_ref[8 * e : 8 * e + 8, :] = jnp.where(lane == 127, value_ref[...], part)


def call(kernel, outs, args, values=0, scratch=(), smem=()):
    vmem, scalar = pl.BlockSpec(memory_space=pltpu.VMEM), pl.BlockSpec(memory_space=pltpu.SMEM)
    return pl.pallas_call(
        kernel,
        in_specs=[scalar if i in smem else vmem for i in range(len(args))],
        out_specs=[vmem] * (len(outs) - values) + [scalar] * values,
        out_shape=[jax.ShapeDtypeStruct(shape, dtype) for shape, dtype in outs],
        scratch_shapes=[pltpu.VMEM(shape, dtype) for shape, dtype in scratch],
        compiler_params=pltpu.CompilerParams(vmem_limit_bytes=32 * 1024 * 1024),
    )(*args)


def local(
    saved_states,
    adjoint_final,
    bathymetry,
    wind_speed,
    wind_angle,
    drag_rate,
    metrics,
    face_link,
    face_tag,
    send_faces,
):
    devices = lax.axis_size("dom")
    groups = [list(range(g, g + GROUP)) for g in range(0, devices, GROUP)]
    back3, flip3, grad3, take2, spread3 = constants()
    tables = [back3, flip3, grad3, take2, spread3]

    mixed, x_out = ((3, 32, E), F32), ((GROUP * 8, 128), F32)
    sends_out, sums_out = ((128, 384), BF16), ((5, 32, E), F32)
    pairs = [(i, i) for i in range(ROW)] + [(i, i) for i in range(devices - ROW, devices)]
    for row in range(1, devices // ROW - 1, 2):
        for i in range(row * ROW, row * ROW + ROW):
            pairs += [(i, i + ROW), (i + ROW, i)]
    pack_args = (saved_states, adjoint_final, bathymetry)
    pack_args += (metrics, face_tag, face_link, send_faces)
    mine = call(pack_kernel, [((PACKED, E), F32)], pack_args)[0]
    halo = lax.ppermute(mine, "dom", pairs)
    both = [mine, halo]

    near_out, far_out = ((3 * E, 3 * E), BF16), ((128, 3 * E), BF16)
    my_sends, boxes, rate, my_near, my_far = call(
        own_first_kernel,
        [sends_out, ((64, 128), F32), ((8, E), F32), near_out, far_out],
        [mine, flip3, drag_rate] + tables,
        smem=(2,),
    )
    tables.append(rate)
    x, halo_sends = call(halo_first_kernel, [x_out, sends_out], (halo, flip3, boxes))
    def exchange(x):
        return lax.all_to_all(x, "dom", 0, 0, tiled=True, axis_index_groups=groups)

    bases, faces = ((2, 3, 32, E), F32), ((2, 3, 24, E), F32)
    far_outs, near_outs = [mixed, mixed, x_out], [bases, faces, faces, sums_out]
    sends = [my_sends, halo_sends]

    y = exchange(x)
    lam3, _, x, normals, sums, halo_near, halo_far = got = call(
        round3_kernel,
        far_outs + [((2, 3, 8, E), F32), sums_out, near_out, far_out],
        tables + both + [saved_states, y] + sends + [my_near, my_far],
        scratch=[bases, faces, faces, ((4, 24, E), F32)],
    )
    y = exchange(x)
    x, base, ahead, motion, sums = call(
        round2_kernel,
        [x_out] + near_outs,
        tables + list(got[0:2]) + both + [sums, saved_states, y, normals] + sends
        + [my_near, halo_near, my_far, halo_far],
        scratch=[bases, faces, faces, mixed, mixed, sums_out],
    )
    y = exchange(x)
    within = call(fold_kernel, [((8, 128), F32)], (y,))[0]
    within = lax.ppermute(within, "dom", spread_pairs(devices))
    lam1, _, x = call(
        lambda *refs: (far_kernel(1, 2, *refs), None)[1],
        far_outs,
        [y, spread3, base, motion] + both + [my_far, halo_far, normals, ahead] + sends,
    )
    args = tables + [lam1, mine, my_near, sums, saved_states, lam3, wind_speed, wind_angle]
    base, motion, depth_gradient, speed_gradient, angle_gradient = call(
        lambda *refs: near_kernel(0, 1, *refs),
        [((1, 3, 32, E), F32), ((1, 3, 24, E), F32)] + [((28, E), F32)] * 3,
        args,
    )
    x, base = lax.optimization_barrier((x, base))
    y = exchange(call(insert_kernel, [x_out], (x, within))[0])
    initial, drag_gradient = call(
        lambda *refs: (far_kernel(0, 1, *refs), None)[1],
        [((3, 28, E), F32), ((1,), F32)],
        [y, spread3, base, motion, mine, my_far, normals],
        values=1,
    )
    return (initial, depth_gradient, speed_gradient, angle_gradient, drag_gradient)


def solution(mesh):
    return jax.shard_map(
        local,
        mesh=mesh,
        in_specs=(
            P(None, None, None, "dom"),
            P(None, None, "dom"),
            P(None, "dom"),
            P(None, "dom"),
            P(None, "dom"),
            P(),
            P(None, "dom"),
            P(None, "dom"),
            P(None, "dom"),
            P(None, "dom"),
        ),
        out_specs=(P(None, None, "dom"), P(None, "dom"), P(None, "dom"), P(None, "dom"), P()),
        check_vma=False,
    )
```

```python
import math

import jax
import jax.numpy as jnp
import ml_dtypes
import numpy as np
from jax import lax
from jax.experimental import pallas as pl
from jax.experimental.pallas import tpu as pltpu
from jax.sharding import PartitionSpec as P

GRAVITY = 1.0
PENALTY = 3.0
WIND_COEF = 5.0
TIME_STEP = 0.01
HALF = 0.5 * TIME_STEP
SIXTH = TIME_STEP / 6.0

GROUP = 32
STRIDE = 16
ROW = 16
REACH = 4
DIRS = 8
SLOTS = 16
E = 128
DEPTH, MISC = 12, 24
PACKED = MISC + 28 * 13 + 4
F32 = jnp.float32
BF16 = jnp.bfloat16


def solve_dense(matrix, right):
    system = np.array(matrix) + 0.0
    result = np.array(right) + 0.0
    extent = system.shape[0]
    for column in range(extent):
        pivot_index = column + int(np.argmax(np.abs(system[column:, column])))
        system[[column, pivot_index]] = system[[pivot_index, column]]
        result[[column, pivot_index]] = result[[pivot_index, column]]
        for target in range(column + 1, extent):
            factor = system[target, column] / system[column, column]
            system[target] = system[target] - factor * system[column]
            result[target] = result[target] - factor * result[column]
    solution = np.zeros(result.shape)
    for column in range(extent - 1, -1, -1):
        solution[column] = (
            result[column] - system[column, column + 1 :] @ solution[column + 1 :]
        ) / system[column, column]
    return solution


def element_tables():
    degree = 6
    nodes = [
        (column, row_index)
        for row_index in range(degree + 1)
        for column in range(degree + 1 - row_index)
    ]
    node_total = len(nodes)
    coord_x = np.array([node[0] / degree for node in nodes])
    coord_y = np.array([node[1] / degree for node in nodes])
    vander = np.zeros((node_total, node_total))
    vander_r = np.zeros((node_total, node_total))
    vander_s = np.zeros((node_total, node_total))
    grams = np.zeros((node_total, node_total))
    for column_index, power in enumerate(nodes):
        first, second = power
        vander[:, column_index] = coord_x**first * coord_y**second
        if first > 0:
            vander_r[:, column_index] = 0.5 * first * coord_x ** (first - 1) * coord_y**second
        if second > 0:
            vander_s[:, column_index] = 0.5 * second * coord_x**first * coord_y ** (second - 1)
        for other_index, other_power in enumerate(nodes):
            sum_x = first + other_power[0]
            sum_y = second + other_power[1]
            grams[column_index, other_index] = (
                4.0
                * math.factorial(sum_x)
                * math.factorial(sum_y)
                / math.factorial(sum_x + sum_y + 2)
            )
    deriv_r = solve_dense(vander.T, vander_r.T).T
    deriv_s = solve_dense(vander.T, vander_s.T).T
    mass_inverse = vander @ solve_dense(grams, vander.T)
    points = np.arange(degree + 1) / degree
    line_vander = np.stack([points**power for power in range(degree + 1)], axis=1)
    line_grams = np.array(
        [
            [2.0 / (first + second + 1) for second in range(degree + 1)]
            for first in range(degree + 1)
        ]
    )
    line_inverse = solve_dense(line_vander, np.eye(degree + 1))
    line_mass = line_inverse.T @ line_grams @ line_inverse
    lookup = {node: number for number, node in enumerate(nodes)}
    face_nodes = [
        [lookup[step, 0] for step in range(degree + 1)],
        [lookup[degree - step, step] for step in range(degree + 1)],
        [lookup[0, degree - step] for step in range(degree + 1)],
    ]
    embed = np.zeros((node_total, 3 * (degree + 1)))
    extract = np.zeros((3 * (degree + 1), node_total))
    for face_index in range(3):
        for step in range(degree + 1):
            extract[face_index * (degree + 1) + step, face_nodes[face_index][step]] = 1.0
            for other_step in range(degree + 1):
                embed[
                    face_nodes[face_index][other_step], face_index * (degree + 1) + step
                ] += line_mass[other_step, step]
    lifting = mass_inverse @ embed
    return deriv_r, deriv_s, lifting, extract


def offset_of(direction):
    return direction + 1 if direction < REACH else REACH - direction - 1


def neighbours():
    me = jnp.bitwise_and(lax.axis_index("dom"), GROUP - 1)
    found = []
    for own in (me + ROW, jnp.where(me < ROW, me, me + 2 * ROW)):
        for j in range(DIRS):
            place = own + offset_of(j)
            inner = (place >= ROW) & (place < ROW + GROUP)
            exists = (place >= 0) & (place < 4 * ROW)
            device = jnp.where(inner, place - ROW, jnp.where(place < ROW, place, place - 2 * ROW))
            found.append((jnp.where(exists, device, 0), jnp.where(inner, 0, 1), exists))
    return found


def spread_place(dx, dy):
    half, odd = dx // 2, dx % 2
    if dy == 0:
        return 6 + half + ROW * odd
    if dy == 2:
        return 4 + half + ROW * (1 - odd)
    return dx + (ROW if dy == 1 else 0)


def spread_pairs(devices):
    pairs = []
    for group in range(devices // GROUP):
        for dx in range(4):
            for dy in range(4):
                other = (group // 4 + dx) % 4 * 4 + (group % 4 + dy) % 4
                place = spread_place(dx, dy)
                source = place if dy == 0 else (place + ROW) % GROUP
                pairs.append((other * GROUP + source, group * GROUP + place))
    return pairs


def parts3(matrix, width):
    padded = np.zeros((matrix.shape[0], width))
    padded[:, : matrix.shape[1]] = matrix
    hi = padded.astype(np.float32).astype(ml_dtypes.bfloat16)
    lo = (padded - hi.astype(np.float64)).astype(ml_dtypes.bfloat16)
    return np.concatenate([hi, lo, hi], axis=1)


def constants():
    deriv_r, deriv_s, lifting, extract = element_tables()

    def pad_rows(matrix):
        return np.concatenate([matrix, np.zeros((4, matrix.shape[1]))])

    lift = np.zeros((24, 28))
    flip = np.zeros((24, 28))
    take = np.zeros((24, 28))
    give = np.zeros((24, 28))
    for face in range(3):
        for k in range(7):
            lift[8 * face + k] = lifting[:, 7 * face + k]
            flip[8 * face + k] = lifting[:, 7 * face + 6 - k]
            take[8 * face + k] = extract[7 * face + k]
            give[8 * face + k] = extract[7 * face + k]
        take[8 * face + 7] = extract[7 * face + 6]
    back = np.concatenate([pad_rows(deriv_r.T), pad_rows(deriv_s.T), lift, flip])
    back3 = parts3(back, 32)
    flip3 = parts3(flip, 32)
    grad3 = parts3(np.concatenate([pad_rows(deriv_r), pad_rows(deriv_s)]), 32)
    take2 = np.zeros((24, 64))
    take2[:, 0:28] = take
    take2[:, 32:60] = take
    spread = np.concatenate([pad_rows(give.T), flip @ give.T])
    spread3 = parts3(spread, 24)
    spread3 = np.concatenate([spread3, np.zeros((56, 8), ml_dtypes.bfloat16)], axis=1)
    as_bf16 = lambda m: jnp.asarray(np.asarray(m).astype(ml_dtypes.bfloat16))
    return as_bf16(back3), as_bf16(flip3), as_bf16(grad3), as_bf16(take2), as_bf16(spread3)


def dot(a, b):
    return jnp.dot(a, b, preferred_element_type=F32)


def dot_nt(a, b):
    return lax.dot_general(a, b, (((1,), (1,)), ((), ())), preferred_element_type=F32)


def halves(x):
    hi = x.astype(BF16).astype(F32)
    return hi, x - hi


def times3(matrix3, x):
    hi = x.astype(BF16)
    lo = (x - hi.astype(F32)).astype(BF16)
    return dot(matrix3, jnp.concatenate([hi, hi, lo], axis=0))


def spread_faces(spread3, faces):
    hi, lo = halves(faces)
    stack = jnp.concatenate([hi, hi, lo, jnp.zeros((8, faces.shape[1]), F32)], axis=0)
    return dot(spread3, stack.astype(BF16))


def geometry(misc):
    rx, ry, sx, sy = misc[0:1], misc[1:2], misc[2:3], misc[3:4]
    normals = []
    for nx, ny in ((-sx, -sy), (rx + sx, ry + sy), (-rx, -ry)):
        normals.append((nx, ny, jnp.sqrt(nx * nx + ny * ny)))
    return (rx, ry, sx, sy), normals


def jump_back(n, t, u, v, gh):
    nx, ny, size = n
    un = nx * u + ny * v
    mixed = u * t[1] + v * t[2]
    pull = 0.5 * PENALTY * size
    return (
        0.5 * (gh * (nx * t[1] + ny * t[2]) - un * mixed) - pull * t[0],
        0.5 * (nx * (t[0] + mixed) + un * t[1]) - pull * t[1],
        0.5 * (ny * (t[0] + mixed) + un * t[2]) - pull * t[2],
    )


def traces(flipped, normals):
    last = lax.broadcasted_iota(jnp.int32, (8, E), 0) == 7
    rows = []
    for c in range(3):
        rows.append(
            jnp.concatenate(
                [jnp.where(last, normals[f][c], flipped[c][f]) for f in range(3)], axis=1
            )
        )
    return jnp.concatenate(rows, axis=0)


def far_index(link, width=8):
    v = link - 3 * E
    j = lax.shift_right_arithmetic(v, 4)
    c = jnp.bitwise_and(v, 15)
    part = lax.shift_right_arithmetic(c, width.bit_length() - 1)
    row = part * (DIRS * width) + j * width + jnp.bitwise_and(c, width - 1)
    return jnp.where(v >= 0, row, -1)


def slot_rows(sends, v, block):
    first = 64 * block
    n = v.shape[1]
    hi, lo = halves(v)
    rows = [jnp.zeros((first, n), F32)] if block else []
    rest = [jnp.zeros((32 - v.shape[0], n), F32)] if v.shape[0] < 32 else []
    rows += [hi] + rest + [lo] + rest + [jnp.zeros((64 - first, n), F32)] * (1 - block)
    out = dot_nt(sends, jnp.concatenate(rows, axis=0).astype(BF16))
    lane = lax.broadcasted_iota(jnp.int32, (128, 128), 1)
    out = jnp.where((lane >= first) & (lane < first + 32), out + pltpu.roll(out, 96, 1), 0.0)
    return out[0:64] + pltpu.roll(out[64:128], 32, 1)


def quarter_rows(sends, v):
    hi, lo = halves(v)
    rest = jnp.zeros((8, v.shape[1]), F32)
    stack = jnp.concatenate([hi, rest, lo, rest, jnp.zeros((64, v.shape[1]), F32)], axis=0)
    out = dot_nt(sends, stack.astype(BF16))
    lane = lax.broadcasted_iota(jnp.int32, (128, 128), 1)
    out = jnp.where(lane < 32, out + pltpu.roll(out, 96, 1), 0.0)
    total = out[0:32]
    for h in range(1, 4):
        total = total + pltpu.roll(out[32 * h : 32 * h + 32], 32 * h, 1)
    return total


def send_quarters(x_ref, near_by, boxes):
    x_ref[...] = jnp.zeros(x_ref.shape, F32)
    for b in range(2):
        for j in range(DIRS):
            device, second, exists = near_by[DIRS * b + j]
            box = jnp.where(exists & (second == 0), boxes[b][4 * j : 4 * j + 4], 0.0)
            x_ref[device] = x_ref[device] + box


def send(x_ref, near_by, boxes):
    x_ref[...] = jnp.zeros(x_ref.shape, F32)
    for b in range(2):
        for j in range(DIRS):
            device, _, exists = near_by[DIRS * b + j]
            rows = pl.ds(pl.multiple_of(device * 8, 8), 8)
            box = jnp.where(exists, boxes[b][8 * j : 8 * j + 8], 0.0)
            x_ref[rows, :] = x_ref[rows, :] + box


def send_matrix(misc, width=8):
    faces = misc[16:24]
    lane = lax.broadcasted_iota(jnp.int32, (8, 128), 1)
    both = jnp.zeros((8, 128), F32)
    for h in range(SLOTS // width):
        part = jnp.where((lane >= width * h) & (lane < width * h + width), faces, 0.0)
        both = both + (pltpu.roll(part, (DIRS - 1) * width * h, 1) if h else part)
    row = lax.broadcasted_iota(jnp.int32, (8, 128), 0)
    lined = jnp.zeros((8, 128), F32)
    for j in range(DIRS):
        moved = both if j == 0 else pltpu.roll(both, width * j, 1)
        lined = lined + jnp.where(row == j, moved, 0.0)
    line = jnp.sum(lined, axis=0, keepdims=True)
    column = jnp.transpose(jnp.broadcast_to(line, (128, 128)))
    face = lax.broadcasted_iota(jnp.int32, (128, 128), 1).astype(F32)
    pieces = [jnp.where(column == face + float(128 * f), 1.0, 0.0) for f in range(3)]
    return jnp.concatenate(pieces, axis=1).astype(BF16)


def pack_kernel(q_ref, lam_ref, depth_ref, metric_ref, tag_ref, link_ref, face_ref, out_ref):
    out_ref[0:MISC, :] = jnp.zeros((MISC, E), F32)
    out_ref[0:4, :] = metric_ref[...]
    out_ref[4:7, :] = tag_ref[...].astype(F32)
    out_ref[8:11, :] = link_ref[...].astype(F32)
    out_ref[16:24, 0:16] = face_ref[...].astype(F32)
    for c in range(3):
        out_ref[MISC + 28 * c : MISC + 28 * c + 28, :] = lam_ref[c]
    for s in range(3):
        for c in range(3):
            first = MISC + 28 * (3 * (3 - s) + c)
            out_ref[first : first + 28, :] = q_ref[s + 1, c]
    out_ref[MISC + 28 * DEPTH : MISC + 28 * DEPTH + 28, :] = depth_ref[...]
    out_ref[PACKED - 4 : PACKED, :] = jnp.zeros((4, E), F32)


def field(part_ref, i, fill):
    first = MISC + 28 * i
    row = lax.broadcasted_iota(jnp.int32, (32, E), 0)
    return jnp.where(row < 28, part_ref[first : first + 32, :], fill)


def first_boxes(part_ref, flip3, block):
    misc = part_ref[0:MISC, :]
    weights = jnp.concatenate([HALF * field(part_ref, c, 0.0) for c in range(3)], axis=1)
    flipped = times3(flip3[...], weights)
    split = [
        [flipped[8 * f : 8 * f + 8, 128 * c : 128 * c + 128] for f in range(3)] for c in range(3)
    ]
    sends = send_matrix(misc)
    return sends, slot_rows(sends, traces(split, geometry(misc)[1]), block)


def own_first_kernel(part_ref, flip3, drag_ref, *refs):
    sends_ref, boxes_ref, rate_ref, near_ref, far_ref, last_ref = refs[-6:]
    links = part_ref[8:11, :].astype(jnp.int32)
    near_ref[...], far_ref[...] = near_match(links), far_match(links)
    last_ref[...] = far_match(links, 4)
    rate_ref[...] = jnp.full((8, E), drag_ref[0], F32)
    sends_ref[...], boxes_ref[...] = first_boxes(part_ref, flip3, 0)


def halo_first_kernel(part_ref, flip3, boxes_ref, x_ref, sends_ref):
    sends_ref[...], boxes = first_boxes(part_ref, flip3, 1)
    send(x_ref, neighbours(), [boxes_ref[...], boxes])


def near_match(links):
    rows = lax.broadcasted_iota(jnp.int32, (3 * E, E), 0)
    return jnp.concatenate(
        [jnp.where(rows == links[f : f + 1], 1.0, 0.0).astype(BF16) for f in range(3)], axis=1
    )


def far_match(links, width=8):
    rows = lax.broadcasted_iota(jnp.int32, (128, E), 0)
    found = [rows == far_index(links[f : f + 1], width) for f in range(3)]
    return jnp.concatenate([jnp.where(x, 1.0, 0.0).astype(BF16) for x in found], axis=1)


def near_kernel(section, blocks, *refs):
    refs = list(refs)
    back3, flip3, grad3, take2, spread3 = [refs.pop(0)[...] for _ in range(5)]
    rate_ref = refs.pop(0)
    lams = [refs.pop(0) for _ in range(blocks)]
    parts = [refs.pop(0) for _ in range(blocks)]
    matches = [refs.pop(0) for _ in range(blocks)]
    old_ref = refs.pop(0) if section < 3 else None
    if section == 3:
        state_ref = refs.pop(0)
    if section == 0:
        state_ref, lam3_ref = refs.pop(0), refs.pop(0)
        speed_ref, angle_ref = refs.pop(0), refs.pop(0)
    base_ref = refs.pop(0)
    if section > 0:
        ahead_ref = refs.pop(0)
    motion_ref = refs.pop(0)
    if section == 3:
        past_ref = refs.pop(0)
    if section > 0:
        sum_ref = refs.pop(0)
    else:
        depth_out, speed_out, angle_out = refs.pop(0), refs.pop(0), refs.pop(0)
    scale = SIXTH if section == 2 else HALF
    later = SIXTH if section == 3 else HALF
    drag_rate = rate_ref[...][0:1]
    pad = jnp.ones((4, E), F32)

    if section == 3:
        lam = [[field(lams[b], c, 0.0) for c in range(3)] for b in range(blocks)]
    else:
        lam = [[lams[b][c] for c in range(3)] for b in range(blocks)]
    w = [[scale * x for x in lam[b]] for b in range(blocks)]
    if section == 0:
        q = [[jnp.concatenate([state_ref[0, c], pad], axis=0) for c in range(3)]]
    else:
        q = [[field(parts[b], 3 * (4 - section) + c, 1.0) for c in range(3)] for b in range(blocks)]
    z = [field(parts[b], DEPTH, 1.0) for b in range(blocks)]
    pulled = times3(back3, jnp.concatenate([x for b in range(blocks) for x in w[b]], axis=1))
    slopes = times3(grad3, jnp.concatenate(z, axis=1))
    fields = jnp.concatenate([x for b in range(blocks) for x in q[b] + [z[b]]], axis=1)
    hi, lo = halves(fields)
    at_faces = dot(take2, jnp.concatenate([hi, lo], axis=0).astype(BF16))

    if section == 3:
        fields = [jnp.concatenate([state_ref[0, c], pad], axis=0) for c in range(3)]
        fields += [field(parts[0], 9 + c, 1.0) for c in range(3)]
        hi, lo = halves(jnp.concatenate(fields, axis=1))
        past = dot(take2, jnp.concatenate([hi, lo], axis=0).astype(BF16))
        for i in range(2):
            finv = 1.0 / past[:, 384 * i : 384 * i + 128]
            past_ref[2 * i] = past[:, 384 * i + 128 : 384 * i + 256] * finv
            past_ref[2 * i + 1] = past[:, 384 * i + 256 : 384 * i + 384] * finv

    face_sums, volumes, opens = [], [], []
    for b in range(blocks):
        misc = parts[b][0:MISC, :]
        (rx, ry, sx, sy), normals = geometry(misc)
        part = lambda r0, r1, c: pulled[r0:r1, 384 * b + 128 * c : 384 * b + 128 * c + 128]
        h = q[b][0]
        inv = 1.0 / h
        u, v = q[b][1] * inv, q[b][2] * inv
        gh = GRAVITY * h
        along = [part(0, 32, c) for c in range(3)]
        across = [part(32, 64, c) for c in range(3)]
        fx = [-(rx * along[c] + sx * across[c]) for c in range(3)]
        fy = [-(ry * along[c] + sy * across[c]) for c in range(3)]
        cross = fx[2] + fy[1]
        slope_r = slopes[0:32, 128 * b : 128 * b + 128]
        slope_s = slopes[32:64, 128 * b : 128 * b + 128]
        slope_x = rx * slope_r + sx * slope_s
        slope_y = ry * slope_r + sy * slope_s
        flow = u * w[b][1] + v * w[b][2]
        drag_inv = drag_rate * inv
        volumes.append(
            (
                gh * (fx[1] + fy[2])
                - u * (u * fx[1] + v * cross)
                - v * v * fy[2]
                + GRAVITY * (slope_x * w[b][1] + slope_y * w[b][2])
                + drag_inv * flow,
                fx[0] + 2.0 * u * fx[1] + v * cross - drag_inv * w[b][1],
                fy[0] + u * cross + 2.0 * v * fy[2] - drag_inv * w[b][2],
            )
        )
        own = [[part(64 + 8 * f, 72 + 8 * f, c) for f in range(3)] for c in range(3)]
        flipped = [[part(88 + 8 * f, 96 + 8 * f, c) for f in range(3)] for c in range(3)]
        hi, lo = halves(traces(flipped, normals))
        pool = jnp.concatenate([hi, lo], axis=0).astype(BF16)
        found = dot(pool, matches[b][...])
        found = found[0:24] + found[24:48]
        opened = []
        sums = [[], [], []]
        for f in range(3):
            got = found[:, 128 * f : 128 * f + 128]
            value = lambda i: at_faces[
                8 * f : 8 * f + 8, 512 * b + 128 * i : 512 * b + 128 * i + 128
            ]
            fh, fm, fn, fz = value(0), value(1), value(2), value(3)
            finv = 1.0 / fh
            fu, fv, fgh = fm * finv, fn * finv, GRAVITY * fh
            motion_ref[b, 0, 8 * f : 8 * f + 8, :] = fu
            motion_ref[b, 1, 8 * f : 8 * f + 8, :] = fv
            motion_ref[b, 2, 8 * f : 8 * f + 8, :] = fgh
            tag = misc[4 + f : 5 + f]
            linked, wall, free = tag == 0.0, tag == 1.0, tag == 2.0
            nx, ny, size = normals[f]
            t = [own[c][f] for c in range(3)]
            mine = jump_back(normals[f], t, fu, fv, fgh)
            inv_size = 1.0 / size
            ux, uy = nx * inv_size, ny * inv_size
            twice = 2.0 * (ux * t[1] + uy * t[2])
            mirrored = (t[0], t[1] - twice * ux, t[2] - twice * uy)
            near = (got[0:8], got[8:16], got[16:24])
            other_n = tuple(
                jnp.where(linked, near[c][7:8], jnp.where(wall, m, 0.0))
                for c, m in enumerate((-nx, -ny, size))
            )
            other_t = [
                jnp.where(linked, near[c], jnp.where(wall, mirrored[c], 0.0)) for c in range(3)
            ]
            theirs = jump_back(other_n, other_t, fu, fv, fgh)
            zinv = 1.0 / fz
            out = jump_back(normals[f], t, fm * zinv, fn * zinv, GRAVITY * fz)
            opened.append(jnp.where(free, -out[0], 0.0))
            sums[0].append(mine[0] - theirs[0])
            sums[1].append(mine[1] - theirs[1] - jnp.where(free, out[1], 0.0))
            sums[2].append(mine[2] - theirs[2] - jnp.where(free, out[2], 0.0))
        face_sums.append([jnp.concatenate(sums[c], axis=0) for c in range(3)])
        if b == 0:
            opens = jnp.concatenate(opened, axis=0)
            height, moved = h, flow
    to_nodes = [x for b in range(blocks) for x in face_sums[b]]
    if section == 0:
        old = [old_ref[i] for i in range(5)]
        opens = opens + old[4][0:24]
        to_nodes.append(opens)
    nodes = spread_faces(spread3, jnp.concatenate(to_nodes, axis=1))
    for b in range(blocks):
        bases = []
        for c in range(3):
            first = lam[b][c]
            if section == 2:
                first = first * (1.0 / 3.0)
            if section == 0:
                first = first + (2.0 / 3.0) * lam3_ref[c]
            where = 384 * b + 128 * c
            bases.append(first + volumes[b][c] + nodes[0:32, where : where + 128])
            base_ref[b, c] = bases[c]
        if section > 0:
            ahead = times3(flip3, later * jnp.concatenate(bases, axis=1))
            for c in range(3):
                ahead_ref[b, c] = ahead[:, 128 * c : 128 * c + 128]
    w1, w2 = w[0][1], w[0][2]
    g1, g2 = height * w1, height * w2
    if section == 3:
        fold = moved[0:8] + moved[8:16] + moved[16:24] + moved[24:32]
        news = [w1, w2, g1, g2]
    else:
        if section > 0:
            old = [old_ref[i] for i in range(5)]
            opens = opens + old[4][0:24]
            fold = old[4][24:32] + (moved[0:8] + moved[8:16] + moved[16:24] + moved[24:32])
        news = [x + y for x, y in zip(old[0:4], (w1, w2, g1, g2))]
    if section > 0:
        for i in range(4):
            sum_ref[i] = news[i]
        sum_ref[4, 0:24, :] = opens
        sum_ref[4, 24:32, :] = fold
    else:
        rx, ry, sx, sy = geometry(parts[0][0:4, :])[0]
        w1, w2, g1, g2 = news
        pair = GRAVITY * jnp.concatenate([rx * g1 + ry * g2, sx * g1 + sy * g2], axis=1)
        pulled = times3(back3, pair)
        depth = pulled[0:32, 0:128] + pulled[32:64, 128:256] + nodes[0:32, 384:512]
        depth_out[...] = depth[0:28]
        speed, angle = speed_ref[...], angle_ref[...]
        cosine, sine = jnp.cos(angle), jnp.sin(angle)
        w1, w2 = w1[0:28], w2[0:28]
        speed_out[...] = (2.0 * WIND_COEF) * speed * (cosine * w1 + sine * w2)
        angle_out[...] = WIND_COEF * speed * speed * (cosine * w2 - sine * w1)


def far_kernel(section, blocks, *refs):
    refs = list(refs)
    y_ref, spread3_ref, base_ref, motion_ref = [refs.pop(0) for _ in range(4)]
    parts = [refs.pop(0) for _ in range(blocks)]
    matches = [refs.pop(0) for _ in range(blocks)]
    if section < 3:
        normal_ref = refs.pop(0)
    if section > 0:
        ahead_ref = refs.pop(0)
    if section > 1:
        sends_refs = [refs.pop(0), refs.pop(0)]
    if section == 3:
        past_ref = refs.pop(0)
    lam_refs = [refs.pop(0) for _ in range(blocks)]
    if section > 0:
        x_ref = refs.pop(0)
    if section == 3:
        normal_ref = refs.pop(0)
    if section == 0:
        drag_ref = refs.pop(0)
    later = SIXTH if section == 3 else HALF

    lane = lax.broadcasted_iota(jnp.int32, (8, 128), 1)
    place_in = jnp.bitwise_and(lane, 31)
    spare = (place_in >= 24) | (place_in == 7) | (place_in == 15) | (place_in == 23)
    near_by = neighbours()
    boxes, extras = [], []
    for b in range(2):
        for j in range(DIRS):
            if b < blocks:
                device, second, exists = near_by[DIRS * b + j]
                if section == 0:
                    boxes.append(jnp.where(exists, y_ref[device], 0.0))
                    continue
                raw = y_ref[pl.ds(pl.multiple_of(device * 8, 8), 8), :]
                turned = pltpu.roll(raw, 64, 1)
                if section == 2:
                    box = jnp.where(second == 1, jnp.where(spare, 0.0, turned), raw)
                    extras.append(jnp.where(exists & (second == 0), turned, 0.0))
                else:
                    box = jnp.where(second == 1, turned, raw)
                boxes.append(jnp.where(exists, box, 0.0))
            elif section > 0:
                boxes.append(jnp.zeros((8, 128), F32))
    if section == 0:
        boxes.append(jnp.zeros((96, 128), F32))
    stacks = [jnp.transpose(jnp.concatenate(boxes, axis=0))]
    if section == 2:
        stacks.append(jnp.transpose(jnp.concatenate(extras, axis=0)))
    left = lax.broadcasted_iota(jnp.int32, (32, 128), 1) < 64
    row = lax.broadcasted_iota(jnp.int32, (8, E), 0)
    face_sums, factors = [], []
    for b in range(blocks):
        pools = []
        for turned in stacks:
            low, high = turned[0:32], turned[32:64]
            if section == 0:
                pool = low
                for h in range(1, 4):
                    pool = pool + pltpu.roll(turned[32 * h : 32 * h + 32], 32 * h, 1)
                pools.append(pool)
            elif b == 0:
                pools.append(jnp.where(left, low, pltpu.roll(high, 64, 1)))
            else:
                pools.append(jnp.where(left, pltpu.roll(low, 64, 1), high))
        pool = jnp.concatenate(pools, axis=0)
        tall = pool.shape[0]
        pool = jnp.concatenate(halves(pool), axis=0).astype(BF16)
        got = dot(pool, matches[b][...])
        got = got[0:tall] + got[tall:]
        sums, scales = [[], [], []], [[], [], []]
        for f in range(3):
            piece = lambda r: got[r : r + 8, 128 * f : 128 * f + 128]
            far = [piece(8 * c) for c in range(3)]
            if section == 3:
                normal = tuple(x[7:8] for x in far)
                for i in range(3):
                    normal_ref[b, f, i : i + 1, :] = normal[i]
            else:
                normal = tuple(normal_ref[b, f, i : i + 1, :] for i in range(3))
            motion = [motion_ref[b, i, 8 * f : 8 * f + 8, :] for i in range(3)]
            theirs = jump_back(normal, far, *motion)
            for c in range(3):
                sums[c].append(-theirs[c])
            if section == 3 and b == 0:
                u0, v0, u1, v1 = [past_ref[i, 8 * f : 8 * f + 8, :] for i in range(4)]
                nx, ny, size = normal
                mean = 0.5 * (nx * u0 + ny * v0)
                rate = 0.5 * (nx * u1 + ny * v1) - 0.5 * PENALTY * size
                factors.append((mean, mean * u1 + u0 * rate, mean * v1 + v0 * rate))
            if section == 2:
                singles = (piece(24)[7:8], piece(56)[7:8], far[0][7:8], far[1][7:8], far[2][7:8])
                singles += (piece(32)[7:8], piece(40)[7:8])
                third = jnp.zeros((8, E), F32)
                for k in range(7):
                    third = jnp.where(row == k, singles[k], third)
                factors.append((piece(24), piece(56), third))
        face_sums += [jnp.concatenate(sums[c], axis=0) for c in range(3)]
    spread = spread_faces(spread3_ref[...], jnp.concatenate(face_sums, axis=1))
    slots = []
    partial = jnp.zeros((8, E), F32)
    for b in range(blocks):
        lam = []
        for c in range(3):
            where = 384 * b + 128 * c
            lam.append(base_ref[b, c] + spread[0:32, where : where + 128])
        if section > 0:
            for c in range(3):
                lam_refs[b][c] = lam[c]
            flipped = [
                ahead_ref[b, c]
                + later * spread[32:56, 384 * b + 128 * c : 384 * b + 128 * c + 128]
                for c in range(3)
            ]
            split = [[flipped[c][8 * f : 8 * f + 8] for f in range(3)] for c in range(3)]
            none = jnp.zeros((1, E), F32)
            lasts = [(none,) * 3] * 3
            if section == 3 and b == 0:
                lasts = [tuple(factors[f][2][k : k + 1] for k in (2, 3, 4)) for f in range(3)]
            trace = traces(split, lasts)
            if section == 3 and b == 0:
                last = row == 7
                third = lambda f, k: factors[f][2][k : k + 1]
                one = [jnp.where(last, third(f, 0), factors[f][0]) for f in range(3)]
                two = [jnp.where(last, third(f, 1), factors[f][1]) for f in range(3)]
                five = [jnp.where(last, third(f, 5), 0.0) for f in range(3)]
                six = [jnp.where(last, third(f, 6), 0.0) for f in range(3)]
                line = lambda parts: jnp.concatenate(parts, axis=1)
                trace = jnp.concatenate([trace, line(one)], axis=0)
                extra = [line(five), line(six), jnp.zeros((8, 3 * E), F32), line(two)]
                slots.append(
                    slot_rows(sends_refs[0][...], trace, 0)
                    + slot_rows(sends_refs[0][...], jnp.concatenate(extra, axis=0), 1)
                )
            elif section == 1:
                slots.append(quarter_rows(send_matrix(parts[b][0:MISC, :], 4), trace))
            else:
                slots.append(slot_rows(sends_refs[b][...], trace, b))
            if section == 2:
                for f in range(3):
                    for c in range(3):
                        partial = partial + split[c][f] * factors[3 * b + f][c]
        else:
            for c in range(3):
                lam_refs[b][c] = lam[c][0:28]
    if section > 0:
        (send_quarters if section == 1 else send)(x_ref, near_by, slots)
    else:
        group = lax.shift_right_logical(lax.axis_index("dom"), 5)
        total = jnp.zeros((4, 128), F32)
        for g in range(STRIDE):
            dx = jnp.bitwise_and(g // 4 - lax.shift_right_logical(group, 2), 3)
            dy = jnp.bitwise_and(g % 4 - jnp.bitwise_and(group, 3), 3)
            device = jnp.int32(0)
            for x in range(4):
                for y in range(4):
                    device = jnp.where((dx == x) & (dy == y), spread_place(x, y), device)
            total = total + y_ref[device]
        drag_ref[0] = jnp.sum(jnp.where(lane[0:4] == 127, total, 0.0))
    return partial


def round3_kernel(*refs):
    refs = list(refs)
    take = lambda n: [refs.pop(0) for _ in range(n)]
    tables, parts, (state_ref, y_ref), sends = take(6), take(2), take(2), take(2)
    my_near, my_far = take(2)
    lams, (x_ref, normal_ref, sum_ref, halo_near, halo_far) = take(2), take(5)
    base, ahead, motion, past = refs
    links = parts[1][8:11, :].astype(jnp.int32)
    halo_near[...], halo_far[...] = near_match(links), far_match(links)
    near_kernel(
        3, 2, *tables, *parts, *parts, my_near, halo_near, state_ref,
        base, ahead, motion, past, sum_ref,
    )
    far_kernel(
        3, 2, y_ref, tables[4], base, motion, *parts, my_far, halo_far, ahead, *sends, past,
        *lams, x_ref, normal_ref,
    )


def round2_kernel(*refs):
    refs = list(refs)
    take = lambda n: [refs.pop(0) for _ in range(n)]
    tables, lams, parts, (old_ref, state_ref, y_ref) = take(6), take(2), take(2), take(3)
    (normal_ref,), sends, near_matches, far_matches = take(1), take(2), take(2), take(2)
    x_ref, base_ref, ahead_ref, motion_ref, sum_ref = take(5)
    base, ahead, motion, lam, halo_lam, sums = refs
    near_kernel(
        2, 2, *tables, *lams, *parts, *near_matches, old_ref, base, ahead, motion, sums
    )
    partial = far_kernel(
        2, 2, y_ref, tables[4], base, motion, *parts, *far_matches, normal_ref, ahead, *sends,
        lam, halo_lam, x_ref,
    )
    near_kernel(
        1, 2, *tables, lam, halo_lam, *parts, *near_matches, sums,
        base_ref, ahead_ref, motion_ref, sum_ref,
    )
    flow = state_ref[0, 1] * base_ref[0, 1, 0:28, :] + state_ref[0, 2] * base_ref[0, 2, 0:28, :]
    flow = jnp.concatenate([flow * (HALF / state_ref[0, 0]), jnp.zeros((4, E), F32)], axis=0)
    flow = flow[0:8] + flow[8:16] + flow[16:24] + flow[24:32]
    total = sum_ref[4, 24:32, :] - HALF * partial + flow
    put_value(x_ref, -jnp.sum(total, axis=1, keepdims=True))


def put_value(x_ref, value):
    lane = lax.broadcasted_iota(jnp.int32, (8, 128), 1)
    for e in range(GROUP):
        part = x_ref[8 * e : 8 * e + 8, :]
        x_ref[8 * e : 8 * e + 8, :] = jnp.where(lane == 127, value, part)


def fold_kernel(y_ref, out_ref):
    total = y_ref[0:8, :]
    for e in range(1, GROUP):
        total = total + y_ref[8 * e : 8 * e + 8, :]
    out_ref[...] = jnp.broadcast_to(total[:, 127:128], (8, 128))


def insert_kernel(x_ref, value_ref, out_ref):
    lane = lax.broadcasted_iota(jnp.int32, (4, 128), 1)
    value = value_ref[0:4, :] + value_ref[4:8, :]
    for e in range(GROUP):
        out_ref[e] = jnp.where(lane == 127, value, x_ref[e])


def call(kernel, outs, args, values=0, scratch=(), smem=()):
    vmem, scalar = pl.BlockSpec(memory_space=pltpu.VMEM), pl.BlockSpec(memory_space=pltpu.SMEM)
    return pl.pallas_call(
        kernel,
        in_specs=[scalar if i in smem else vmem for i in range(len(args))],
        out_specs=[vmem] * (len(outs) - values) + [scalar] * values,
        out_shape=[jax.ShapeDtypeStruct(shape, dtype) for shape, dtype in outs],
        scratch_shapes=[pltpu.VMEM(shape, dtype) for shape, dtype in scratch],
        compiler_params=pltpu.CompilerParams(vmem_limit_bytes=32 * 1024 * 1024),
    )(*args)


def local(
    saved_states,
    adjoint_final,
    bathymetry,
    wind_speed,
    wind_angle,
    drag_rate,
    metrics,
    face_link,
    face_tag,
    send_faces,
):
    devices = lax.axis_size("dom")
    groups = [list(range(g, g + GROUP)) for g in range(0, devices, GROUP)]
    back3, flip3, grad3, take2, spread3 = constants()
    tables = [back3, flip3, grad3, take2, spread3]

    mixed, x_out = ((3, 32, E), F32), ((GROUP * 8, 128), F32)
    sends_out, sums_out = ((128, 384), BF16), ((5, 32, E), F32)
    pairs = [(i, i) for i in range(ROW)] + [(i, i) for i in range(devices - ROW, devices)]
    for row in range(1, devices // ROW - 1, 2):
        for i in range(row * ROW, row * ROW + ROW):
            pairs += [(i, i + ROW), (i + ROW, i)]
    pack_args = (saved_states, adjoint_final, bathymetry)
    pack_args += (metrics, face_tag, face_link, send_faces)
    mine = call(pack_kernel, [((PACKED, E), F32)], pack_args)[0]
    halo = lax.ppermute(mine, "dom", pairs)
    both = [mine, halo]

    near_out, far_out = ((3 * E, 3 * E), BF16), ((128, 3 * E), BF16)
    my_sends, boxes, rate, my_near, my_far, my_last = call(
        own_first_kernel,
        [sends_out, ((64, 128), F32), ((8, E), F32), near_out, far_out, far_out],
        [mine, flip3, drag_rate] + tables,
        smem=(2,),
    )
    tables.append(rate)
    x, halo_sends = call(halo_first_kernel, [x_out, sends_out], (halo, flip3, boxes))
    def exchange(x):
        return lax.all_to_all(x, "dom", 0, 0, tiled=True, axis_index_groups=groups)

    bases, faces = ((2, 3, 32, E), F32), ((2, 3, 24, E), F32)
    far_outs, near_outs = [mixed, mixed, x_out], [bases, faces, faces, sums_out]
    sends = [my_sends, halo_sends]

    y = exchange(x)
    lam3, _, x, normals, sums, halo_near, halo_far = got = call(
        round3_kernel,
        far_outs + [((2, 3, 8, E), F32), sums_out, near_out, far_out],
        tables + both + [saved_states, y] + sends + [my_near, my_far],
        scratch=[bases, faces, faces, ((4, 24, E), F32)],
    )
    y = exchange(x)
    x, base, ahead, motion, sums = call(
        round2_kernel,
        [x_out] + near_outs,
        tables + list(got[0:2]) + both + [sums, saved_states, y, normals] + sends
        + [my_near, halo_near, my_far, halo_far],
        scratch=[bases, faces, faces, mixed, mixed, sums_out],
    )
    y = exchange(x)
    within = call(fold_kernel, [((8, 128), F32)], (y,))[0]
    within = lax.ppermute(within, "dom", spread_pairs(devices))
    last_out = ((GROUP, 4, 128), F32)
    lam1, _, x = call(
        lambda *refs: (far_kernel(1, 2, *refs), None)[1],
        [mixed, mixed, last_out],
        [y, spread3, base, motion] + both + [my_far, halo_far, normals, ahead],
    )
    args = tables + [lam1, mine, my_near, sums, saved_states, lam3, wind_speed, wind_angle]
    base, motion, depth_gradient, speed_gradient, angle_gradient = call(
        lambda *refs: near_kernel(0, 1, *refs),
        [((1, 3, 32, E), F32), ((1, 3, 24, E), F32)] + [((28, E), F32)] * 3,
        args,
    )
    x, base = lax.optimization_barrier((x, base))
    y = exchange(call(insert_kernel, [last_out], (x, within))[0])
    initial, drag_gradient = call(
        lambda *refs: (far_kernel(0, 1, *refs), None)[1],
        [((3, 28, E), F32), ((1,), F32)],
        [y, spread3, base, motion, mine, my_last, normals],
        values=1,
    )
    return (initial, depth_gradient, speed_gradient, angle_gradient, drag_gradient)


def solution(mesh):
    return jax.shard_map(
        local,
        mesh=mesh,
        in_specs=(
            P(None, None, None, "dom"),
            P(None, None, "dom"),
            P(None, "dom"),
            P(None, "dom"),
            P(None, "dom"),
            P(),
            P(None, "dom"),
            P(None, "dom"),
            P(None, "dom"),
            P(None, "dom"),
        ),
        out_specs=(P(None, None, "dom"), P(None, "dom"), P(None, "dom"), P(None, "dom"), P()),
        check_vma=False,
    )
```

```python
import math

import jax
import jax.numpy as jnp
import ml_dtypes
import numpy as np
from jax import lax
from jax.experimental import pallas as pl
from jax.experimental.pallas import tpu as pltpu
from jax.sharding import PartitionSpec as P

GRAVITY = 1.0
PENALTY = 3.0
WIND_COEF = 5.0
TIME_STEP = 0.01
HALF = 0.5 * TIME_STEP
SIXTH = TIME_STEP / 6.0

GROUP = 32
STRIDE = 16
ROW = 16
REACH = 4
DIRS = 8
SLOTS = 16
E = 128
DEPTH, MISC = 12, 24
PACKED = MISC + 28 * 13 + 4
F32 = jnp.float32
BF16 = jnp.bfloat16


def solve_dense(matrix, right):
    system = np.array(matrix) + 0.0
    result = np.array(right) + 0.0
    extent = system.shape[0]
    for column in range(extent):
        pivot_index = column + int(np.argmax(np.abs(system[column:, column])))
        system[[column, pivot_index]] = system[[pivot_index, column]]
        result[[column, pivot_index]] = result[[pivot_index, column]]
        for target in range(column + 1, extent):
            factor = system[target, column] / system[column, column]
            system[target] = system[target] - factor * system[column]
            result[target] = result[target] - factor * result[column]
    solution = np.zeros(result.shape)
    for column in range(extent - 1, -1, -1):
        solution[column] = (
            result[column] - system[column, column + 1 :] @ solution[column + 1 :]
        ) / system[column, column]
    return solution


def element_tables():
    degree = 6
    nodes = [
        (column, row_index)
        for row_index in range(degree + 1)
        for column in range(degree + 1 - row_index)
    ]
    node_total = len(nodes)
    coord_x = np.array([node[0] / degree for node in nodes])
    coord_y = np.array([node[1] / degree for node in nodes])
    vander = np.zeros((node_total, node_total))
    vander_r = np.zeros((node_total, node_total))
    vander_s = np.zeros((node_total, node_total))
    grams = np.zeros((node_total, node_total))
    for column_index, power in enumerate(nodes):
        first, second = power
        vander[:, column_index] = coord_x**first * coord_y**second
        if first > 0:
            vander_r[:, column_index] = 0.5 * first * coord_x ** (first - 1) * coord_y**second
        if second > 0:
            vander_s[:, column_index] = 0.5 * second * coord_x**first * coord_y ** (second - 1)
        for other_index, other_power in enumerate(nodes):
            sum_x = first + other_power[0]
            sum_y = second + other_power[1]
            grams[column_index, other_index] = (
                4.0
                * math.factorial(sum_x)
                * math.factorial(sum_y)
                / math.factorial(sum_x + sum_y + 2)
            )
    deriv_r = solve_dense(vander.T, vander_r.T).T
    deriv_s = solve_dense(vander.T, vander_s.T).T
    mass_inverse = vander @ solve_dense(grams, vander.T)
    points = np.arange(degree + 1) / degree
    line_vander = np.stack([points**power for power in range(degree + 1)], axis=1)
    line_grams = np.array(
        [
            [2.0 / (first + second + 1) for second in range(degree + 1)]
            for first in range(degree + 1)
        ]
    )
    line_inverse = solve_dense(line_vander, np.eye(degree + 1))
    line_mass = line_inverse.T @ line_grams @ line_inverse
    lookup = {node: number for number, node in enumerate(nodes)}
    face_nodes = [
        [lookup[step, 0] for step in range(degree + 1)],
        [lookup[degree - step, step] for step in range(degree + 1)],
        [lookup[0, degree - step] for step in range(degree + 1)],
    ]
    embed = np.zeros((node_total, 3 * (degree + 1)))
    extract = np.zeros((3 * (degree + 1), node_total))
    for face_index in range(3):
        for step in range(degree + 1):
            extract[face_index * (degree + 1) + step, face_nodes[face_index][step]] = 1.0
            for other_step in range(degree + 1):
                embed[
                    face_nodes[face_index][other_step], face_index * (degree + 1) + step
                ] += line_mass[other_step, step]
    lifting = mass_inverse @ embed
    return deriv_r, deriv_s, lifting, extract


def offset_of(direction):
    return direction + 1 if direction < REACH else REACH - direction - 1


def neighbours():
    me = jnp.bitwise_and(lax.axis_index("dom"), GROUP - 1)
    found = []
    for own in (me + ROW, jnp.where(me < ROW, me, me + 2 * ROW)):
        for j in range(DIRS):
            place = own + offset_of(j)
            inner = (place >= ROW) & (place < ROW + GROUP)
            exists = (place >= 0) & (place < 4 * ROW)
            device = jnp.where(inner, place - ROW, jnp.where(place < ROW, place, place - 2 * ROW))
            found.append((jnp.where(exists, device, 0), jnp.where(inner, 0, 1), exists))
    return found


def spread_place(dx, dy):
    half, odd = dx // 2, dx % 2
    if dy == 0:
        return 6 + half + ROW * odd
    if dy == 2:
        return 4 + half + ROW * (1 - odd)
    return dx + (ROW if dy == 1 else 0)


def spread_pairs(devices):
    pairs = []
    for group in range(devices // GROUP):
        for dx in range(4):
            for dy in range(4):
                other = (group // 4 + dx) % 4 * 4 + (group % 4 + dy) % 4
                place = spread_place(dx, dy)
                source = place if dy == 0 else (place + ROW) % GROUP
                pairs.append((other * GROUP + source, group * GROUP + place))
    return pairs


def parts3(matrix, width):
    padded = np.zeros((matrix.shape[0], width))
    padded[:, : matrix.shape[1]] = matrix
    hi = padded.astype(np.float32).astype(ml_dtypes.bfloat16)
    lo = (padded - hi.astype(np.float64)).astype(ml_dtypes.bfloat16)
    return np.concatenate([hi, lo, hi], axis=1)


def constants():
    deriv_r, deriv_s, lifting, extract = element_tables()

    def pad_rows(matrix):
        return np.concatenate([matrix, np.zeros((4, matrix.shape[1]))])

    lift = np.zeros((24, 28))
    flip = np.zeros((24, 28))
    take = np.zeros((24, 28))
    give = np.zeros((24, 28))
    for face in range(3):
        for k in range(7):
            lift[8 * face + k] = lifting[:, 7 * face + k]
            flip[8 * face + k] = lifting[:, 7 * face + 6 - k]
            take[8 * face + k] = extract[7 * face + k]
            give[8 * face + k] = extract[7 * face + k]
        take[8 * face + 7] = extract[7 * face + 6]
    back = np.concatenate([pad_rows(deriv_r.T), pad_rows(deriv_s.T), lift, flip])
    back3 = parts3(back, 32)
    flip3 = parts3(flip, 32)
    grad3 = parts3(np.concatenate([pad_rows(deriv_r), pad_rows(deriv_s)]), 32)
    take2 = np.zeros((24, 64))
    take2[:, 0:28] = take
    take2[:, 32:60] = take
    spread = np.concatenate([pad_rows(give.T), flip @ give.T])
    spread3 = parts3(spread, 24)
    spread3 = np.concatenate([spread3, np.zeros((56, 8), ml_dtypes.bfloat16)], axis=1)
    as_bf16 = lambda m: jnp.asarray(np.asarray(m).astype(ml_dtypes.bfloat16))
    return as_bf16(back3), as_bf16(flip3), as_bf16(grad3), as_bf16(take2), as_bf16(spread3)


def dot(a, b):
    return jnp.dot(a, b, preferred_element_type=F32)


def dot_nt(a, b):
    return lax.dot_general(a, b, (((1,), (1,)), ((), ())), preferred_element_type=F32)


def halves(x):
    hi = x.astype(BF16).astype(F32)
    return hi, x - hi


def times3(matrix3, x):
    hi = x.astype(BF16)
    lo = (x - hi.astype(F32)).astype(BF16)
    return dot(matrix3, jnp.concatenate([hi, hi, lo], axis=0))


def spread_faces(spread3, faces):
    hi, lo = halves(faces)
    stack = jnp.concatenate([hi, hi, lo, jnp.zeros((8, faces.shape[1]), F32)], axis=0)
    return dot(spread3, stack.astype(BF16))


def geometry(misc):
    rx, ry, sx, sy = misc[0:1], misc[1:2], misc[2:3], misc[3:4]
    normals = []
    for nx, ny in ((-sx, -sy), (rx + sx, ry + sy), (-rx, -ry)):
        normals.append((nx, ny, jnp.sqrt(nx * nx + ny * ny)))
    return (rx, ry, sx, sy), normals


def jump_back(n, t, u, v, gh):
    nx, ny, size = n
    un = nx * u + ny * v
    mixed = u * t[1] + v * t[2]
    pull = 0.5 * PENALTY * size
    return (
        0.5 * (gh * (nx * t[1] + ny * t[2]) - un * mixed) - pull * t[0],
        0.5 * (nx * (t[0] + mixed) + un * t[1]) - pull * t[1],
        0.5 * (ny * (t[0] + mixed) + un * t[2]) - pull * t[2],
    )


def traces(flipped, normals):
    last = lax.broadcasted_iota(jnp.int32, (8, E), 0) == 7
    rows = []
    for c in range(3):
        rows.append(
            jnp.concatenate(
                [jnp.where(last, normals[f][c], flipped[c][f]) for f in range(3)], axis=1
            )
        )
    return jnp.concatenate(rows, axis=0)


def far_index(link, width=8):
    v = link - 3 * E
    j = lax.shift_right_arithmetic(v, 4)
    c = jnp.bitwise_and(v, 15)
    part = lax.shift_right_arithmetic(c, width.bit_length() - 1)
    row = part * (DIRS * width) + j * width + jnp.bitwise_and(c, width - 1)
    return jnp.where(v >= 0, row, -1)


def slot_rows(sends, v, block):
    first = 64 * block
    n = v.shape[1]
    hi, lo = halves(v)
    rows = [jnp.zeros((first, n), F32)] if block else []
    rest = [jnp.zeros((32 - v.shape[0], n), F32)] if v.shape[0] < 32 else []
    rows += [hi] + rest + [lo] + rest + [jnp.zeros((64 - first, n), F32)] * (1 - block)
    out = dot_nt(sends, jnp.concatenate(rows, axis=0).astype(BF16))
    lane = lax.broadcasted_iota(jnp.int32, (128, 128), 1)
    out = jnp.where((lane >= first) & (lane < first + 32), out + pltpu.roll(out, 96, 1), 0.0)
    return out[0:64] + pltpu.roll(out[64:128], 32, 1)


def quarter_rows(sends, v):
    hi, lo = halves(v)
    rest = jnp.zeros((8, v.shape[1]), F32)
    stack = jnp.concatenate([hi, rest, lo, rest, jnp.zeros((64, v.shape[1]), F32)], axis=0)
    out = dot_nt(sends, stack.astype(BF16))
    lane = lax.broadcasted_iota(jnp.int32, (128, 128), 1)
    out = jnp.where(lane < 32, out + pltpu.roll(out, 96, 1), 0.0)
    total = out[0:32]
    for h in range(1, 4):
        total = total + pltpu.roll(out[32 * h : 32 * h + 32], 32 * h, 1)
    return total


def send_quarters(x_ref, near_by, boxes):
    x_ref[...] = jnp.zeros(x_ref.shape, F32)
    for b in range(2):
        for j in range(DIRS):
            device, second, exists = near_by[DIRS * b + j]
            box = jnp.where(exists & (second == 0), boxes[b][4 * j : 4 * j + 4], 0.0)
            x_ref[device] = x_ref[device] + box


def send(x_ref, near_by, boxes):
    x_ref[...] = jnp.zeros(x_ref.shape, F32)
    for b in range(2):
        for j in range(DIRS):
            device, _, exists = near_by[DIRS * b + j]
            rows = pl.ds(pl.multiple_of(device * 8, 8), 8)
            box = jnp.where(exists, boxes[b][8 * j : 8 * j + 8], 0.0)
            x_ref[rows, :] = x_ref[rows, :] + box


def send_matrix(misc, width=8):
    faces = misc[16:24]
    lane = lax.broadcasted_iota(jnp.int32, (8, 128), 1)
    both = jnp.zeros((8, 128), F32)
    for h in range(SLOTS // width):
        part = jnp.where((lane >= width * h) & (lane < width * h + width), faces, 0.0)
        both = both + (pltpu.roll(part, (DIRS - 1) * width * h, 1) if h else part)
    row = lax.broadcasted_iota(jnp.int32, (8, 128), 0)
    lined = jnp.zeros((8, 128), F32)
    for j in range(DIRS):
        moved = both if j == 0 else pltpu.roll(both, width * j, 1)
        lined = lined + jnp.where(row == j, moved, 0.0)
    line = jnp.sum(lined, axis=0, keepdims=True)
    column = jnp.transpose(jnp.broadcast_to(line, (128, 128)))
    face = lax.broadcasted_iota(jnp.int32, (128, 128), 1).astype(F32)
    pieces = [jnp.where(column == face + float(128 * f), 1.0, 0.0) for f in range(3)]
    return jnp.concatenate(pieces, axis=1).astype(BF16)


def pack_kernel(q_ref, lam_ref, depth_ref, metric_ref, tag_ref, link_ref, face_ref, out_ref):
    out_ref[0:MISC, :] = jnp.zeros((MISC, E), F32)
    out_ref[0:4, :] = metric_ref[...]
    out_ref[4:7, :] = tag_ref[...].astype(F32)
    out_ref[8:11, :] = link_ref[...].astype(F32)
    out_ref[16:24, 0:16] = face_ref[...].astype(F32)
    for c in range(3):
        out_ref[MISC + 28 * c : MISC + 28 * c + 28, :] = lam_ref[c]
    for s in range(3):
        for c in range(3):
            first = MISC + 28 * (3 * (3 - s) + c)
            out_ref[first : first + 28, :] = q_ref[s + 1, c]
    out_ref[MISC + 28 * DEPTH : MISC + 28 * DEPTH + 28, :] = depth_ref[...]
    out_ref[PACKED - 4 : PACKED, :] = jnp.zeros((4, E), F32)


def field(part_ref, i, fill):
    first = MISC + 28 * i
    row = lax.broadcasted_iota(jnp.int32, (32, E), 0)
    return jnp.where(row < 28, part_ref[first : first + 32, :], fill)


def first_boxes(part_ref, flip3, block):
    misc = part_ref[0:MISC, :]
    weights = jnp.concatenate([HALF * field(part_ref, c, 0.0) for c in range(3)], axis=1)
    flipped = times3(flip3[...], weights)
    split = [
        [flipped[8 * f : 8 * f + 8, 128 * c : 128 * c + 128] for f in range(3)] for c in range(3)
    ]
    sends = send_matrix(misc)
    return sends, slot_rows(sends, traces(split, geometry(misc)[1]), block)


def own_first_kernel(part_ref, flip3, drag_ref, *refs):
    tables, state_ref = refs[0:5], refs[5]
    sends_ref, boxes_ref, rate_ref, near_ref, far_ref, last_ref = refs[6:12]
    links = part_ref[8:11, :].astype(jnp.int32)
    near_ref[...], far_ref[...] = near_match(links), far_match(links)
    last_ref[...] = far_match(links, 4)
    rate_ref[...] = jnp.full((8, E), drag_ref[0], F32)
    near_kernel(3, 1, *tables, rate_ref, part_ref, part_ref, near_ref, state_ref, *refs[12:])
    sends_ref[...], boxes_ref[...] = first_boxes(part_ref, flip3, 0)


def halo_first_kernel(part_ref, flip3, boxes_ref, x_ref, sends_ref):
    sends_ref[...], boxes = first_boxes(part_ref, flip3, 1)
    send(x_ref, neighbours(), [boxes_ref[...], boxes])


def near_match(links):
    rows = lax.broadcasted_iota(jnp.int32, (3 * E, E), 0)
    return jnp.concatenate(
        [jnp.where(rows == links[f : f + 1], 1.0, 0.0).astype(BF16) for f in range(3)], axis=1
    )


def far_match(links, width=8):
    rows = lax.broadcasted_iota(jnp.int32, (128, E), 0)
    found = [rows == far_index(links[f : f + 1], width) for f in range(3)]
    return jnp.concatenate([jnp.where(x, 1.0, 0.0).astype(BF16) for x in found], axis=1)


def near_kernel(section, blocks, *refs, light=False):
    refs = list(refs)
    back3, flip3, grad3, take2, spread3 = [refs.pop(0)[...] for _ in range(5)]
    rate_ref = refs.pop(0)
    lams = [refs.pop(0) for _ in range(blocks)]
    parts = [refs.pop(0) for _ in range(blocks)]
    matches = [refs.pop(0) for _ in range(blocks)]
    old_ref = refs.pop(0) if section < 3 else None
    if section == 3 and not light:
        state_ref = refs.pop(0)
    if section == 0:
        state_ref, lam3_ref = refs.pop(0), refs.pop(0)
        speed_ref, angle_ref = refs.pop(0), refs.pop(0)
    base_ref = refs.pop(0)
    if section > 0:
        ahead_ref = refs.pop(0)
    motion_ref = refs.pop(0)
    if section == 3 and not light:
        past_ref = refs.pop(0)
    if light:
        pass
    elif section > 0:
        sum_ref = refs.pop(0)
    else:
        depth_out, speed_out, angle_out = refs.pop(0), refs.pop(0), refs.pop(0)
    scale = SIXTH if section == 2 else HALF
    later = SIXTH if section == 3 else HALF
    drag_rate = rate_ref[...][0:1]
    pad = jnp.ones((4, E), F32)

    if section == 3:
        lam = [[field(lams[b], c, 0.0) for c in range(3)] for b in range(blocks)]
    else:
        lam = [[lams[b][c] for c in range(3)] for b in range(blocks)]
    w = [[scale * x for x in lam[b]] for b in range(blocks)]
    if section == 0:
        q = [[jnp.concatenate([state_ref[0, c], pad], axis=0) for c in range(3)]]
    else:
        q = [[field(parts[b], 3 * (4 - section) + c, 1.0) for c in range(3)] for b in range(blocks)]
    z = [field(parts[b], DEPTH, 1.0) for b in range(blocks)]
    pulled = times3(back3, jnp.concatenate([x for b in range(blocks) for x in w[b]], axis=1))
    slopes = times3(grad3, jnp.concatenate(z, axis=1))
    fields = jnp.concatenate([x for b in range(blocks) for x in q[b] + [z[b]]], axis=1)
    hi, lo = halves(fields)
    at_faces = dot(take2, jnp.concatenate([hi, lo], axis=0).astype(BF16))

    if section == 3 and not light:
        fields = [jnp.concatenate([state_ref[0, c], pad], axis=0) for c in range(3)]
        fields += [field(parts[0], 9 + c, 1.0) for c in range(3)]
        hi, lo = halves(jnp.concatenate(fields, axis=1))
        past = dot(take2, jnp.concatenate([hi, lo], axis=0).astype(BF16))
        for i in range(2):
            finv = 1.0 / past[:, 384 * i : 384 * i + 128]
            past_ref[2 * i] = past[:, 384 * i + 128 : 384 * i + 256] * finv
            past_ref[2 * i + 1] = past[:, 384 * i + 256 : 384 * i + 384] * finv

    face_sums, volumes, opens = [], [], []
    for b in range(blocks):
        misc = parts[b][0:MISC, :]
        (rx, ry, sx, sy), normals = geometry(misc)
        part = lambda r0, r1, c: pulled[r0:r1, 384 * b + 128 * c : 384 * b + 128 * c + 128]
        h = q[b][0]
        inv = 1.0 / h
        u, v = q[b][1] * inv, q[b][2] * inv
        gh = GRAVITY * h
        along = [part(0, 32, c) for c in range(3)]
        across = [part(32, 64, c) for c in range(3)]
        fx = [-(rx * along[c] + sx * across[c]) for c in range(3)]
        fy = [-(ry * along[c] + sy * across[c]) for c in range(3)]
        cross = fx[2] + fy[1]
        slope_r = slopes[0:32, 128 * b : 128 * b + 128]
        slope_s = slopes[32:64, 128 * b : 128 * b + 128]
        slope_x = rx * slope_r + sx * slope_s
        slope_y = ry * slope_r + sy * slope_s
        flow = u * w[b][1] + v * w[b][2]
        drag_inv = drag_rate * inv
        volumes.append(
            (
                gh * (fx[1] + fy[2])
                - u * (u * fx[1] + v * cross)
                - v * v * fy[2]
                + GRAVITY * (slope_x * w[b][1] + slope_y * w[b][2])
                + drag_inv * flow,
                fx[0] + 2.0 * u * fx[1] + v * cross - drag_inv * w[b][1],
                fy[0] + u * cross + 2.0 * v * fy[2] - drag_inv * w[b][2],
            )
        )
        own = [[part(64 + 8 * f, 72 + 8 * f, c) for f in range(3)] for c in range(3)]
        flipped = [[part(88 + 8 * f, 96 + 8 * f, c) for f in range(3)] for c in range(3)]
        hi, lo = halves(traces(flipped, normals))
        pool = jnp.concatenate([hi, lo], axis=0).astype(BF16)
        found = dot(pool, matches[b][...])
        found = found[0:24] + found[24:48]
        opened = []
        sums = [[], [], []]
        for f in range(3):
            got = found[:, 128 * f : 128 * f + 128]
            value = lambda i: at_faces[
                8 * f : 8 * f + 8, 512 * b + 128 * i : 512 * b + 128 * i + 128
            ]
            fh, fm, fn, fz = value(0), value(1), value(2), value(3)
            finv = 1.0 / fh
            fu, fv, fgh = fm * finv, fn * finv, GRAVITY * fh
            motion_ref[b, 0, 8 * f : 8 * f + 8, :] = fu
            motion_ref[b, 1, 8 * f : 8 * f + 8, :] = fv
            motion_ref[b, 2, 8 * f : 8 * f + 8, :] = fgh
            tag = misc[4 + f : 5 + f]
            linked, wall, free = tag == 0.0, tag == 1.0, tag == 2.0
            nx, ny, size = normals[f]
            t = [own[c][f] for c in range(3)]
            mine = jump_back(normals[f], t, fu, fv, fgh)
            inv_size = 1.0 / size
            ux, uy = nx * inv_size, ny * inv_size
            twice = 2.0 * (ux * t[1] + uy * t[2])
            mirrored = (t[0], t[1] - twice * ux, t[2] - twice * uy)
            near = (got[0:8], got[8:16], got[16:24])
            other_n = tuple(
                jnp.where(linked, near[c][7:8], jnp.where(wall, m, 0.0))
                for c, m in enumerate((-nx, -ny, size))
            )
            other_t = [
                jnp.where(linked, near[c], jnp.where(wall, mirrored[c], 0.0)) for c in range(3)
            ]
            theirs = jump_back(other_n, other_t, fu, fv, fgh)
            zinv = 1.0 / fz
            out = jump_back(normals[f], t, fm * zinv, fn * zinv, GRAVITY * fz)
            opened.append(jnp.where(free, -out[0], 0.0))
            sums[0].append(mine[0] - theirs[0])
            sums[1].append(mine[1] - theirs[1] - jnp.where(free, out[1], 0.0))
            sums[2].append(mine[2] - theirs[2] - jnp.where(free, out[2], 0.0))
        face_sums.append([jnp.concatenate(sums[c], axis=0) for c in range(3)])
        if b == 0:
            opens = jnp.concatenate(opened, axis=0)
            height, moved = h, flow
    to_nodes = [x for b in range(blocks) for x in face_sums[b]]
    if section == 0:
        old = [old_ref[i] for i in range(5)]
        opens = opens + old[4][0:24]
        to_nodes.append(opens)
    nodes = spread_faces(spread3, jnp.concatenate(to_nodes, axis=1))
    for b in range(blocks):
        bases = []
        for c in range(3):
            first = lam[b][c]
            if section == 2:
                first = first * (1.0 / 3.0)
            if section == 0:
                first = first + (2.0 / 3.0) * lam3_ref[c]
            where = 384 * b + 128 * c
            bases.append(first + volumes[b][c] + nodes[0:32, where : where + 128])
            base_ref[b, c] = bases[c]
        if section > 0:
            ahead = times3(flip3, later * jnp.concatenate(bases, axis=1))
            for c in range(3):
                ahead_ref[b, c] = ahead[:, 128 * c : 128 * c + 128]
    if light:
        return
    w1, w2 = w[0][1], w[0][2]
    g1, g2 = height * w1, height * w2
    if section == 3:
        fold = moved[0:8] + moved[8:16] + moved[16:24] + moved[24:32]
        news = [w1, w2, g1, g2]
    else:
        if section > 0:
            old = [old_ref[i] for i in range(5)]
            opens = opens + old[4][0:24]
            fold = old[4][24:32] + (moved[0:8] + moved[8:16] + moved[16:24] + moved[24:32])
        news = [x + y for x, y in zip(old[0:4], (w1, w2, g1, g2))]
    if section > 0:
        for i in range(4):
            sum_ref[i] = news[i]
        sum_ref[4, 0:24, :] = opens
        sum_ref[4, 24:32, :] = fold
    else:
        rx, ry, sx, sy = geometry(parts[0][0:4, :])[0]
        w1, w2, g1, g2 = news
        pair = GRAVITY * jnp.concatenate([rx * g1 + ry * g2, sx * g1 + sy * g2], axis=1)
        pulled = times3(back3, pair)
        depth = pulled[0:32, 0:128] + pulled[32:64, 128:256] + nodes[0:32, 384:512]
        depth_out[...] = depth[0:28]
        speed, angle = speed_ref[...], angle_ref[...]
        cosine, sine = jnp.cos(angle), jnp.sin(angle)
        w1, w2 = w1[0:28], w2[0:28]
        speed_out[...] = (2.0 * WIND_COEF) * speed * (cosine * w1 + sine * w2)
        angle_out[...] = WIND_COEF * speed * speed * (cosine * w2 - sine * w1)


def far_kernel(section, blocks, *refs):
    refs = list(refs)
    y_ref, spread3_ref, base_ref, motion_ref = [refs.pop(0) for _ in range(4)]
    parts = [refs.pop(0) for _ in range(blocks)]
    matches = [refs.pop(0) for _ in range(blocks)]
    if section < 3:
        normal_ref = refs.pop(0)
    if section > 0:
        ahead_ref = refs.pop(0)
    if section > 1:
        sends_refs = [refs.pop(0), refs.pop(0)]
    if section == 3:
        past_ref = refs.pop(0)
    lam_refs = [refs.pop(0) for _ in range(blocks)]
    if section > 0:
        x_ref = refs.pop(0)
    if section == 3:
        normal_ref = refs.pop(0)
    if section == 0:
        drag_ref = refs.pop(0)
    later = SIXTH if section == 3 else HALF

    lane = lax.broadcasted_iota(jnp.int32, (8, 128), 1)
    place_in = jnp.bitwise_and(lane, 31)
    spare = (place_in >= 24) | (place_in == 7) | (place_in == 15) | (place_in == 23)
    near_by = neighbours()
    boxes, extras = [], []
    for b in range(2):
        for j in range(DIRS):
            if b < blocks:
                device, second, exists = near_by[DIRS * b + j]
                if section == 0:
                    boxes.append(jnp.where(exists, y_ref[device], 0.0))
                    continue
                raw = y_ref[pl.ds(pl.multiple_of(device * 8, 8), 8), :]
                turned = pltpu.roll(raw, 64, 1)
                if section == 2:
                    box = jnp.where(second == 1, jnp.where(spare, 0.0, turned), raw)
                    extras.append(jnp.where(exists & (second == 0), turned, 0.0))
                else:
                    box = jnp.where(second == 1, turned, raw)
                boxes.append(jnp.where(exists, box, 0.0))
            elif section > 0:
                boxes.append(jnp.zeros((8, 128), F32))
    if section == 0:
        boxes.append(jnp.zeros((96, 128), F32))
    stacks = [jnp.transpose(jnp.concatenate(boxes, axis=0))]
    if section == 2:
        stacks.append(jnp.transpose(jnp.concatenate(extras, axis=0)))
    left = lax.broadcasted_iota(jnp.int32, (32, 128), 1) < 64
    row = lax.broadcasted_iota(jnp.int32, (8, E), 0)
    face_sums, factors = [], []
    for b in range(blocks):
        pools = []
        for turned in stacks:
            low, high = turned[0:32], turned[32:64]
            if section == 0:
                pool = low
                for h in range(1, 4):
                    pool = pool + pltpu.roll(turned[32 * h : 32 * h + 32], 32 * h, 1)
                pools.append(pool)
            elif b == 0:
                pools.append(jnp.where(left, low, pltpu.roll(high, 64, 1)))
            else:
                pools.append(jnp.where(left, pltpu.roll(low, 64, 1), high))
        pool = jnp.concatenate(pools, axis=0)
        tall = pool.shape[0]
        pool = jnp.concatenate(halves(pool), axis=0).astype(BF16)
        got = dot(pool, matches[b][...])
        got = got[0:tall] + got[tall:]
        sums, scales = [[], [], []], [[], [], []]
        for f in range(3):
            piece = lambda r: got[r : r + 8, 128 * f : 128 * f + 128]
            far = [piece(8 * c) for c in range(3)]
            if section == 3:
                normal = tuple(x[7:8] for x in far)
                for i in range(3):
                    normal_ref[b, f, i : i + 1, :] = normal[i]
            else:
                normal = tuple(normal_ref[b, f, i : i + 1, :] for i in range(3))
            motion = [motion_ref[b, i, 8 * f : 8 * f + 8, :] for i in range(3)]
            theirs = jump_back(normal, far, *motion)
            for c in range(3):
                sums[c].append(-theirs[c])
            if section == 3 and b == 0:
                u0, v0, u1, v1 = [past_ref[i, 8 * f : 8 * f + 8, :] for i in range(4)]
                nx, ny, size = normal
                mean = 0.5 * (nx * u0 + ny * v0)
                rate = 0.5 * (nx * u1 + ny * v1) - 0.5 * PENALTY * size
                factors.append((mean, mean * u1 + u0 * rate, mean * v1 + v0 * rate))
            if section == 2:
                singles = (piece(24)[7:8], piece(56)[7:8], far[0][7:8], far[1][7:8], far[2][7:8])
                singles += (piece(32)[7:8], piece(40)[7:8])
                third = jnp.zeros((8, E), F32)
                for k in range(7):
                    third = jnp.where(row == k, singles[k], third)
                factors.append((piece(24), piece(56), third))
        face_sums += [jnp.concatenate(sums[c], axis=0) for c in range(3)]
    spread = spread_faces(spread3_ref[...], jnp.concatenate(face_sums, axis=1))
    slots = []
    partial = jnp.zeros((8, E), F32)
    for b in range(blocks):
        lam = []
        for c in range(3):
            where = 384 * b + 128 * c
            lam.append(base_ref[b, c] + spread[0:32, where : where + 128])
        if section > 0:
            for c in range(3):
                lam_refs[b][c] = lam[c]
            flipped = [
                ahead_ref[b, c]
                + later * spread[32:56, 384 * b + 128 * c : 384 * b + 128 * c + 128]
                for c in range(3)
            ]
            split = [[flipped[c][8 * f : 8 * f + 8] for f in range(3)] for c in range(3)]
            none = jnp.zeros((1, E), F32)
            lasts = [(none,) * 3] * 3
            if section == 3 and b == 0:
                lasts = [tuple(factors[f][2][k : k + 1] for k in (2, 3, 4)) for f in range(3)]
            trace = traces(split, lasts)
            if section == 3 and b == 0:
                last = row == 7
                third = lambda f, k: factors[f][2][k : k + 1]
                one = [jnp.where(last, third(f, 0), factors[f][0]) for f in range(3)]
                two = [jnp.where(last, third(f, 1), factors[f][1]) for f in range(3)]
                five = [jnp.where(last, third(f, 5), 0.0) for f in range(3)]
                six = [jnp.where(last, third(f, 6), 0.0) for f in range(3)]
                line = lambda parts: jnp.concatenate(parts, axis=1)
                trace = jnp.concatenate([trace, line(one)], axis=0)
                extra = [line(five), line(six), jnp.zeros((8, 3 * E), F32), line(two)]
                slots.append(
                    slot_rows(sends_refs[0][...], trace, 0)
                    + slot_rows(sends_refs[0][...], jnp.concatenate(extra, axis=0), 1)
                )
            elif section == 1:
                slots.append(quarter_rows(send_matrix(parts[b][0:MISC, :], 4), trace))
            else:
                slots.append(slot_rows(sends_refs[b][...], trace, b))
            if section == 2:
                for f in range(3):
                    for c in range(3):
                        partial = partial + split[c][f] * factors[3 * b + f][c]
        else:
            for c in range(3):
                lam_refs[b][c] = lam[c][0:28]
    if section > 0:
        (send_quarters if section == 1 else send)(x_ref, near_by, slots)
    else:
        group = lax.shift_right_logical(lax.axis_index("dom"), 5)
        total = jnp.zeros((4, 128), F32)
        for g in range(STRIDE):
            dx = jnp.bitwise_and(g // 4 - lax.shift_right_logical(group, 2), 3)
            dy = jnp.bitwise_and(g % 4 - jnp.bitwise_and(group, 3), 3)
            device = jnp.int32(0)
            for x in range(4):
                for y in range(4):
                    device = jnp.where((dx == x) & (dy == y), spread_place(x, y), device)
            total = total + y_ref[device]
        drag_ref[0] = jnp.sum(jnp.where(lane[0:4] == 127, total, 0.0))
    return partial


def round3_kernel(*refs):
    refs = list(refs)
    take = lambda n: [refs.pop(0) for _ in range(n)]
    tables, parts, (y_ref,), sends = take(6), take(2), take(1), take(2)
    (my_far,), done, (past,) = take(1), take(3), take(1)
    lams, (x_ref, normal_ref, halo_near, halo_far) = take(2), take(4)
    base, ahead, motion, *theirs = refs
    links = parts[1][8:11, :].astype(jnp.int32)
    halo_near[...], halo_far[...] = near_match(links), far_match(links)
    near_kernel(3, 1, *tables, parts[1], parts[1], halo_near, *theirs, light=True)
    for both, ours, other in zip((base, ahead, motion), done, theirs):
        both[0] = ours[0]
        both[1] = other[0]
    far_kernel(
        3, 2, y_ref, tables[4], base, motion, *parts, my_far, halo_far, ahead, *sends, past,
        *lams, x_ref, normal_ref,
    )


def round2_kernel(*refs):
    refs = list(refs)
    take = lambda n: [refs.pop(0) for _ in range(n)]
    tables, lams, parts, (old_ref, state_ref, y_ref) = take(6), take(2), take(2), take(3)
    (normal_ref,), sends, near_matches, far_matches = take(1), take(2), take(2), take(2)
    x_ref, base_ref, ahead_ref, motion_ref, sum_ref = take(5)
    base, ahead, motion, lam, halo_lam, sums = refs
    near_kernel(
        2, 2, *tables, *lams, *parts, *near_matches, old_ref, base, ahead, motion, sums
    )
    partial = far_kernel(
        2, 2, y_ref, tables[4], base, motion, *parts, *far_matches, normal_ref, ahead, *sends,
        lam, halo_lam, x_ref,
    )
    near_kernel(
        1, 2, *tables, lam, halo_lam, *parts, *near_matches, sums,
        base_ref, ahead_ref, motion_ref, sum_ref,
    )
    flow = state_ref[0, 1] * base_ref[0, 1, 0:28, :] + state_ref[0, 2] * base_ref[0, 2, 0:28, :]
    flow = jnp.concatenate([flow * (HALF / state_ref[0, 0]), jnp.zeros((4, E), F32)], axis=0)
    flow = flow[0:8] + flow[8:16] + flow[16:24] + flow[24:32]
    total = sum_ref[4, 24:32, :] - HALF * partial + flow
    put_value(x_ref, -jnp.sum(total, axis=1, keepdims=True))


def put_value(x_ref, value):
    lane = lax.broadcasted_iota(jnp.int32, (8, 128), 1)
    for e in range(GROUP):
        part = x_ref[8 * e : 8 * e + 8, :]
        x_ref[8 * e : 8 * e + 8, :] = jnp.where(lane == 127, value, part)


def fold_kernel(y_ref, out_ref):
    total = y_ref[0:8, :]
    for e in range(1, GROUP):
        total = total + y_ref[8 * e : 8 * e + 8, :]
    out_ref[...] = jnp.broadcast_to(total[:, 127:128], (8, 128))


def insert_kernel(x_ref, value_ref, out_ref):
    lane = lax.broadcasted_iota(jnp.int32, (4, 128), 1)
    value = value_ref[0:4, :] + value_ref[4:8, :]
    for e in range(GROUP):
        out_ref[e] = jnp.where(lane == 127, value, x_ref[e])


def call(kernel, outs, args, values=0, scratch=(), smem=()):
    vmem, scalar = pl.BlockSpec(memory_space=pltpu.VMEM), pl.BlockSpec(memory_space=pltpu.SMEM)
    return pl.pallas_call(
        kernel,
        in_specs=[scalar if i in smem else vmem for i in range(len(args))],
        out_specs=[vmem] * (len(outs) - values) + [scalar] * values,
        out_shape=[jax.ShapeDtypeStruct(shape, dtype) for shape, dtype in outs],
        scratch_shapes=[pltpu.VMEM(shape, dtype) for shape, dtype in scratch],
        compiler_params=pltpu.CompilerParams(vmem_limit_bytes=32 * 1024 * 1024),
    )(*args)


def local(
    saved_states,
    adjoint_final,
    bathymetry,
    wind_speed,
    wind_angle,
    drag_rate,
    metrics,
    face_link,
    face_tag,
    send_faces,
):
    devices = lax.axis_size("dom")
    groups = [list(range(g, g + GROUP)) for g in range(0, devices, GROUP)]
    back3, flip3, grad3, take2, spread3 = constants()
    tables = [back3, flip3, grad3, take2, spread3]

    mixed, x_out = ((3, 32, E), F32), ((GROUP * 8, 128), F32)
    sends_out, sums_out = ((128, 384), BF16), ((5, 32, E), F32)
    pairs = [(i, i) for i in range(ROW)] + [(i, i) for i in range(devices - ROW, devices)]
    for row in range(1, devices // ROW - 1, 2):
        for i in range(row * ROW, row * ROW + ROW):
            pairs += [(i, i + ROW), (i + ROW, i)]
    pack_args = (saved_states, adjoint_final, bathymetry)
    pack_args += (metrics, face_tag, face_link, send_faces)
    mine = call(pack_kernel, [((PACKED, E), F32)], pack_args)[0]
    halo = lax.ppermute(mine, "dom", pairs)
    both = [mine, halo]

    near_out, far_out = ((3 * E, 3 * E), BF16), ((128, 3 * E), BF16)
    my_sends, boxes, rate, my_near, my_far, my_last, *near3, past, sums = call(
        own_first_kernel,
        [sends_out, ((64, 128), F32), ((8, E), F32), near_out, far_out, far_out]
        + [((1, 3, 32, E), F32), ((1, 3, 24, E), F32), ((1, 3, 24, E), F32), ((4, 24, E), F32), sums_out],
        [mine, flip3, drag_rate] + tables + [saved_states],
        smem=(2,),
    )
    tables.append(rate)
    x, halo_sends = call(halo_first_kernel, [x_out, sends_out], (halo, flip3, boxes))
    def exchange(x):
        return lax.all_to_all(x, "dom", 0, 0, tiled=True, axis_index_groups=groups)

    bases, faces = ((2, 3, 32, E), F32), ((2, 3, 24, E), F32)
    far_outs, near_outs = [mixed, mixed, x_out], [bases, faces, faces, sums_out]
    sends = [my_sends, halo_sends]

    y = exchange(x)
    lam3, _, x, normals, halo_near, halo_far = got = call(
        round3_kernel,
        far_outs + [((2, 3, 8, E), F32), near_out, far_out],
        tables + both + [y] + sends + [my_far] + near3 + [past],
        scratch=[bases, faces, faces] + [((1,) + shape[1:], F32) for shape, _ in (bases, faces, faces)],
    )
    y = exchange(x)
    x, base, ahead, motion, sums = call(
        round2_kernel,
        [x_out] + near_outs,
        tables + list(got[0:2]) + both + [sums, saved_states, y, normals] + sends
        + [my_near, halo_near, my_far, halo_far],
        scratch=[bases, faces, faces, mixed, mixed, sums_out],
    )
    y = exchange(x)
    within = call(fold_kernel, [((8, 128), F32)], (y,))[0]
    within = lax.ppermute(within, "dom", spread_pairs(devices))
    last_out = ((GROUP, 4, 128), F32)
    lam1, _, x = call(
        lambda *refs: (far_kernel(1, 2, *refs), None)[1],
        [mixed, mixed, last_out],
        [y, spread3, base, motion] + both + [my_far, halo_far, normals, ahead],
    )
    args = tables + [lam1, mine, my_near, sums, saved_states, lam3, wind_speed, wind_angle]
    base, motion, depth_gradient, speed_gradient, angle_gradient = call(
        lambda *refs: near_kernel(0, 1, *refs),
        [((1, 3, 32, E), F32), ((1, 3, 24, E), F32)] + [((28, E), F32)] * 3,
        args,
    )
    x, base = lax.optimization_barrier((x, base))
    y = exchange(call(insert_kernel, [last_out], (x, within))[0])
    initial, drag_gradient = call(
        lambda *refs: (far_kernel(0, 1, *refs), None)[1],
        [((3, 28, E), F32), ((1,), F32)],
        [y, spread3, base, motion, mine, my_last, normals],
        values=1,
    )
    return (initial, depth_gradient, speed_gradient, angle_gradient, drag_gradient)


def solution(mesh):
    return jax.shard_map(
        local,
        mesh=mesh,
        in_specs=(
            P(None, None, None, "dom"),
            P(None, None, "dom"),
            P(None, "dom"),
            P(None, "dom"),
            P(None, "dom"),
            P(),
            P(None, "dom"),
            P(None, "dom"),
            P(None, "dom"),
            P(None, "dom"),
        ),
        out_specs=(P(None, None, "dom"), P(None, "dom"), P(None, "dom"), P(None, "dom"), P()),
        check_vma=False,
    )
```

```python
import math

import jax
import jax.numpy as jnp
import ml_dtypes
import numpy as np
from jax import lax
from jax.experimental import pallas as pl
from jax.experimental.pallas import tpu as pltpu
from jax.sharding import PartitionSpec as P

GRAVITY = 1.0
PENALTY = 3.0
WIND_COEF = 5.0
TIME_STEP = 0.01
HALF = 0.5 * TIME_STEP
SIXTH = TIME_STEP / 6.0

GROUP = 32
STRIDE = 16
ROW = 16
REACH = 4
DIRS = 8
SLOTS = 16
E = 128
DEPTH, MISC = 12, 24
PACKED = MISC + 28 * 13 + 4
F32 = jnp.float32
BF16 = jnp.bfloat16


def solve_dense(matrix, right):
    system = np.array(matrix) + 0.0
    result = np.array(right) + 0.0
    extent = system.shape[0]
    for column in range(extent):
        pivot_index = column + int(np.argmax(np.abs(system[column:, column])))
        system[[column, pivot_index]] = system[[pivot_index, column]]
        result[[column, pivot_index]] = result[[pivot_index, column]]
        for target in range(column + 1, extent):
            factor = system[target, column] / system[column, column]
            system[target] = system[target] - factor * system[column]
            result[target] = result[target] - factor * result[column]
    solution = np.zeros(result.shape)
    for column in range(extent - 1, -1, -1):
        solution[column] = (
            result[column] - system[column, column + 1 :] @ solution[column + 1 :]
        ) / system[column, column]
    return solution


def element_tables():
    degree = 6
    nodes = [
        (column, row_index)
        for row_index in range(degree + 1)
        for column in range(degree + 1 - row_index)
    ]
    node_total = len(nodes)
    coord_x = np.array([node[0] / degree for node in nodes])
    coord_y = np.array([node[1] / degree for node in nodes])
    vander = np.zeros((node_total, node_total))
    vander_r = np.zeros((node_total, node_total))
    vander_s = np.zeros((node_total, node_total))
    grams = np.zeros((node_total, node_total))
    for column_index, power in enumerate(nodes):
        first, second = power
        vander[:, column_index] = coord_x**first * coord_y**second
        if first > 0:
            vander_r[:, column_index] = 0.5 * first * coord_x ** (first - 1) * coord_y**second
        if second > 0:
            vander_s[:, column_index] = 0.5 * second * coord_x**first * coord_y ** (second - 1)
        for other_index, other_power in enumerate(nodes):
            sum_x = first + other_power[0]
            sum_y = second + other_power[1]
            grams[column_index, other_index] = (
                4.0
                * math.factorial(sum_x)
                * math.factorial(sum_y)
                / math.factorial(sum_x + sum_y + 2)
            )
    deriv_r = solve_dense(vander.T, vander_r.T).T
    deriv_s = solve_dense(vander.T, vander_s.T).T
    mass_inverse = vander @ solve_dense(grams, vander.T)
    points = np.arange(degree + 1) / degree
    line_vander = np.stack([points**power for power in range(degree + 1)], axis=1)
    line_grams = np.array(
        [
            [2.0 / (first + second + 1) for second in range(degree + 1)]
            for first in range(degree + 1)
        ]
    )
    line_inverse = solve_dense(line_vander, np.eye(degree + 1))
    line_mass = line_inverse.T @ line_grams @ line_inverse
    lookup = {node: number for number, node in enumerate(nodes)}
    face_nodes = [
        [lookup[step, 0] for step in range(degree + 1)],
        [lookup[degree - step, step] for step in range(degree + 1)],
        [lookup[0, degree - step] for step in range(degree + 1)],
    ]
    embed = np.zeros((node_total, 3 * (degree + 1)))
    extract = np.zeros((3 * (degree + 1), node_total))
    for face_index in range(3):
        for step in range(degree + 1):
            extract[face_index * (degree + 1) + step, face_nodes[face_index][step]] = 1.0
            for other_step in range(degree + 1):
                embed[
                    face_nodes[face_index][other_step], face_index * (degree + 1) + step
                ] += line_mass[other_step, step]
    lifting = mass_inverse @ embed
    return deriv_r, deriv_s, lifting, extract


def offset_of(direction):
    return direction + 1 if direction < REACH else REACH - direction - 1


def neighbours():
    me = jnp.bitwise_and(lax.axis_index("dom"), GROUP - 1)
    found = []
    for own in (me + ROW, jnp.where(me < ROW, me, me + 2 * ROW)):
        for j in range(DIRS):
            place = own + offset_of(j)
            inner = (place >= ROW) & (place < ROW + GROUP)
            exists = (place >= 0) & (place < 4 * ROW)
            device = jnp.where(inner, place - ROW, jnp.where(place < ROW, place, place - 2 * ROW))
            found.append((jnp.where(exists, device, 0), jnp.where(inner, 0, 1), exists))
    return found


def spread_place(dx, dy):
    half, odd = dx // 2, dx % 2
    if dy == 0:
        return 6 + half + ROW * odd
    if dy == 2:
        return 4 + half + ROW * (1 - odd)
    return dx + (ROW if dy == 1 else 0)


def spread_pairs(devices):
    pairs = []
    for group in range(devices // GROUP):
        for dx in range(4):
            for dy in range(4):
                other = (group // 4 + dx) % 4 * 4 + (group % 4 + dy) % 4
                place = spread_place(dx, dy)
                source = place if dy == 0 else (place + ROW) % GROUP
                pairs.append((other * GROUP + source, group * GROUP + place))
    return pairs


def parts3(matrix, width):
    padded = np.zeros((matrix.shape[0], width))
    padded[:, : matrix.shape[1]] = matrix
    hi = padded.astype(np.float32).astype(ml_dtypes.bfloat16)
    lo = (padded - hi.astype(np.float64)).astype(ml_dtypes.bfloat16)
    return np.concatenate([hi, lo, hi], axis=1)


def constants():
    deriv_r, deriv_s, lifting, extract = element_tables()

    def pad_rows(matrix):
        return np.concatenate([matrix, np.zeros((4, matrix.shape[1]))])

    lift = np.zeros((24, 28))
    flip = np.zeros((24, 28))
    take = np.zeros((24, 28))
    give = np.zeros((24, 28))
    for face in range(3):
        for k in range(7):
            lift[8 * face + k] = lifting[:, 7 * face + k]
            flip[8 * face + k] = lifting[:, 7 * face + 6 - k]
            take[8 * face + k] = extract[7 * face + k]
            give[8 * face + k] = extract[7 * face + k]
        take[8 * face + 7] = extract[7 * face + 6]
    back = np.concatenate([pad_rows(deriv_r.T), pad_rows(deriv_s.T), lift, flip])
    back3 = parts3(back, 32)
    flip3 = parts3(flip, 32)
    grad3 = parts3(np.concatenate([pad_rows(deriv_r), pad_rows(deriv_s)]), 32)
    take2 = np.zeros((24, 64))
    take2[:, 0:28] = take
    take2[:, 32:60] = take
    spread = np.concatenate([pad_rows(give.T), flip @ give.T])
    spread3 = parts3(spread, 24)
    spread3 = np.concatenate([spread3, np.zeros((56, 8), ml_dtypes.bfloat16)], axis=1)
    as_bf16 = lambda m: jnp.asarray(np.asarray(m).astype(ml_dtypes.bfloat16))
    return as_bf16(back3), as_bf16(flip3), as_bf16(grad3), as_bf16(take2), as_bf16(spread3)


def dot(a, b):
    return jnp.dot(a, b, preferred_element_type=F32)


def dot_nt(a, b):
    return lax.dot_general(a, b, (((1,), (1,)), ((), ())), preferred_element_type=F32)


def halves(x):
    hi = x.astype(BF16).astype(F32)
    return hi, x - hi


def times3(matrix3, x):
    hi = x.astype(BF16)
    lo = (x - hi.astype(F32)).astype(BF16)
    return dot(matrix3, jnp.concatenate([hi, hi, lo], axis=0))


def spread_faces(spread3, faces):
    hi, lo = halves(faces)
    stack = jnp.concatenate([hi, hi, lo, jnp.zeros((8, faces.shape[1]), F32)], axis=0)
    return dot(spread3, stack.astype(BF16))


def geometry(misc):
    rx, ry, sx, sy = misc[0:1], misc[1:2], misc[2:3], misc[3:4]
    normals = []
    for nx, ny in ((-sx, -sy), (rx + sx, ry + sy), (-rx, -ry)):
        normals.append((nx, ny, jnp.sqrt(nx * nx + ny * ny)))
    return (rx, ry, sx, sy), normals


def jump_back(n, t, u, v, gh):
    nx, ny, size = n
    un = nx * u + ny * v
    mixed = u * t[1] + v * t[2]
    pull = 0.5 * PENALTY * size
    return (
        0.5 * (gh * (nx * t[1] + ny * t[2]) - un * mixed) - pull * t[0],
        0.5 * (nx * (t[0] + mixed) + un * t[1]) - pull * t[1],
        0.5 * (ny * (t[0] + mixed) + un * t[2]) - pull * t[2],
    )


def traces(flipped, normals):
    last = lax.broadcasted_iota(jnp.int32, (8, E), 0) == 7
    rows = []
    for c in range(3):
        rows.append(
            jnp.concatenate(
                [jnp.where(last, normals[f][c], flipped[c][f]) for f in range(3)], axis=1
            )
        )
    return jnp.concatenate(rows, axis=0)


def far_index(link, width=8):
    v = link - 3 * E
    j = lax.shift_right_arithmetic(v, 4)
    c = jnp.bitwise_and(v, 15)
    part = lax.shift_right_arithmetic(c, width.bit_length() - 1)
    row = part * (DIRS * width) + j * width + jnp.bitwise_and(c, width - 1)
    return jnp.where(v >= 0, row, -1)


def slot_rows(sends, v, block):
    first = 64 * block
    n = v.shape[1]
    hi, lo = halves(v)
    rows = [jnp.zeros((first, n), F32)] if block else []
    rest = [jnp.zeros((32 - v.shape[0], n), F32)] if v.shape[0] < 32 else []
    rows += [hi] + rest + [lo] + rest + [jnp.zeros((64 - first, n), F32)] * (1 - block)
    out = dot_nt(sends, jnp.concatenate(rows, axis=0).astype(BF16))
    lane = lax.broadcasted_iota(jnp.int32, (128, 128), 1)
    out = jnp.where((lane >= first) & (lane < first + 32), out + pltpu.roll(out, 96, 1), 0.0)
    return out[0:64] + pltpu.roll(out[64:128], 32, 1)


def quarter_rows(sends, v):
    hi, lo = halves(v)
    rest = jnp.zeros((8, v.shape[1]), F32)
    stack = jnp.concatenate([hi, rest, lo, rest, jnp.zeros((64, v.shape[1]), F32)], axis=0)
    out = dot_nt(sends, stack.astype(BF16))
    lane = lax.broadcasted_iota(jnp.int32, (128, 128), 1)
    out = jnp.where(lane < 32, out + pltpu.roll(out, 96, 1), 0.0)
    total = out[0:32]
    for h in range(1, 4):
        total = total + pltpu.roll(out[32 * h : 32 * h + 32], 32 * h, 1)
    return total


def send_quarters(x_ref, near_by, boxes):
    x_ref[...] = jnp.zeros(x_ref.shape, F32)
    for b in range(2):
        for j in range(DIRS):
            device, second, exists = near_by[DIRS * b + j]
            box = jnp.where(exists & (second == 0), boxes[b][4 * j : 4 * j + 4], 0.0)
            x_ref[device] = x_ref[device] + box


def send(x_ref, near_by, boxes):
    x_ref[...] = jnp.zeros(x_ref.shape, F32)
    for b in range(2):
        for j in range(DIRS):
            device, _, exists = near_by[DIRS * b + j]
            rows = pl.ds(pl.multiple_of(device * 8, 8), 8)
            box = jnp.where(exists, boxes[b][8 * j : 8 * j + 8], 0.0)
            x_ref[rows, :] = x_ref[rows, :] + box


def send_matrix(misc, width=8):
    faces = misc[16:24]
    lane = lax.broadcasted_iota(jnp.int32, (8, 128), 1)
    both = jnp.zeros((8, 128), F32)
    for h in range(SLOTS // width):
        part = jnp.where((lane >= width * h) & (lane < width * h + width), faces, 0.0)
        both = both + (pltpu.roll(part, (DIRS - 1) * width * h, 1) if h else part)
    row = lax.broadcasted_iota(jnp.int32, (8, 128), 0)
    lined = jnp.zeros((8, 128), F32)
    for j in range(DIRS):
        moved = both if j == 0 else pltpu.roll(both, width * j, 1)
        lined = lined + jnp.where(row == j, moved, 0.0)
    line = jnp.sum(lined, axis=0, keepdims=True)
    column = jnp.transpose(jnp.broadcast_to(line, (128, 128)))
    face = lax.broadcasted_iota(jnp.int32, (128, 128), 1).astype(F32)
    pieces = [jnp.where(column == face + float(128 * f), 1.0, 0.0) for f in range(3)]
    return jnp.concatenate(pieces, axis=1).astype(BF16)


def pack_kernel(q_ref, lam_ref, depth_ref, metric_ref, tag_ref, link_ref, face_ref, out_ref):
    out_ref[0:MISC, :] = jnp.zeros((MISC, E), F32)
    out_ref[0:4, :] = metric_ref[...]
    out_ref[4:7, :] = tag_ref[...].astype(F32)
    out_ref[8:11, :] = link_ref[...].astype(F32)
    out_ref[16:24, 0:16] = face_ref[...].astype(F32)
    for c in range(3):
        out_ref[MISC + 28 * c : MISC + 28 * c + 28, :] = lam_ref[c]
    for s in range(3):
        for c in range(3):
            first = MISC + 28 * (3 * (3 - s) + c)
            out_ref[first : first + 28, :] = q_ref[s + 1, c]
    out_ref[MISC + 28 * DEPTH : MISC + 28 * DEPTH + 28, :] = depth_ref[...]
    out_ref[PACKED - 4 : PACKED, :] = jnp.zeros((4, E), F32)


def field(part_ref, i, fill):
    first = MISC + 28 * i
    row = lax.broadcasted_iota(jnp.int32, (32, E), 0)
    return jnp.where(row < 28, part_ref[first : first + 32, :], fill)


def first_boxes(part_ref, flip3, block):
    misc = part_ref[0:MISC, :]
    weights = jnp.concatenate([HALF * field(part_ref, c, 0.0) for c in range(3)], axis=1)
    flipped = times3(flip3[...], weights)
    split = [
        [flipped[8 * f : 8 * f + 8, 128 * c : 128 * c + 128] for f in range(3)] for c in range(3)
    ]
    sends = send_matrix(misc)
    return sends, slot_rows(sends, traces(split, geometry(misc)[1]), block)


def own_first_kernel(part_ref, flip3, drag_ref, *refs):
    tables, state_ref = refs[0:5], refs[5]
    sends_ref, boxes_ref, rate_ref, near_ref, far_ref, last_ref = refs[6:12]
    links = part_ref[8:11, :].astype(jnp.int32)
    near_ref[...], far_ref[...] = near_match(links), far_match(links)
    last_ref[...] = far_match(links, 4)
    rate_ref[...] = jnp.full((8, E), drag_ref[0], F32)
    near_kernel(3, 1, *tables, rate_ref, part_ref, part_ref, near_ref, state_ref, *refs[12:])
    sends_ref[...], boxes_ref[...] = first_boxes(part_ref, flip3, 0)


def halo_first_kernel(part_ref, flip3, boxes_ref, x_ref, sends_ref):
    sends_ref[...], boxes = first_boxes(part_ref, flip3, 1)
    send(x_ref, neighbours(), [boxes_ref[...], boxes])


def near_match(links):
    rows = lax.broadcasted_iota(jnp.int32, (3 * E, E), 0)
    return jnp.concatenate(
        [jnp.where(rows == links[f : f + 1], 1.0, 0.0).astype(BF16) for f in range(3)], axis=1
    )


def far_match(links, width=8):
    rows = lax.broadcasted_iota(jnp.int32, (128, E), 0)
    found = [rows == far_index(links[f : f + 1], width) for f in range(3)]
    return jnp.concatenate([jnp.where(x, 1.0, 0.0).astype(BF16) for x in found], axis=1)


def near_kernel(section, blocks, *refs, light=False):
    refs = list(refs)
    back3, flip3, grad3, take2, spread3 = [refs.pop(0)[...] for _ in range(5)]
    rate_ref = refs.pop(0)
    lams = [refs.pop(0) for _ in range(blocks)]
    parts = [refs.pop(0) for _ in range(blocks)]
    matches = [refs.pop(0) for _ in range(blocks)]
    old_ref = refs.pop(0) if section < 3 else None
    if section == 3 and not light:
        state_ref = refs.pop(0)
    if section == 0:
        state_ref, lam3_ref = refs.pop(0), refs.pop(0)
        speed_ref, angle_ref = refs.pop(0), refs.pop(0)
    base_ref = refs.pop(0)
    if section > 0:
        ahead_ref = refs.pop(0)
    motion_ref = refs.pop(0)
    if section == 3 and not light:
        past_ref = refs.pop(0)
    if light:
        pass
    elif section > 0:
        sum_ref = refs.pop(0)
    else:
        depth_out, speed_out, angle_out = refs.pop(0), refs.pop(0), refs.pop(0)
    scale = SIXTH if section == 2 else HALF
    later = SIXTH if section == 3 else HALF
    drag_rate = rate_ref[...][0:1]
    pad = jnp.ones((4, E), F32)

    if section == 3:
        lam = [[field(lams[b], c, 0.0) for c in range(3)] for b in range(blocks)]
    else:
        lam = [[lams[b][c] for c in range(3)] for b in range(blocks)]
    w = [[scale * x for x in lam[b]] for b in range(blocks)]
    if section == 0:
        q = [[jnp.concatenate([state_ref[0, c], pad], axis=0) for c in range(3)]]
    else:
        q = [[field(parts[b], 3 * (4 - section) + c, 1.0) for c in range(3)] for b in range(blocks)]
    z = [field(parts[b], DEPTH, 1.0) for b in range(blocks)]
    pulled = times3(back3, jnp.concatenate([x for b in range(blocks) for x in w[b]], axis=1))
    slopes = times3(grad3, jnp.concatenate(z, axis=1))
    fields = jnp.concatenate([x for b in range(blocks) for x in q[b] + [z[b]]], axis=1)
    hi, lo = halves(fields)
    at_faces = dot(take2, jnp.concatenate([hi, lo], axis=0).astype(BF16))

    if section == 3 and not light:
        fields = [jnp.concatenate([state_ref[0, c], pad], axis=0) for c in range(3)]
        fields += [field(parts[0], 9 + c, 1.0) for c in range(3)]
        hi, lo = halves(jnp.concatenate(fields, axis=1))
        past = dot(take2, jnp.concatenate([hi, lo], axis=0).astype(BF16))
        for i in range(2):
            finv = 1.0 / past[:, 384 * i : 384 * i + 128]
            past_ref[2 * i] = past[:, 384 * i + 128 : 384 * i + 256] * finv
            past_ref[2 * i + 1] = past[:, 384 * i + 256 : 384 * i + 384] * finv

    face_sums, volumes, opens = [], [], []
    for b in range(blocks):
        misc = parts[b][0:MISC, :]
        (rx, ry, sx, sy), normals = geometry(misc)
        part = lambda r0, r1, c: pulled[r0:r1, 384 * b + 128 * c : 384 * b + 128 * c + 128]
        h = q[b][0]
        inv = 1.0 / h
        u, v = q[b][1] * inv, q[b][2] * inv
        gh = GRAVITY * h
        along = [part(0, 32, c) for c in range(3)]
        across = [part(32, 64, c) for c in range(3)]
        fx = [-(rx * along[c] + sx * across[c]) for c in range(3)]
        fy = [-(ry * along[c] + sy * across[c]) for c in range(3)]
        cross = fx[2] + fy[1]
        slope_r = slopes[0:32, 128 * b : 128 * b + 128]
        slope_s = slopes[32:64, 128 * b : 128 * b + 128]
        slope_x = rx * slope_r + sx * slope_s
        slope_y = ry * slope_r + sy * slope_s
        flow = u * w[b][1] + v * w[b][2]
        drag_inv = drag_rate * inv
        volumes.append(
            (
                gh * (fx[1] + fy[2])
                - u * (u * fx[1] + v * cross)
                - v * v * fy[2]
                + GRAVITY * (slope_x * w[b][1] + slope_y * w[b][2])
                + drag_inv * flow,
                fx[0] + 2.0 * u * fx[1] + v * cross - drag_inv * w[b][1],
                fy[0] + u * cross + 2.0 * v * fy[2] - drag_inv * w[b][2],
            )
        )
        own = [[part(64 + 8 * f, 72 + 8 * f, c) for f in range(3)] for c in range(3)]
        flipped = [[part(88 + 8 * f, 96 + 8 * f, c) for f in range(3)] for c in range(3)]
        hi, lo = halves(traces(flipped, normals))
        pool = jnp.concatenate([hi, lo], axis=0).astype(BF16)
        found = dot(pool, matches[b][...])
        found = found[0:24] + found[24:48]
        opened = []
        sums = [[], [], []]
        for f in range(3):
            got = found[:, 128 * f : 128 * f + 128]
            value = lambda i: at_faces[
                8 * f : 8 * f + 8, 512 * b + 128 * i : 512 * b + 128 * i + 128
            ]
            fh, fm, fn, fz = value(0), value(1), value(2), value(3)
            finv = 1.0 / fh
            fu, fv, fgh = fm * finv, fn * finv, GRAVITY * fh
            motion_ref[b, 0, 8 * f : 8 * f + 8, :] = fu
            motion_ref[b, 1, 8 * f : 8 * f + 8, :] = fv
            motion_ref[b, 2, 8 * f : 8 * f + 8, :] = fgh
            tag = misc[4 + f : 5 + f]
            linked, wall, free = tag == 0.0, tag == 1.0, tag == 2.0
            nx, ny, size = normals[f]
            t = [own[c][f] for c in range(3)]
            mine = jump_back(normals[f], t, fu, fv, fgh)
            inv_size = 1.0 / size
            ux, uy = nx * inv_size, ny * inv_size
            twice = 2.0 * (ux * t[1] + uy * t[2])
            mirrored = (t[0], t[1] - twice * ux, t[2] - twice * uy)
            near = (got[0:8], got[8:16], got[16:24])
            other_n = tuple(
                jnp.where(linked, near[c][7:8], jnp.where(wall, m, 0.0))
                for c, m in enumerate((-nx, -ny, size))
            )
            other_t = [
                jnp.where(linked, near[c], jnp.where(wall, mirrored[c], 0.0)) for c in range(3)
            ]
            theirs = jump_back(other_n, other_t, fu, fv, fgh)
            zinv = 1.0 / fz
            out = jump_back(normals[f], t, fm * zinv, fn * zinv, GRAVITY * fz)
            opened.append(jnp.where(free, -out[0], 0.0))
            sums[0].append(mine[0] - theirs[0])
            sums[1].append(mine[1] - theirs[1] - jnp.where(free, out[1], 0.0))
            sums[2].append(mine[2] - theirs[2] - jnp.where(free, out[2], 0.0))
        face_sums.append([jnp.concatenate(sums[c], axis=0) for c in range(3)])
        if b == 0:
            opens = jnp.concatenate(opened, axis=0)
            height, moved = h, flow
    to_nodes = [x for b in range(blocks) for x in face_sums[b]]
    if section == 0:
        old = [old_ref[i] for i in range(5)]
        opens = opens + old[4][0:24]
        to_nodes.append(opens)
    nodes = spread_faces(spread3, jnp.concatenate(to_nodes, axis=1))
    for b in range(blocks):
        bases = []
        for c in range(3):
            first = lam[b][c]
            if section == 2:
                first = first * (1.0 / 3.0)
            if section == 0:
                first = first + (2.0 / 3.0) * lam3_ref[c]
            where = 384 * b + 128 * c
            bases.append(first + volumes[b][c] + nodes[0:32, where : where + 128])
            base_ref[b, c] = bases[c]
        if section > 0:
            ahead = times3(flip3, later * jnp.concatenate(bases, axis=1))
            for c in range(3):
                ahead_ref[b, c] = ahead[:, 128 * c : 128 * c + 128]
    if light:
        return
    w1, w2 = w[0][1], w[0][2]
    g1, g2 = height * w1, height * w2
    if section == 3:
        fold = moved[0:8] + moved[8:16] + moved[16:24] + moved[24:32]
        news = [w1, w2, g1, g2]
    else:
        if section > 0:
            old = [old_ref[i] for i in range(5)]
            opens = opens + old[4][0:24]
            fold = old[4][24:32] + (moved[0:8] + moved[8:16] + moved[16:24] + moved[24:32])
        news = [x + y for x, y in zip(old[0:4], (w1, w2, g1, g2))]
    if section > 0:
        for i in range(4):
            sum_ref[i] = news[i]
        sum_ref[4, 0:24, :] = opens
        sum_ref[4, 24:32, :] = fold
    else:
        rx, ry, sx, sy = geometry(parts[0][0:4, :])[0]
        w1, w2, g1, g2 = news
        pair = GRAVITY * jnp.concatenate([rx * g1 + ry * g2, sx * g1 + sy * g2], axis=1)
        pulled = times3(back3, pair)
        depth = pulled[0:32, 0:128] + pulled[32:64, 128:256] + nodes[0:32, 384:512]
        depth_out[...] = depth[0:28]
        speed, angle = speed_ref[...], angle_ref[...]
        cosine, sine = jnp.cos(angle), jnp.sin(angle)
        w1, w2 = w1[0:28], w2[0:28]
        speed_out[...] = (2.0 * WIND_COEF) * speed * (cosine * w1 + sine * w2)
        angle_out[...] = WIND_COEF * speed * speed * (cosine * w2 - sine * w1)


def far_kernel(section, blocks, *refs):
    refs = list(refs)
    y_ref, spread3_ref, base_ref, motion_ref = [refs.pop(0) for _ in range(4)]
    parts = [refs.pop(0) for _ in range(blocks)]
    matches = [refs.pop(0) for _ in range(blocks)]
    if section < 3:
        normal_ref = refs.pop(0)
    if section > 0:
        ahead_ref = refs.pop(0)
    if section > 1:
        sends_refs = [refs.pop(0), refs.pop(0)]
    if section == 3:
        past_ref = refs.pop(0)
    lam_refs = [refs.pop(0) for _ in range(blocks)]
    if section > 0:
        x_ref = refs.pop(0)
    if section == 3:
        normal_ref = refs.pop(0)
    if section == 0:
        drag_ref = refs.pop(0)
    later = SIXTH if section == 3 else HALF

    lane = lax.broadcasted_iota(jnp.int32, (8, 128), 1)
    place_in = jnp.bitwise_and(lane, 31)
    spare = (place_in >= 24) | (place_in == 7) | (place_in == 15) | (place_in == 23)
    near_by = neighbours()
    boxes, extras = [], []
    for b in range(2):
        for j in range(DIRS):
            if b < blocks:
                device, second, exists = near_by[DIRS * b + j]
                if section == 0:
                    boxes.append(jnp.where(exists, y_ref[device], 0.0))
                    continue
                raw = y_ref[pl.ds(pl.multiple_of(device * 8, 8), 8), :]
                turned = pltpu.roll(raw, 64, 1)
                if section == 2:
                    box = jnp.where(second == 1, jnp.where(spare, 0.0, turned), raw)
                    extras.append(jnp.where(exists & (second == 0), turned, 0.0))
                else:
                    box = jnp.where(second == 1, turned, raw)
                boxes.append(jnp.where(exists, box, 0.0))
            elif section > 0:
                boxes.append(jnp.zeros((8, 128), F32))
    if section == 0:
        boxes.append(jnp.zeros((96, 128), F32))
    stacks = [jnp.transpose(jnp.concatenate(boxes, axis=0))]
    if section == 2:
        stacks.append(jnp.transpose(jnp.concatenate(extras, axis=0)))
    left = lax.broadcasted_iota(jnp.int32, (32, 128), 1) < 64
    row = lax.broadcasted_iota(jnp.int32, (8, E), 0)
    face_sums, factors = [], []
    for b in range(blocks):
        pools = []
        for turned in stacks:
            low, high = turned[0:32], turned[32:64]
            if section == 0:
                pool = low
                for h in range(1, 4):
                    pool = pool + pltpu.roll(turned[32 * h : 32 * h + 32], 32 * h, 1)
                pools.append(pool)
            elif b == 0:
                pools.append(jnp.where(left, low, pltpu.roll(high, 64, 1)))
            else:
                pools.append(jnp.where(left, pltpu.roll(low, 64, 1), high))
        pool = jnp.concatenate(pools, axis=0)
        tall = pool.shape[0]
        pool = jnp.concatenate(halves(pool), axis=0).astype(BF16)
        got = dot(pool, matches[b][...])
        got = got[0:tall] + got[tall:]
        sums, scales = [[], [], []], [[], [], []]
        for f in range(3):
            piece = lambda r: got[r : r + 8, 128 * f : 128 * f + 128]
            far = [piece(8 * c) for c in range(3)]
            if section == 3:
                normal = tuple(x[7:8] for x in far)
                for i in range(3):
                    normal_ref[b, f, i : i + 1, :] = normal[i]
            else:
                normal = tuple(normal_ref[b, f, i : i + 1, :] for i in range(3))
            motion = [motion_ref[b, i, 8 * f : 8 * f + 8, :] for i in range(3)]
            theirs = jump_back(normal, far, *motion)
            for c in range(3):
                sums[c].append(-theirs[c])
            if section == 3 and b == 0:
                u0, v0, u1, v1 = [past_ref[i, 8 * f : 8 * f + 8, :] for i in range(4)]
                nx, ny, size = normal
                mean = 0.5 * (nx * u0 + ny * v0)
                rate = 0.5 * (nx * u1 + ny * v1) - 0.5 * PENALTY * size
                factors.append((mean, mean * u1 + u0 * rate, mean * v1 + v0 * rate))
            if section == 2:
                singles = (piece(24)[7:8], piece(56)[7:8], far[0][7:8], far[1][7:8], far[2][7:8])
                singles += (piece(32)[7:8], piece(40)[7:8])
                third = jnp.zeros((8, E), F32)
                for k in range(7):
                    third = jnp.where(row == k, singles[k], third)
                factors.append((piece(24), piece(56), third))
        face_sums += [jnp.concatenate(sums[c], axis=0) for c in range(3)]
    spread = spread_faces(spread3_ref[...], jnp.concatenate(face_sums, axis=1))
    slots = []
    partial = jnp.zeros((8, E), F32)
    for b in range(blocks):
        lam = []
        for c in range(3):
            where = 384 * b + 128 * c
            lam.append(base_ref[b, c] + spread[0:32, where : where + 128])
        if section > 0:
            for c in range(3):
                lam_refs[b][c] = lam[c]
            flipped = [
                ahead_ref[b, c]
                + later * spread[32:56, 384 * b + 128 * c : 384 * b + 128 * c + 128]
                for c in range(3)
            ]
            split = [[flipped[c][8 * f : 8 * f + 8] for f in range(3)] for c in range(3)]
            none = jnp.zeros((1, E), F32)
            lasts = [(none,) * 3] * 3
            if section == 3 and b == 0:
                lasts = [tuple(factors[f][2][k : k + 1] for k in (2, 3, 4)) for f in range(3)]
            trace = traces(split, lasts)
            if section == 3 and b == 0:
                last = row == 7
                third = lambda f, k: factors[f][2][k : k + 1]
                one = [jnp.where(last, third(f, 0), factors[f][0]) for f in range(3)]
                two = [jnp.where(last, third(f, 1), factors[f][1]) for f in range(3)]
                five = [jnp.where(last, third(f, 5), 0.0) for f in range(3)]
                six = [jnp.where(last, third(f, 6), 0.0) for f in range(3)]
                line = lambda parts: jnp.concatenate(parts, axis=1)
                trace = jnp.concatenate([trace, line(one)], axis=0)
                extra = [line(five), line(six), jnp.zeros((8, 3 * E), F32), line(two)]
                slots.append(
                    slot_rows(sends_refs[0][...], trace, 0)
                    + slot_rows(sends_refs[0][...], jnp.concatenate(extra, axis=0), 1)
                )
            elif section == 1:
                slots.append(quarter_rows(send_matrix(parts[b][0:MISC, :], 4), trace))
            else:
                slots.append(slot_rows(sends_refs[b][...], trace, b))
            if section == 2:
                for f in range(3):
                    for c in range(3):
                        partial = partial + split[c][f] * factors[3 * b + f][c]
        else:
            for c in range(3):
                lam_refs[b][c] = lam[c][0:28]
    if section > 0:
        (send_quarters if section == 1 else send)(x_ref, near_by, slots)
    else:
        group = lax.shift_right_logical(lax.axis_index("dom"), 5)
        total = jnp.zeros((4, 128), F32)
        for g in range(STRIDE):
            dx = jnp.bitwise_and(g // 4 - lax.shift_right_logical(group, 2), 3)
            dy = jnp.bitwise_and(g % 4 - jnp.bitwise_and(group, 3), 3)
            device = jnp.int32(0)
            for x in range(4):
                for y in range(4):
                    device = jnp.where((dx == x) & (dy == y), spread_place(x, y), device)
            total = total + y_ref[device]
        drag_ref[0] = jnp.sum(jnp.where(lane[0:4] == 127, total, 0.0))
    return partial


def round3_kernel(*refs):
    refs = list(refs)
    take = lambda n: [refs.pop(0) for _ in range(n)]
    tables, parts, (y_ref,), sends = take(6), take(2), take(1), take(2)
    (my_far,), done, (past,) = take(1), take(3), take(1)
    lams, (x_ref, normal_ref, halo_near, halo_far) = take(2), take(4)
    base, ahead, motion, *theirs = refs
    links = parts[1][8:11, :].astype(jnp.int32)
    halo_near[...], halo_far[...] = near_match(links), far_match(links)
    near_kernel(3, 1, *tables, parts[1], parts[1], halo_near, *theirs, light=True)
    for both, ours, other in zip((base, ahead, motion), done, theirs):
        both[0] = ours[0]
        both[1] = other[0]
    far_kernel(
        3, 2, y_ref, tables[4], base, motion, *parts, my_far, halo_far, ahead, *sends, past,
        *lams, x_ref, normal_ref,
    )


def round2_kernel(*refs):
    refs = list(refs)
    take = lambda n: [refs.pop(0) for _ in range(n)]
    tables, lams, parts, (old_ref, state_ref, y_ref) = take(6), take(2), take(2), take(3)
    (normal_ref,), sends, near_matches, far_matches = take(1), take(2), take(2), take(2)
    x_ref, base_ref, ahead_ref, motion_ref, sum_ref = take(5)
    base, ahead, motion, lam, halo_lam, sums = refs
    near_kernel(
        2, 2, *tables, *lams, *parts, *near_matches, old_ref, base, ahead, motion, sums
    )
    partial = far_kernel(
        2, 2, y_ref, tables[4], base, motion, *parts, *far_matches, normal_ref, ahead, *sends,
        lam, halo_lam, x_ref,
    )
    near_kernel(
        1, 2, *tables, lam, halo_lam, *parts, *near_matches, sums,
        base_ref, ahead_ref, motion_ref, sum_ref,
    )
    flow = state_ref[0, 1] * base_ref[0, 1, 0:28, :] + state_ref[0, 2] * base_ref[0, 2, 0:28, :]
    flow = jnp.concatenate([flow * (HALF / state_ref[0, 0]), jnp.zeros((4, E), F32)], axis=0)
    flow = flow[0:8] + flow[8:16] + flow[16:24] + flow[24:32]
    total = sum_ref[4, 24:32, :] - HALF * partial + flow
    put_value(x_ref, -jnp.sum(total, axis=1, keepdims=True))


def put_value(x_ref, value):
    lane = lax.broadcasted_iota(jnp.int32, (8, 128), 1)
    for e in range(GROUP):
        part = x_ref[8 * e : 8 * e + 8, :]
        x_ref[8 * e : 8 * e + 8, :] = jnp.where(lane == 127, value, part)


def fold_kernel(y_ref, out_ref):
    total = y_ref[0:8, :]
    for e in range(1, GROUP):
        total = total + y_ref[8 * e : 8 * e + 8, :]
    out_ref[...] = jnp.broadcast_to(total[:, 127:128], (8, 128))


def insert_kernel(x_ref, value_ref, out_ref):
    lane = lax.broadcasted_iota(jnp.int32, (4, 128), 1)
    value = value_ref[0:4, :] + value_ref[4:8, :]
    for e in range(GROUP):
        out_ref[e] = jnp.where(lane == 127, value, x_ref[e])


def call(kernel, outs, args, values=0, scratch=(), smem=()):
    vmem, scalar = pl.BlockSpec(memory_space=pltpu.VMEM), pl.BlockSpec(memory_space=pltpu.SMEM)
    return pl.pallas_call(
        kernel,
        in_specs=[scalar if i in smem else vmem for i in range(len(args))],
        out_specs=[vmem] * (len(outs) - values) + [scalar] * values,
        out_shape=[jax.ShapeDtypeStruct(shape, dtype) for shape, dtype in outs],
        scratch_shapes=[pltpu.VMEM(shape, dtype) for shape, dtype in scratch],
        compiler_params=pltpu.CompilerParams(vmem_limit_bytes=32 * 1024 * 1024),
    )(*args)


def local(
    saved_states,
    adjoint_final,
    bathymetry,
    wind_speed,
    wind_angle,
    drag_rate,
    metrics,
    face_link,
    face_tag,
    send_faces,
):
    devices = lax.axis_size("dom")
    groups = [list(range(g, g + GROUP)) for g in range(0, devices, GROUP)]
    back3, flip3, grad3, take2, spread3 = constants()
    tables = [back3, flip3, grad3, take2, spread3]

    mixed, x_out = ((3, 32, E), F32), ((GROUP * 8, 128), F32)
    sends_out, sums_out = ((128, 384), BF16), ((5, 32, E), F32)
    pairs = [(i, i) for i in range(ROW)] + [(i, i) for i in range(devices - ROW, devices)]
    for row in range(1, devices // ROW - 1, 2):
        for i in range(row * ROW, row * ROW + ROW):
            pairs += [(i, i + ROW), (i + ROW, i)]
    pack_args = (saved_states, adjoint_final, bathymetry)
    pack_args += (metrics, face_tag, face_link, send_faces)
    mine = call(pack_kernel, [((PACKED, E), F32)], pack_args)[0]
    halo = lax.ppermute(mine, "dom", pairs)
    both = [mine, halo]

    near_out, far_out = ((3 * E, 3 * E), BF16), ((128, 3 * E), BF16)
    my_sends, boxes, rate, my_near, my_far, my_last, *near3, past, sums = call(
        own_first_kernel,
        [sends_out, ((64, 128), F32), ((8, E), F32), near_out, far_out, far_out]
        + [((1, 3, 32, E), F32), ((1, 3, 24, E), F32), ((1, 3, 24, E), F32), ((4, 24, E), F32), sums_out],
        [mine, flip3, drag_rate] + tables + [saved_states],
        smem=(2,),
    )
    tables.append(rate)
    x, halo_sends = call(halo_first_kernel, [x_out, sends_out], (halo, flip3, boxes))
    def exchange(x):
        return lax.all_to_all(x, "dom", 0, 0, tiled=True, axis_index_groups=groups)

    bases, faces = ((2, 3, 32, E), F32), ((2, 3, 24, E), F32)
    far_outs, near_outs = [mixed, mixed, x_out], [bases, faces, faces, sums_out]
    sends = [my_sends, halo_sends]

    y = exchange(x)
    lam3, _, x, normals, halo_near, halo_far = got = call(
        round3_kernel,
        far_outs + [((2, 3, 8, E), F32), near_out, far_out],
        tables + both + [y] + sends + [my_far] + near3 + [past],
        scratch=[bases, faces, faces] + [((1,) + shape[1:], F32) for shape, _ in (bases, faces, faces)],
    )
    y = exchange(x)
    x, base, ahead, motion, sums = call(
        round2_kernel,
        [x_out] + near_outs,
        tables + list(got[0:2]) + both + [sums, saved_states, y, normals] + sends
        + [my_near, halo_near, my_far, halo_far],
        scratch=[bases, faces, faces, mixed, mixed, sums_out],
    )
    y = exchange(x)
    within = call(fold_kernel, [((8, 128), F32)], (y,))[0]
    within = lax.ppermute(within, "dom", spread_pairs(devices))
    last_out = ((GROUP, 4, 128), F32)
    lam1, x = call(
        lambda *refs: (far_kernel(1, 2, *refs[:-2], refs[-1], refs[-2]), None)[1],
        [mixed, last_out],
        [y, spread3, base, motion] + both + [my_far, halo_far, normals, ahead],
        scratch=[mixed],
    )
    args = tables + [lam1, mine, my_near, sums, saved_states, lam3, wind_speed, wind_angle]
    base, motion, depth_gradient, speed_gradient, angle_gradient = call(
        lambda *refs: near_kernel(0, 1, *refs),
        [((1, 3, 32, E), F32), ((1, 3, 24, E), F32)] + [((28, E), F32)] * 3,
        args,
    )
    x, base = lax.optimization_barrier((x, base))
    y = exchange(call(insert_kernel, [last_out], (x, within))[0])
    initial, drag_gradient = call(
        lambda *refs: (far_kernel(0, 1, *refs), None)[1],
        [((3, 28, E), F32), ((1,), F32)],
        [y, spread3, base, motion, mine, my_last, normals],
        values=1,
    )
    return (initial, depth_gradient, speed_gradient, angle_gradient, drag_gradient)


def solution(mesh):
    return jax.shard_map(
        local,
        mesh=mesh,
        in_specs=(
            P(None, None, None, "dom"),
            P(None, None, "dom"),
            P(None, "dom"),
            P(None, "dom"),
            P(None, "dom"),
            P(),
            P(None, "dom"),
            P(None, "dom"),
            P(None, "dom"),
            P(None, "dom"),
        ),
        out_specs=(P(None, None, "dom"), P(None, "dom"), P(None, "dom"), P(None, "dom"), P()),
        check_vma=False,
    )
```
